32 devices in a mesh: seq: 8 (over z, y), grp: 4 (over x, core).
Axes of the slice: x: 2, y: 2, z: 4, core: 2. Of those that a mesh axis runs over, the one named last changes fastest.
Arguments:
- frames_in: bfloat16 [128, 256, 1024], P(('grp', 'seq')), may hold values from -6 to 6
- action_codes: int32 [128], P(('grp', 'seq')), may hold values from 0 to 7
- cotangent: bfloat16 [128, 256, 1024], P(('grp', 'seq')), may hold values from -40 to 40, as said below
- attn_master: float32 [2, 1024, 4096], P(None, 'seq'), as said below
- attn_first: float32 [2, 1024, 4096], P(None, 'seq'), may hold values from -0.0014648438 to 0.0014648438
- attn_second: float32 [2, 1024, 4096], P(None, 'seq'), may hold values from 6e-08 to 2.4e-07
- ffn_master: float32 [2, 1024, 4096], P(None, 'seq'), may hold values from -0.1875 to 0.1875
- ffn_first: float32 [2, 1024, 4096], P(None, 'seq'), may hold values from -0.0014648438 to 0.0014648438
- ffn_second: float32 [2, 1024, 4096], P(None, 'seq'), may hold values from 6e-08 to 2.4e-07
- small_master: float32 [11, 1024], P(None, 'seq'), as said below
- small_first: float32 [11, 1024], P(None, 'seq'), may hold values from -0.0014648438 to 0.0014648438
- small_second: float32 [11, 1024], P(None, 'seq'), may hold values from 6e-08 to 2.4e-07
Outputs:
- block_out: bfloat16 [128, 256, 1024], P(('grp', 'seq'))
- input_grad: bfloat16 [128, 256, 1024], P(('grp', 'seq'))
- grad_norm: float32 [], replicated
- attn_updated: float32 [2, 1024, 4096], P(None, 'seq')
- attn_first_new: float32 [2, 1024, 4096], P(None, 'seq')
- attn_second_new: float32 [2, 1024, 4096], P(None, 'seq')
- ffn_updated: float32 [2, 1024, 4096], P(None, 'seq')
- ffn_first_new: float32 [2, 1024, 4096], P(None, 'seq')
- ffn_second_new: float32 [2, 1024, 4096], P(None, 'seq')
- small_updated: float32 [11, 1024], P(None, 'seq')
- small_first_new: float32 [11, 1024], P(None, 'seq')
- small_second_new: float32 [11, 1024], P(None, 'seq')
The draws below stay inside these ranges and needn't reach their ends.
Inputs may be any that keep to these rules, and one draw needn't show every extreme that they name: `attn_master`: attention weights of order 1024 to the power -1/2, output columns larger. `small_master`: gains positive, between 0.3 and 3.5, table rows of order one half. `cotangent`: entries of order one, their spread varying by feature within a factor of six.
All inputs are finite; a program needn't handle non-finite values.
Results may differ from the reference program's by a relative error of at most 0.02.
Values may be sent and summed in bfloat16 or wider, within the bound.
No kernel may reach another device: no remote copies, remote signals or barrier semaphores. Data moves between devices by JAX's collectives and lax.ppermute only.
A program may use at most 384 MiB of HBM per device.

```python
import math
import jax
import jax.numpy as jnp
from jax import lax

D = 1024
H = 16
HD = 64
FF = 4096
P_SIZE = 256
FPV = 16
CODES = 8
STEP = 5
FRAMES = 128


def draw_attn_master(key, part):
    key = jax.random.fold_in(key, 11)
    noise = jax.random.normal(key, (2, D, 4 * D), jnp.float32)
    column = jnp.arange(4 * D)[None, None, :]
    layer = jnp.arange(2)[:, None, None]
    boost = jnp.where(column >= 3 * D, jnp.where(layer == 0, 0.5 * math.sqrt(P_SIZE), 2.0), 1.0)
    return noise * boost * D ** (-0.5)


def draw_small_master(key, part):
    key = jax.random.fold_in(key, 12)
    noise = jax.random.normal(key, (3 + CODES, D), jnp.float32)
    row_index = jnp.arange(3 + CODES)[:, None]
    place = jnp.arange(D)[None, :].astype(jnp.float32) / (D - 1)
    rising = 0.6 * 3.0 ** place
    gains = rising * (1.0 + 0.1 * jnp.clip(noise, -3.0, 3.0))
    return jnp.where(row_index < 3, gains, 0.5 * noise)


def draw_cotangent(key, part):
    key = jax.random.fold_in(key, 13)
    place = jnp.arange(D)[None, None, :].astype(jnp.float32) / (D - 1)
    noise = jnp.clip(jax.random.normal(key, (FRAMES, P_SIZE, D), jnp.float32), -6.0, 6.0)
    return (noise * (1.0 + 2.0 * place)).astype(jnp.bfloat16)


def with_ends(entries, key, low, top_value):
    index_at = [jax.random.randint(jax.random.fold_in(key, axis), (), 0, length) for axis, length in enumerate(entries.shape)]
    widest = entries.shape.index(max(entries.shape))
    beside = index_at[:widest] + [(index_at[widest] + 1) % entries.shape[widest]] + index_at[widest + 1:]
    return entries.at[tuple(index_at)].set(low).at[tuple(beside)].set(top_value)


def shard_levels(key, extent, split, low, high):
    def one(dim, blocks):
        steps = jax.random.uniform(jax.random.fold_in(jax.random.fold_in(key, 6), dim), (blocks,), jnp.float32, low / len(split), high / len(split))
        return jnp.repeat(jnp.exp(steps), extent[dim] // blocks).reshape((-1,) + (1,) * (len(extent) - dim - 1))

    factor_of = one(*split[0])
    for cut in split[1:]:
        factor_of = factor_of * one(*cut)
    return factor_of


def bell_draw(own_key, extent, scale, limit, pieces=(), dtype=jnp.bfloat16):
    level = shard_levels(own_key, extent, pieces, -0.22, 0.18) if pieces else 1.0
    values = jax.random.normal(own_key, extent, jnp.float32) * scale * level
    return jnp.minimum(jnp.maximum(values, -limit), limit).astype(dtype)


def setup_inputs(seed: int = 0) -> dict:
    keys = jax.random.split(jax.random.key(seed), 13)
    return {
        "frames_in": bell_draw(keys[0], (FRAMES, P_SIZE, D), 1.0, 6.0, ((0, 32),)),
        "action_codes": with_ends(jax.random.randint(keys[1], (FRAMES,), 0, CODES), jax.random.fold_in(keys[1], 1), 0, CODES - 1).astype(jnp.int32),
        "cotangent": draw_cotangent(jax.random.fold_in(keys[12], 71), 0),
        "attn_master": draw_attn_master(jax.random.fold_in(keys[12], 71), 0),
        "attn_first": bell_draw(keys[4], (2, D, 4 * D), 0.00024, 0.0014648438, ((1, 8),), jnp.float32),
        "attn_second": jnp.clip(jnp.exp(math.log(2.399999914359796e-07) - 1.3862944 * jax.random.uniform(keys[5], (2, D, 4 * D), jnp.float32) ** shard_levels(keys[5], (2, D, 4 * D), ((1, 8),), -0.2, 0.2)), 5.99999978589949e-08, 2.399999914359796e-07),
        "ffn_master": bell_draw(keys[6], (2, D, FF), D ** -0.5, 0.1875, ((1, 8),), jnp.float32),
        "ffn_first": bell_draw(keys[7], (2, D, FF), 0.00024, 0.0014648438, ((1, 8),), jnp.float32),
        "ffn_second": jnp.clip(jnp.exp(math.log(2.399999914359796e-07) - 1.3862944 * jax.random.uniform(keys[8], (2, D, FF), jnp.float32) ** shard_levels(keys[8], (2, D, FF), ((1, 8),), -0.2, 0.2)), 5.99999978589949e-08, 2.399999914359796e-07),
        "small_master": draw_small_master(jax.random.fold_in(keys[12], 71), 0),
        "small_first": bell_draw(keys[10], (3 + CODES, D), 0.00024, 0.0014648438, ((1, 8),), jnp.float32),
        "small_second": jnp.clip(jnp.exp(math.log(2.399999914359796e-07) - 1.3862944 * jax.random.uniform(keys[11], (3 + CODES, D), jnp.float32) ** shard_levels(keys[11], (3 + CODES, D), ((1, 8),), -0.2, 0.2)), 5.99999978589949e-08, 2.399999914359796e-07),
    }


@jax.custom_vjp
def low(v):
    return lax.optimization_barrier(v.astype(jnp.bfloat16)).astype(jnp.float32)

@jax.custom_vjp
def low_back(v):
    return v

def low_keep(v):
    return (low(v), None)

def low_pass(kept, grad):
    return (grad,)

def back_keep(v):
    return (v, None)

def back_low(kept, grad):
    return (low(grad),)
low.defvjp(low_keep, low_pass)
low_back.defvjp(back_keep, back_low)
eps_norm = 1e-05
beta_first = 0.5
beta_second = 0.5
rate_matrix = 0.02
rate_small = 0.3
decay_rate = 0.1
eps_adam = 1e-08
masked_score = -1000000000.0

def layer_norm(values, gain_vec):
    centre = values - lax.optimization_barrier(jnp.mean(values, axis=-1, keepdims=True))
    spread = lax.optimization_barrier(jnp.mean(centre * centre, axis=-1, keepdims=True))
    return centre * lax.rsqrt(spread + eps_norm) * gain_vec

def spatial_mix(normed, weights):
    model_width = normed.shape[-1]
    frames, positions = (normed.shape[0], normed.shape[1])
    packed = low_back(low(jnp.einsum('fpd,de->fpe', normed, weights[:, :3 * model_width], precision=lax.Precision.HIGHEST)))
    packed = packed.reshape(frames, positions, 3, H, HD)
    queries, key_rows, values = (packed[:, :, 0], packed[:, :, 1], packed[:, :, 2])
    scores = low_back(jnp.einsum('fqhc,fkhc->fhqk', queries, key_rows, precision=lax.Precision.HIGHEST) * HD ** (-0.5))
    attn_probs = low(jax.nn.softmax(scores, axis=-1))
    heads = jnp.einsum('fhqk,fkhc->fqhc', attn_probs, values, precision=lax.Precision.HIGHEST)
    heads = low_back(low(heads.reshape(frames, positions, model_width)))
    return low_back(jnp.einsum('fpd,de->fpe', heads, weights[:, 3 * model_width:], precision=lax.Precision.HIGHEST))

def temporal_mix(normed, weights):
    model_width = normed.shape[-1]
    positions = normed.shape[1]
    packed = low_back(low(jnp.einsum('fpd,de->fpe', normed, weights[:, :3 * model_width], precision=lax.Precision.HIGHEST)))
    packed = packed.reshape(FPV, positions, 3, H, HD)
    queries, key_rows, values = (packed[:, :, 0], packed[:, :, 1], packed[:, :, 2])
    scores = low_back(jnp.einsum('tphc,uphc->phtu', queries, key_rows, precision=lax.Precision.HIGHEST) * HD ** (-0.5))
    causal = jnp.arange(FPV)[:, None] >= jnp.arange(FPV)[None, :]
    attn_probs = low(jax.nn.softmax(jnp.where(causal, scores, masked_score), axis=-1))
    heads = jnp.einsum('phtu,uphc->tphc', attn_probs, values, precision=lax.Precision.HIGHEST)
    heads = low_back(low(heads.reshape(FPV, positions, model_width)))
    return low_back(jnp.einsum('fpd,de->fpe', heads, weights[:, 3 * model_width:], precision=lax.Precision.HIGHEST))

def forward(attn_w, ffn_w, small_w, video_in, video_codes):
    attn_low = low(attn_w)
    ffn_low = low(ffn_w)
    small_low = low(small_w)
    onehot = (video_codes[:, None] == jnp.arange(CODES)[None, :]).astype(jnp.float32)
    code_shift = jnp.dot(onehot, small_low[3:], precision=lax.Precision.HIGHEST)
    resid_zero = video_in + code_shift[:, None, :]
    normed_one = low(layer_norm(resid_zero, small_low[0]))
    resid_one = resid_zero + spatial_mix(normed_one, attn_low[0])
    normed_two = low(layer_norm(resid_one, small_low[1]))
    resid_two = resid_one + temporal_mix(normed_two, attn_low[1])
    normed_three = low(layer_norm(resid_two, small_low[2]))
    ffn_pre = low_back(jnp.einsum('fpd,de->fpe', normed_three, ffn_low[0], precision=lax.Precision.HIGHEST))
    ffn_act = low(jax.nn.gelu(ffn_pre))
    branch = low_back(jnp.einsum('fpe,de->fpd', ffn_act, ffn_low[1], precision=lax.Precision.HIGHEST))
    return resid_two + branch

def adamw(weight, moment_one, moment_two, gradient, step_rate, decay_coef):
    first_new = beta_first * moment_one + (1.0 - beta_first) * gradient
    second_new = beta_second * moment_two + (1.0 - beta_second) * gradient * gradient
    fix_first = 1.0 - beta_first ** STEP
    fix_second = 1.0 - beta_second ** STEP
    update = first_new / fix_first / (jnp.sqrt(second_new / fix_second) + eps_adam)
    return (weight - step_rate * (update + decay_coef * weight), first_new, second_new)

def reference(frames_in, action_codes, cotangent, attn_master, attn_first, attn_second, ffn_master, ffn_first, ffn_second, small_master, small_first, small_second):
    videos = FRAMES // FPV
    video_inputs = frames_in.astype(jnp.float32).reshape(videos, FPV, P_SIZE, D)
    video_code_rows = action_codes.reshape(videos, FPV)
    video_cots = cotangent.astype(jnp.float32).reshape(videos, FPV, P_SIZE, D)
    zeros_start = (jnp.zeros_like(attn_master), jnp.zeros_like(ffn_master), jnp.zeros_like(small_master))

    def video_step(running, entry):
        video_in, video_codes, video_cot = entry

        def video_fn(attn_w, ffn_w, small_w, inputs_f):
            return forward(attn_w, ffn_w, small_w, inputs_f, video_codes)
        video_out, pullback = jax.vjp(video_fn, attn_master, ffn_master, small_master, video_in)
        grad_attn, grad_ffn, grad_small, grad_input = pullback(video_cot)
        summed = (running[0] + grad_attn, running[1] + grad_ffn, running[2] + grad_small)
        return (summed, (video_out.astype(jnp.bfloat16), grad_input.astype(jnp.bfloat16)))
    grads, outputs = lax.scan(video_step, zeros_start, (video_inputs, video_code_rows, video_cots))
    grad_attn, grad_ffn, grad_small = grads
    block_out = outputs[0].reshape(FRAMES, P_SIZE, D)
    input_grad = outputs[1].reshape(FRAMES, P_SIZE, D)
    grad_norm = jnp.sqrt(jnp.sum(grad_attn * grad_attn) + jnp.sum(grad_ffn * grad_ffn) + jnp.sum(grad_small * grad_small))
    clip_factor = 1.0 / jnp.maximum(grad_norm, 1.0)
    small_decay = jnp.where(jnp.arange(3 + CODES)[:, None] >= 3, decay_rate, 0.0)
    attn_new = adamw(attn_master, attn_first, attn_second, grad_attn * clip_factor, rate_matrix, decay_rate)
    ffn_new = adamw(ffn_master, ffn_first, ffn_second, grad_ffn * clip_factor, rate_matrix, decay_rate)
    small_new = adamw(small_master, small_first, small_second, grad_small * clip_factor, rate_small, small_decay)
    return (block_out, input_grad, grad_norm, attn_new[0], attn_new[1], attn_new[2], ffn_new[0], ffn_new[1], ffn_new[2], small_new[0], small_new[1], small_new[2])
```

```python
import functools

import jax
import jax.numpy as jnp
from jax import lax
from jax.experimental import pallas as pl
from jax.experimental.pallas import tpu as pltpu
from jax.sharding import PartitionSpec as P

HD = 64
FPV = 16
CODES = 8
STEP = 5
BF = jnp.bfloat16
F32 = jnp.float32

eps_norm = 1e-05
beta_first = 0.5
beta_second = 0.5
rate_matrix = 0.02
rate_small = 0.3
decay_rate = 0.1
eps_adam = 1e-08
masked_score = -1000000000.0
score_scale = HD**-0.5

CORE, XPOS, YPOS, ZPOS, MEMBER = range(5)
ANY = pl.BlockSpec(memory_space=pl.ANY)
MIB = 1 << 20


def dot_nn(a, b):
    return lax.dot_general(a, b, (((1,), (0,)), ((), ())), preferred_element_type=F32)


def dot_nt(a, b):
    return lax.dot_general(a, b, (((1,), (1,)), ((), ())), preferred_element_type=F32)


def swap(value, axis, bit):
    size = lax.axis_size(axis)
    return lax.ppermute(value, axis, [(i, i ^ bit) for i in range(size)])


def shift_z(value, step):
    size = lax.axis_size("seq")
    return lax.ppermute(value, "seq", [(i, (i + 2 * step) % size) for i in range(size)])


def z_groups():
    size = lax.axis_size("seq")
    return [list(range(first, size, 2)) for first in range(2)]


def gather_z(piece):
    nz = lax.axis_size("seq") // 2
    if nz <= 4:
        return jnp.stack([piece] + [shift_z(piece, k) for k in range(1, nz)])
    whole = lax.all_gather(piece, "seq", axis_index_groups=z_groups())
    here = lax.axis_index("seq") // 2
    return jnp.take(whole, (here - jnp.arange(nz)) % nz, axis=0)


def scatter_z(parts):
    nz = lax.axis_size("seq") // 2
    if nz <= 4:
        come = [parts[0]] + [shift_z(parts[k], k) for k in range(1, nz)]
        total = come[0].astype(F32)
        for item in come[1:]:
            total = total + item.astype(F32)
        return total.astype(BF)
    here = lax.axis_index("seq") // 2
    ordered = jnp.take(parts, (jnp.arange(nz) - here) % nz, axis=0)
    return lax.psum_scatter(ordered, "seq", axis_index_groups=z_groups())


def column_part(block, start, width):
    return lax.dynamic_slice_in_dim(block, start, width, 2)


def gather_weights(block, kind, place):
    width = block.shape[2]
    if kind == "zyx":
        part = width // 4
        piece = column_part(block, (place[CORE] * 2 + place[XPOS]) * part, part)
    else:
        part = width // 2
        piece = column_part(block, place[CORE] * part, part)
    below = gather_z(piece)
    beside = swap(below, "seq", 1)
    stacks = [(below, 0, 0), (beside, 1, 0)]
    if kind == "zyx":
        stacks += [(swap(s, "grp", 2), y, 1) for s, y, _ in stacks]
    out = [(s, (y, 0, x)) for s, y, x in stacks]
    out += [(swap(s, "grp", 1), (y, 1, x)) for s, y, x in stacks]
    return [s for s, _ in out], [m if kind == "zyx" else (m[0], m[1], None) for _, m in out]


def add_low(a, b):
    return (a.astype(F32) + b.astype(F32)).astype(BF)


def reduce_grads(parts, kind):
    half = [add_low(parts[0][x], swap(parts[1][x], "grp", 1)) for x in range(2)]
    if kind == "xyz":
        quarter = add_low(half[0], swap(half[1], "grp", 2))
        rows = add_low(quarter[0], swap(quarter[1], "seq", 1))
        return scatter_z(rows)
    rows = [add_low(h[0], swap(h[1], "seq", 1)) for h in half]
    ends = [scatter_z(r) for r in rows]
    return add_low(ends[0], swap(ends[1], "grp", 2))


def share_quarters(quarter):
    beside = swap(quarter, "grp", 2)
    return [quarter, beside, swap(quarter, "grp", 1), swap(beside, "grp", 1)]


def exchange(pieces):
    return [pieces[0]] + [swap(pieces[j], "seq", j) for j in range(1, len(pieces))]


def start_weights(place, stacks, metas, target, sem):
    for stack, (y_rel, c_rel, x_rel) in zip(stacks, metas):
        nz, _, rows, width = stack.shape
        column = place[CORE] ^ c_rel
        if x_rel is not None:
            column = column * 2 + (place[XPOS] ^ x_rel)
        column = pl.multiple_of(column * width, 128)

        def one(k, carry, stack=stack, y_rel=y_rel, rows=rows, width=width, column=column, nz=nz):
            shard = lax.rem(place[ZPOS] - k + nz, nz) * 2 + (place[YPOS] ^ y_rel)
            row = pl.multiple_of(shard * rows, rows)
            pltpu.make_async_copy(
                stack.at[k], target.at[:, pl.ds(row, rows), pl.ds(column, width)], sem
            ).start()
            return carry

        if nz <= 4:
            for k in range(nz):
                one(k, 0)
        else:
            lax.fori_loop(0, nz, one, 0)


def wait_all(target, sem):
    pltpu.make_async_copy(target, target, sem).wait()


def start_grads(place, source, index, outs, sem):
    for rel, out in enumerate(outs):
        _, nz, _, rows, width = out.shape
        column = (place[CORE] ^ (rel // 2)) * 2 + (place[XPOS] ^ (rel % 2))
        column = pl.multiple_of(column * width, 128)
        for y_rel in range(2):

            def one(k, carry, out=out, y_rel=y_rel, column=column, nz=nz, rows=rows, width=width):
                shard = lax.rem(place[ZPOS] + k, nz) * 2 + (place[YPOS] ^ y_rel)
                row = pl.multiple_of(shard * rows, rows)
                pltpu.make_async_copy(
                    source.at[pl.ds(row, rows), pl.ds(column, width)],
                    out.at[y_rel, k, index],
                    sem,
                ).start()
                return carry

            if nz <= 4:
                for k in range(nz):
                    one(k, 0)
            else:
                lax.fori_loop(0, nz, one, 0)


def norm_parts(values):
    centre = values - jnp.mean(values, axis=-1, keepdims=True)
    spread = jnp.mean(centre * centre, axis=-1, keepdims=True)
    scale = lax.rsqrt(spread + eps_norm)
    return centre * scale, scale


def norm_back(values, h_grad, gain):
    xhat, scale = norm_parts(values)
    e = h_grad * gain
    inner = jnp.mean(e * xhat, axis=-1, keepdims=True)
    v_grad = scale * (e - jnp.mean(e, axis=-1, keepdims=True) - xhat * inner)
    return v_grad, jnp.sum(h_grad * xhat, axis=0, keepdims=True)


def two_heads(x):
    lane = lax.broadcasted_iota(jnp.int32, x.shape, 1)
    zero = jnp.zeros_like(x)
    return jnp.where(lane < HD, x, zero), jnp.where(lane < HD, zero, x)


def video_mask(rows, positions):
    key = lax.broadcasted_iota(jnp.int32, (rows, rows), 0)
    query = lax.broadcasted_iota(jnp.int32, (rows, rows), 1)
    return (lax.rem(key, positions) == lax.rem(query, positions)) & (key <= query)


def attend(packed_ref, heads_ref, lse_ref, mask):
    width = heads_ref.shape[-1]
    for pair in range(width // 128):
        lo = pair * 128
        queries = two_heads(packed_ref[0, :, lo : lo + 128] * jnp.asarray(score_scale, BF))
        keys = packed_ref[0, :, width + lo : width + lo + 128]
        values_t = packed_ref[0, :, 2 * width + lo : 2 * width + lo + 128].T
        out = []
        for half in range(2):
            scores = dot_nt(keys, queries[half])
            if mask is not None:
                scores = jnp.where(mask, scores, masked_score)
            top = jnp.max(scores, axis=0, keepdims=True)
            probs = jnp.exp(scores - top)
            total = jnp.sum(probs, axis=0, keepdims=True)
            mixed = dot_nn(values_t[half * HD : half * HD + HD], probs.astype(BF))
            out.append(mixed / total)
            lse_ref[0, 2 * pair + half : 2 * pair + half + 1, :] = top + jnp.log(total)
        heads_ref[0, :, lo : lo + 128] = jnp.concatenate(out, axis=0).astype(BF).T


def attend_back(packed_ref, heads_ref, heads_grad_ref, lse_ref, grad_ref, mask):
    width = heads_ref.shape[-1]
    for pair in range(width // 128):
        lo = pair * 128
        query = packed_ref[0, :, lo : lo + 128] * jnp.asarray(score_scale, BF)
        key = packed_ref[0, :, width + lo : width + lo + 128]
        value = packed_ref[0, :, 2 * width + lo : 2 * width + lo + 128]
        heads_grad = heads_grad_ref[:, lo : lo + 128]
        key_t = key.T
        mixed_t = (heads_grad.astype(F32) * heads_ref[0, :, lo : lo + 128].astype(F32)).T
        queries, head_grads = two_heads(query), two_heads(heads_grad)
        probs_two, score_two, query_grad = [], [], []
        for half in range(2):
            scores = dot_nt(key, queries[half])
            if mask is not None:
                scores = jnp.where(mask, scores, masked_score)
            probs = jnp.exp(scores - lse_ref[0, 2 * pair + half : 2 * pair + half + 1, :])
            delta = jnp.sum(mixed_t[half * HD : half * HD + HD], axis=0, keepdims=True)
            probs_grad = dot_nt(value, head_grads[half])
            score_grad = (probs * (probs_grad - delta)).astype(BF)
            probs_two.append(probs.astype(BF))
            score_two.append(score_grad)
            query_grad.append(dot_nn(key_t[half * HD : half * HD + HD], score_grad))
        value_grad = dot_nn(jnp.concatenate(probs_two, 1), jnp.concatenate(head_grads, 0))
        key_grad = dot_nn(jnp.concatenate(score_two, 1), jnp.concatenate(queries, 0))
        grad_ref[0, :, lo : lo + 128] = (
            (jnp.concatenate(query_grad, 0) * score_scale).astype(BF).T
        )
        grad_ref[0, :, width + lo : width + lo + 128] = key_grad.astype(BF)
        grad_ref[0, :, 2 * width + lo : 2 * width + lo + 128] = value_grad.astype(BF)


def gelu_both(pre):
    root = 0.7978845608028654
    square = pre * pre
    bend = jnp.tanh(root * pre * (1.0 + 0.044715 * square))
    half = 0.5 * (1.0 + bend)
    slope = half + 0.5 * pre * (1.0 - bend * bend) * (root * (1.0 + 3 * 0.044715 * square))
    return pre * half, slope


def spatial_fwd_body(
    metas_qkv, metas_out, place, frames_ref, shift_ref, gain_ref, *refs
):
    n_qkv, n_out = len(metas_qkv), len(metas_out)
    qkv_stacks, out_stacks = refs[:n_qkv], refs[n_qkv : n_qkv + n_out]
    refs = refs[n_qkv + n_out :]
    packed_ref, heads_ref, lse_ref, normed_ref = refs[:4]
    piece_refs = refs[4:8]
    w_qkv, w_out, resid, sems = refs[8:]
    step = pl.program_id(0)

    @pl.when(step == 0)
    def _():
        start_weights(place, qkv_stacks, metas_qkv, w_qkv, sems.at[0])
        start_weights(place, out_stacks, metas_out, w_out, sems.at[1])
        wait_all(w_qkv, sems.at[0])
        wait_all(w_out, sems.at[1])

    values = frames_ref[0].astype(F32) + shift_ref[0]
    xhat, _ = norm_parts(values)
    normed = (xhat * gain_ref[0:1, :]).astype(BF)
    normed_ref[0] = normed
    width = normed.shape[1]
    for b in range(3):
        packed_ref[0, :, b * width : (b + 1) * width] = dot_nn(normed, w_qkv[b]).astype(BF)
    attend(packed_ref, heads_ref, lse_ref, None)
    resid[...] = (values + dot_nn(heads_ref[0], w_out[0])).astype(BF)
    count = piece_refs[0].shape[1]
    for j, piece in enumerate(piece_refs):
        first = pl.multiple_of((place[MEMBER] ^ j) * count, count)
        piece[0] = resid[pl.ds(first, count), :]


def temporal_fwd_body(metas, place, *refs):
    n = len(metas)
    piece_refs, gain_ref, stacks = refs[:4], refs[4], refs[5 : 5 + n]
    packed_ref, heads_ref, lse_ref, normed_ref, tokens_ref, resid_ref, third_ref = refs[5 + n : 12 + n]
    weights, tokens, sems = refs[12 + n :]
    step = pl.program_id(0)

    @pl.when(step == 0)
    def _():
        start_weights(place, stacks, metas, weights, sems.at[0])

    frames, positions = piece_refs[0].shape[0], piece_refs[0].shape[1]
    for j, piece in enumerate(piece_refs):
        tokens[pl.ds((place[MEMBER] ^ j) * frames, frames)] = piece[...]
    low = tokens[...].reshape(tokens_ref.shape[1:])
    tokens_ref[0] = low
    values = low.astype(F32)
    xhat, _ = norm_parts(values)
    normed = (xhat * gain_ref[1:2, :]).astype(BF)
    normed_ref[0] = normed

    @pl.when(step == 0)
    def _():
        wait_all(weights, sems.at[0])

    width = normed.shape[1]
    for b in range(3):
        packed_ref[0, :, b * width : (b + 1) * width] = dot_nn(normed, weights[b]).astype(BF)
    attend(packed_ref, heads_ref, lse_ref, video_mask(low.shape[0], positions))
    resid = values + dot_nn(heads_ref[0], weights[3])
    resid_ref[0] = resid
    xhat, _ = norm_parts(resid)
    third_ref[0] = (xhat * gain_ref[2:3, :]).astype(BF)


def ffn_body(metas, first, last, place, *refs):
    n = len(metas)
    third_ref, cot_ref, resid_ref, dx_in = refs[:4]
    stacks = refs[4 : 4 + n]
    outs = refs[4 + n : 8 + n]
    refs = refs[8 + n :]
    if last:
        dx_out, piece_refs, refs = refs[0], refs[1:5], refs[5:]
    else:
        resid_out, dx_out, refs = refs[0], refs[1], refs[2:]
    third, cot, third_t, cot_t, acc, dx, weights, act, pre_grad, staging, sems = refs
    tokens, width = third.shape
    blocks = weights.shape[0] // 2
    chunk = 256
    loads = [(third_ref, third, 0), (cot_ref, cot, 1), (resid_ref, acc, 2)]
    if not first:
        loads.append((dx_in, dx, 3))
    for source, target, s in loads:
        pltpu.make_async_copy(source, target, sems.at[s]).start()
    start_weights(place, stacks, metas, weights, sems.at[4])
    for source, target, s in loads[:2]:
        pltpu.make_async_copy(source, target, sems.at[s]).wait()
    for r in range(tokens // chunk):
        rows = slice(r * chunk, (r + 1) * chunk)
        third_t[:, rows] = third[rows, :].T
        cot_t[:, rows] = cot[rows, :].T
    wait_all(weights, sems.at[4])
    for source, target, s in loads[2:]:
        pltpu.make_async_copy(source, target, sems.at[s]).wait()
    for b in range(blocks):
        for r in range(tokens // chunk):
            rows = slice(r * chunk, (r + 1) * chunk)
            pre = dot_nn(third[rows, :], weights[b])
            act_grad = dot_nn(cot[rows, :], weights[blocks + b])
            act_now, slope = gelu_both(pre)
            act_now = act_now.astype(BF)
            grad_now = (act_grad * slope).astype(BF)
            act[rows, :] = act_now
            pre_grad[rows, :] = grad_now
            acc[rows, :] += dot_nt(act_now, weights[blocks + b])
            back = dot_nt(grad_now, weights[b])
            if first and b == 0:
                dx[rows, :] = back
            else:
                dx[rows, :] += back
        staging[b] = dot_nn(third_t[...], pre_grad[...]).astype(BF)
        start_grads(place, staging.at[b], b, outs, sems.at[5])
        staging[blocks + b] = dot_nn(cot_t[...], act[...]).astype(BF)
        start_grads(place, staging.at[blocks + b], blocks + b, outs, sems.at[5])
    pltpu.make_async_copy(dx, dx_out, sems.at[6]).start()
    if last:
        low = third
        low[...] = acc[...].astype(BF)
        frames, positions = piece_refs[0].shape[:2]
        tiles = tokens // 256
        per_tile = positions // tiles
        for j, piece in enumerate(piece_refs):
            for tile in range(tiles):
                for f in range(frames):
                    row = pl.multiple_of(
                        tile * (tokens // tiles)
                        + ((place[MEMBER] ^ j) * frames + f) * per_tile,
                        per_tile,
                    )
                    pltpu.make_async_copy(
                        low.at[pl.ds(row, per_tile)],
                        piece.at[f, pl.ds(tile * per_tile, per_tile)],
                        sems.at[7],
                    ).start()
        wait_all(low, sems.at[7])
    else:
        pltpu.make_async_copy(acc, resid_out, sems.at[7]).start()
        pltpu.make_async_copy(acc, resid_out, sems.at[7]).wait()
    pltpu.make_async_copy(dx, dx_out, sems.at[6]).wait()
    wait_all(staging, sems.at[5])


def add_gain(step, ref, row, value):
    @pl.when(step == 0)
    def _():
        ref[row : row + 1, :] = value

    @pl.when(step > 0)
    def _():
        ref[row : row + 1, :] += value


def temporal_bwd_body(metas, place, *refs):
    n = len(metas)
    dx_ref, cot_ref, resid_ref, tokens_ref, packed_ref, heads_ref, lse_ref, gain_ref = refs[:8]
    stacks = refs[8 : 8 + n]
    branch_ref, grad_ref, gains_out = refs[8 + n : 11 + n]
    piece_refs = refs[11 + n : 15 + n]
    weights, heads_grad, total, sems = refs[15 + n :]
    step = pl.program_id(0)

    @pl.when(step == 0)
    def _():
        start_weights(place, stacks, metas, weights, sems.at[0])

    back, gain_three = norm_back(resid_ref[0], dx_ref[0], gain_ref[2:3, :])
    add_gain(step, gains_out, 1, gain_three)
    grad_two = cot_ref[0].astype(F32) + back
    branch = grad_two.astype(BF)
    branch_ref[0] = branch

    @pl.when(step == 0)
    def _():
        wait_all(weights, sems.at[0])

    heads_grad[...] = dot_nt(branch, weights[3]).astype(BF)
    frames, positions = piece_refs[0].shape[0], piece_refs[0].shape[1]
    attend_back(
        packed_ref, heads_ref, heads_grad, lse_ref, grad_ref, video_mask(branch.shape[0], positions)
    )
    width = branch.shape[1]
    normed_grad = dot_nt(grad_ref[0, :, :width], weights[0])
    for b in range(1, 3):
        normed_grad = normed_grad + dot_nt(grad_ref[0, :, b * width : (b + 1) * width], weights[b])
    back, gain_two = norm_back(tokens_ref[0].astype(F32), normed_grad, gain_ref[1:2, :])
    add_gain(step, gains_out, 0, gain_two)
    total[...] = (grad_two + back).astype(BF).reshape(total.shape)
    for j, piece in enumerate(piece_refs):
        piece[...] = total[pl.ds((place[MEMBER] ^ j) * frames, frames)]


def spatial_bwd_body(metas_qkv, metas_out, place, *refs):
    n_qkv, n_out = len(metas_qkv), len(metas_out)
    piece_refs = refs[:4]
    frames_ref, shift_ref, packed_ref, heads_ref, lse_ref, gain_ref = refs[4:10]
    refs = refs[10:]
    qkv_stacks, out_stacks = refs[:n_qkv], refs[n_qkv : n_qkv + n_out]
    refs = refs[n_qkv + n_out :]
    branch_ref, grad_ref, input_ref, gain_out, column_out = refs[:5]
    w_qkv, w_out, heads_grad, sems = refs[5:]
    step = pl.program_id(0)

    @pl.when(step == 0)
    def _():
        start_weights(place, out_stacks, metas_out, w_out, sems.at[1])
        start_weights(place, qkv_stacks, metas_qkv, w_qkv, sems.at[0])
        wait_all(w_out, sems.at[1])
        wait_all(w_qkv, sems.at[0])

    count = piece_refs[0].shape[1]
    for j, piece in enumerate(piece_refs):
        first = pl.multiple_of((place[MEMBER] ^ j) * count, count)
        branch_ref[0, pl.ds(first, count), :] = piece[0]
    branch = branch_ref[0]
    heads_grad[...] = dot_nt(branch, w_out[0]).astype(BF)
    attend_back(packed_ref, heads_ref, heads_grad, lse_ref, grad_ref, None)
    width = branch.shape[1]
    normed_grad = dot_nt(grad_ref[0, :, :width], w_qkv[0])
    for b in range(1, 3):
        normed_grad = normed_grad + dot_nt(grad_ref[0, :, b * width : (b + 1) * width], w_qkv[b])
    values = frames_ref[0].astype(F32) + shift_ref[0]
    back, gain_one = norm_back(values, normed_grad, gain_ref[0:1, :])
    add_gain(step, gain_out, 0, gain_one)
    grad_zero = branch.astype(F32) + back
    input_ref[0] = grad_zero.astype(BF)
    column_out[0] = jnp.sum(grad_zero, axis=0, keepdims=True)


def weight_grad_body(place, normed_ref, heads_ref, grad_ref, branch_ref, *refs):
    outs = refs[:4]
    normed, heads, grad, branch, normed_t, heads_t, staging, sems = refs[4:]
    loads = [(normed_ref, normed), (grad_ref, grad), (heads_ref, heads), (branch_ref, branch)]
    for s, (source, target) in enumerate(loads):
        pltpu.make_async_copy(source, target, sems.at[s]).start()
    tokens, width = normed.shape
    chunk = 256

    def wait(s):
        pltpu.make_async_copy(loads[s][0], loads[s][1], sems.at[s]).wait()

    def turn(source, target):
        for r in range(tokens // chunk):
            rows = slice(r * chunk, (r + 1) * chunk)
            target[:, rows] = source[rows, :].T

    wait(0)
    turn(normed, normed_t)
    wait(1)
    for b in range(3):
        staging[b] = dot_nn(normed_t[...], grad[:, b * width : (b + 1) * width]).astype(BF)
        start_grads(place, staging.at[b], b, outs, sems.at[4])
    wait(2)
    turn(heads, heads_t)
    wait(3)
    staging[3] = dot_nn(heads_t[...], branch[...]).astype(BF)
    start_grads(place, staging.at[3], 3, outs, sems.at[4])
    wait_all(staging, sems.at[4])


def update(weight, moment_one, moment_two, gradient, step_rate, decay_coef):
    first_new = beta_first * moment_one + (1.0 - beta_first) * gradient
    second_new = beta_second * moment_two + (1.0 - beta_second) * gradient * gradient
    fix_first = 1.0 - beta_first**STEP
    fix_second = 1.0 - beta_second**STEP
    change = first_new / fix_first / (jnp.sqrt(second_new / fix_second) + eps_adam)
    return weight - step_rate * (change + decay_coef * weight), first_new, second_new


def update_body(pick, place, clip, *refs):
    lots = [refs[:4], refs[4:8]]
    master, first, second, master_new, first_new, second_new = refs[8:]
    which = pick(pl.program_id(0), pl.program_id(1))
    for lot, pieces in enumerate(lots):

        @pl.when(which == lot)
        def _(pieces=pieces):
            for rel, piece in enumerate(pieces):
                width = piece.shape[2]
                column = (place[CORE] ^ (rel // 2)) * 2 + (place[XPOS] ^ (rel % 2))
                at = pl.ds(pl.multiple_of(column * width, 128), width)
                new = update(
                    master[0, :, at],
                    first[0, :, at],
                    second[0, :, at],
                    piece[0].astype(F32) * clip[0],
                    rate_matrix,
                    decay_rate,
                )
                master_new[0, :, at], first_new[0, :, at], second_new[0, :, at] = new


def join_body(place, *refs):
    pieces, out_ref, sems = refs[:4], refs[4], refs[5]
    count = pieces[0].shape[1]
    copies = []
    for j, piece in enumerate(pieces):
        first = pl.multiple_of((place[MEMBER] ^ j) * count, count)
        copies.append(
            pltpu.make_async_copy(piece, out_ref.at[:, pl.ds(first, count)], sems.at[j])
        )
    for copy in copies:
        copy.start()
    for copy in copies:
        copy.wait()


def tile_body(place, *refs):
    pieces, out_ref, tokens = refs[:4], refs[4], refs[5]
    frames = pieces[0].shape[0]
    for j, piece in enumerate(pieces):
        tokens[pl.ds((place[MEMBER] ^ j) * frames, frames)] = piece[...]
    out_ref[0] = tokens[...].reshape(out_ref.shape[1:])


def call(body, place, args, in_specs, out_specs, out_shape, scratch, grid=(1,), limit=60, flops=0, scalars=1):
    return pl.pallas_call(
        body,
        out_shape=out_shape,
        grid_spec=pltpu.PrefetchScalarGridSpec(
            num_scalar_prefetch=scalars,
            grid=grid,
            in_specs=in_specs,
            out_specs=out_specs,
            scratch_shapes=scratch,
        ),
        compiler_params=pltpu.CompilerParams(vmem_limit_bytes=limit * MIB),
        cost_estimate=pl.CostEstimate(flops=flops, bytes_accessed=16 * MIB, transcendentals=0),
    )(*place, *args)


def tile(*shape):
    return pl.BlockSpec((1,) + shape, lambda i, *_: (i,) + (0,) * len(shape))


def fixed(*shape):
    return pl.BlockSpec(shape, lambda i, *_: (0,) * len(shape))


def shape_of(*shape, dtype=BF):
    return jax.ShapeDtypeStruct(shape, dtype)


def shards(
    frames_in,
    action_codes,
    cotangent,
    attn_master,
    attn_first,
    attn_second,
    ffn_master,
    ffn_first,
    ffn_second,
    small_master,
    small_first,
    small_second,
):
    frames, positions, width = frames_in.shape
    heads_n = width // HD
    members = FPV // frames
    part = positions // members
    spot = positions // FPV
    tiles = part // spot
    rows_tile = FPV * spot
    tokens = tiles * rows_tile
    seq_size = lax.axis_size("seq")
    nz = seq_size // 2
    seq, grp = lax.axis_index("seq"), lax.axis_index("grp")
    place = jnp.stack([grp % 2, grp // 2, seq % 2, seq // 2, seq % members]).astype(jnp.int32)
    spots = (place,)
    local_rows = attn_master.shape[1]

    def blocks(master, picks):
        return jnp.stack(
            [master[m, :, b * width : (b + 1) * width] for m, b in picks]
        ).astype(BF)

    qkv_s, meta_qkv_s = gather_weights(blocks(attn_master, [(0, 0), (0, 1), (0, 2)]), "zy", place)
    small_low = small_master.astype(BF)
    if seq_size <= 8:
        small_all = jnp.stack(
            [small_low] + [lax.ppermute(small_low, "seq", [(i, i ^ j) for i in range(seq_size)]) for j in range(1, seq_size)]
        )
        small_all = jnp.take(small_all, jnp.arange(seq_size) ^ seq, axis=0)
    else:
        small_all = lax.all_gather(small_low, "seq")
    small_w = small_all.transpose(1, 0, 2).reshape(small_low.shape[0], width)
    out_s, meta_out_s = gather_weights(blocks(attn_master, [(0, 3)]), "zyx", place)
    all_t, meta_t = gather_weights(blocks(attn_master, [(1, b) for b in range(4)]), "zyx", place)
    ffn_groups = []
    for group, kind in ((0, "zyx"), (1, "zy")):
        picks = [(m, 2 * group + b) for m in range(2) for b in range(2)]
        ffn_groups.append(gather_weights(blocks(ffn_master, picks), kind, place))

    gains = small_w[:3].astype(F32)
    onehot = (action_codes[:, None] == jnp.arange(CODES)[None, :]).astype(BF)
    code_shift = jnp.dot(onehot, small_w[3:], preferred_element_type=F32)[:, None, :]

    def position_part(array, j):
        return lax.dynamic_slice_in_dim(array, (place[MEMBER] ^ j) * part, part, 1)

    cot_pieces = exchange([position_part(cotangent, j) for j in range(members)])
    piece_spec = pl.BlockSpec((frames, spot, width), lambda i, *_: (0, i, 0))
    cot_tiles = call(
        tile_body,
        spots,
        cot_pieces,
        [piece_spec] * members,
        tile(rows_tile, width),
        shape_of(tiles, rows_tile, width),
        [pltpu.VMEM((FPV, spot, width), BF)],
        grid=(tiles,),
    )

    part_spec = pl.BlockSpec((1, part, width), lambda i, *_: (i, 0, 0))
    sems = pltpu.SemaphoreType.DMA
    result = call(
        functools.partial(spatial_fwd_body, meta_qkv_s, meta_out_s),
        spots,
        [frames_in, code_shift, gains, *qkv_s, *out_s],
        [tile(positions, width), tile(1, width), fixed(3, width)] + [ANY] * (len(qkv_s) + len(out_s)),
        [tile(positions, 3 * width), tile(positions, width), tile(heads_n, positions), tile(positions, width)]
        + [part_spec] * members,
        [
            shape_of(frames, positions, 3 * width),
            shape_of(frames, positions, width),
            shape_of(frames, heads_n, positions, dtype=F32),
            shape_of(frames, positions, width),
        ]
        + [shape_of(frames, part, width)] * members,
        [
            pltpu.VMEM((3, width, width), BF),
            pltpu.VMEM((1, width, width), BF),
            pltpu.VMEM((positions, width), BF),
            sems((2,)),
        ],
        grid=(frames,),
        flops=9 * 10**9,
    )
    packed_s, heads_s, lse_s, normed_s = result[:4]
    token_pieces = exchange(result[4:])

    tile_shapes = shape_of(tiles, rows_tile, width)
    packed_t, heads_t, lse_t, normed_t, tokens_t, resid_two, third = call(
        functools.partial(temporal_fwd_body, meta_t),
        spots,
        [*token_pieces, gains, *all_t],
        [piece_spec] * members + [fixed(3, width)] + [ANY] * len(all_t),
        [tile(rows_tile, 3 * width), tile(rows_tile, width), tile(heads_n, rows_tile)]
        + [tile(rows_tile, width)] * 4,
        [
            shape_of(tiles, rows_tile, 3 * width),
            tile_shapes,
            shape_of(tiles, heads_n, rows_tile, dtype=F32),
            tile_shapes,
            tile_shapes,
            shape_of(tiles, rows_tile, width, dtype=F32),
            tile_shapes,
        ],
        [pltpu.VMEM((4, width, width), BF), pltpu.VMEM((FPV, spot, width), BF), sems((1,))],
        grid=(tiles,),
        flops=9 * 10**9,
    )

    grad_shape = shape_of(2, nz, 4, local_rows, width // 4)
    flat = lambda array: array.reshape(tokens, width)
    resid_now, dx = flat(resid_two), flat(resid_two)
    ffn_grads = []
    full32 = shape_of(tokens, width, dtype=F32)
    for group, (stacks, metas) in enumerate(ffn_groups):
        first, last = group == 0, group == len(ffn_groups) - 1
        ends = [full32] + [shape_of(frames, part, width)] * members if last else [full32, full32]
        outs = call(
            functools.partial(ffn_body, metas, first, last),
            spots,
            [flat(third), flat(cot_tiles), resid_now, dx, *stacks],
            [ANY] * (4 + len(stacks)),
            [ANY] * (4 + len(ends)),
            [grad_shape] * 4 + ends,
            [pltpu.VMEM((tokens, width), BF)] * 2
            + [pltpu.VMEM((width, tokens), BF)] * 2
            + [pltpu.VMEM((tokens, width), F32)] * 2
            + [pltpu.VMEM((4, width, width), BF)]
            + [pltpu.VMEM((tokens, width), BF)] * 2
            + [pltpu.VMEM((4, width, width), BF), sems((8,))],
            flops=26 * 10**9,
        )
        ffn_grads.append(outs[:4])
        if last:
            dx, block_pieces = outs[4], outs[5:]
        else:
            resid_now, dx = outs[4], outs[5]

    def reduced(parts, kind):
        return reduce_grads([[parts[0], parts[1]], [parts[2], parts[3]]], kind)

    quarters = {"ffn0": reduced(ffn_grads[0], "xyz"), "ffn1": reduced(ffn_grads[1], "yzx")}

    block_pieces = exchange(block_pieces)
    join = functools.partial(
        call,
        join_body,
        spots,
        in_specs=[ANY] * members,
        out_specs=ANY,
        out_shape=shape_of(frames, positions, width),
        scratch=[sems((members,))],
    )
    block_out = join(block_pieces)

    outs = call(
        functools.partial(temporal_bwd_body, meta_t),
        spots,
        [dx.reshape(resid_two.shape), cot_tiles, resid_two, tokens_t, packed_t, heads_t, lse_t, gains, *all_t],
        [tile(rows_tile, width)] * 4
        + [tile(rows_tile, 3 * width), tile(rows_tile, width), tile(heads_n, rows_tile), fixed(3, width)]
        + [ANY] * len(all_t),
        [tile(rows_tile, width), tile(rows_tile, 3 * width), fixed(2, width)] + [piece_spec] * members,
        [tile_shapes, shape_of(tiles, rows_tile, 3 * width), shape_of(2, width, dtype=F32)]
        + [shape_of(frames, part, width)] * members,
        [
            pltpu.VMEM((4, width, width), BF),
            pltpu.VMEM((rows_tile, width), BF),
            pltpu.VMEM((FPV, spot, width), BF),
            sems((1,)),
        ],
        grid=(tiles,),
        flops=10 * 10**9,
    )
    branch_t, grad_t, gains_two = outs[:3]
    grad_pieces = exchange(outs[3:])

    def weight_grads(normed, heads, grad, branch):
        return call(
            weight_grad_body,
            spots,
            [flat(normed), flat(heads), grad.reshape(tokens, 3 * width), flat(branch)],
            [ANY] * 4,
            [ANY] * 4,
            [grad_shape] * 4,
            [pltpu.VMEM((tokens, width), BF)] * 2
            + [pltpu.VMEM((tokens, 3 * width), BF), pltpu.VMEM((tokens, width), BF)]
            + [pltpu.VMEM((width, tokens), BF)] * 2
            + [pltpu.VMEM((4, width, width), BF), sems((5,))],
            flops=9 * 10**9,
        )

    quarters["attn1"] = reduced(weight_grads(normed_t, heads_t, grad_t, branch_t), "xyz")

    branch_s, grad_s, input_grad, gain_one, columns = call(
        functools.partial(spatial_bwd_body, meta_qkv_s, meta_out_s),
        spots,
        [*grad_pieces, frames_in, code_shift, packed_s, heads_s, lse_s, gains, *qkv_s, *out_s],
        [part_spec] * members
        + [tile(positions, width), tile(1, width), tile(positions, 3 * width), tile(positions, width)]
        + [tile(heads_n, positions), fixed(3, width)]
        + [ANY] * (len(qkv_s) + len(out_s)),
        [tile(positions, width), tile(positions, 3 * width), tile(positions, width), fixed(1, width), tile(1, width)],
        [
            shape_of(frames, positions, width),
            shape_of(frames, positions, 3 * width),
            shape_of(frames, positions, width),
            shape_of(1, width, dtype=F32),
            shape_of(frames, 1, width, dtype=F32),
        ],
        [
            pltpu.VMEM((3, width, width), BF),
            pltpu.VMEM((1, width, width), BF),
            pltpu.VMEM((positions, width), BF),
            sems((2,)),
        ],
        grid=(frames,),
        flops=10 * 10**9,
    )
    quarters["attn0"] = reduced(weight_grads(normed_s, heads_s, grad_s, branch_s), "yzx")

    table_grad = jnp.dot(
        onehot.astype(F32).T, columns[:, 0, :], precision=lax.Precision.HIGHEST
    )
    small_grad = lax.psum(
        jnp.concatenate([gain_one, gains_two, table_grad], axis=0), ("seq", "grp")
    )

    squares = sum(jnp.sum(jnp.square(q.astype(F32))) for q in quarters.values())
    total_squares = lax.psum(squares, ("seq", "grp")) + jnp.sum(small_grad * small_grad)
    grad_norm = jnp.sqrt(total_squares)
    clip_factor = 1.0 / jnp.maximum(grad_norm, 1.0)
    shared = {name: share_quarters(q) for name, q in quarters.items()}

    def updated(lots, pick, index, master, first, second):
        piece = lambda lot: pl.BlockSpec((1, local_rows, width // 4), lambda m, b, *_: (index(lot, m, b), 0, 0))
        block = pl.BlockSpec((1, local_rows, width), lambda m, b, *_: (m, 0, b))
        return call(
            functools.partial(update_body, pick),
            (place, clip_factor.reshape(1)),
            [*lots[0], *lots[1], master, first, second],
            [piece(0)] * 4 + [piece(1)] * 4 + [block] * 3,
            [block] * 3,
            [shape_of(*master.shape, dtype=F32)] * 3,
            [],
            grid=(2, master.shape[2] // width),
            scalars=2,
        )

    attn_new = updated(
        [shared["attn0"], shared["attn1"]],
        lambda m, b: m,
        lambda lot, m, b: jnp.where(m == lot, b, 3 if lot == 0 else 0),
        attn_master,
        attn_first,
        attn_second,
    )
    ffn_new = updated(
        [shared["ffn0"], shared["ffn1"]],
        lambda m, b: b // 2,
        lambda lot, m, b: m * 2 + b % 2,
        ffn_master,
        ffn_first,
        ffn_second,
    )
    small_decay = jnp.where(jnp.arange(3 + CODES)[:, None] >= 3, decay_rate, 0.0)
    small_cols = small_master.shape[1]
    small_mine = lax.dynamic_slice_in_dim(small_grad, seq * small_cols, small_cols, 1)
    small_new = update(
        small_master, small_first, small_second, small_mine * clip_factor, rate_small, small_decay
    )
    return (block_out, input_grad, grad_norm, *attn_new, *ffn_new, *small_new)


def solution(mesh):
    token = P(("grp", "seq"), None, None)
    matrix = P(None, "seq", None)
    small = P(None, "seq")
    return jax.shard_map(
        shards,
        mesh=mesh,
        in_specs=(token, P(("grp", "seq")), token) + (matrix,) * 6 + (small,) * 3,
        out_specs=(token, token, P()) + (matrix,) * 6 + (small,) * 3,
        check_vma=False,
    )
```

```python
import functools

import jax
import jax.numpy as jnp
from jax import lax
from jax.experimental import pallas as pl
from jax.experimental.pallas import tpu as pltpu
from jax.sharding import PartitionSpec as P

HD = 64
FPV = 16
CODES = 8
STEP = 5
BF = jnp.bfloat16
F32 = jnp.float32

eps_norm = 1e-05
beta_first = 0.5
beta_second = 0.5
rate_matrix = 0.02
rate_small = 0.3
decay_rate = 0.1
eps_adam = 1e-08
masked_score = -1000000000.0
score_scale = HD**-0.5

CORE, XPOS, YPOS, ZPOS, MEMBER = range(5)
ANY = pl.BlockSpec(memory_space=pl.ANY)
MIB = 1 << 20


def dot_nn(a, b):
    return lax.dot_general(a, b, (((1,), (0,)), ((), ())), preferred_element_type=F32)


def dot_nt(a, b):
    return lax.dot_general(a, b, (((1,), (1,)), ((), ())), preferred_element_type=F32)


def after(value, *others):
    return lax.optimization_barrier((value, *others))[0] if others else value


def swap(value, axis, bit):
    size = lax.axis_size(axis)
    return lax.ppermute(value, axis, [(i, i ^ bit) for i in range(size)])


def shift_z(value, step):
    size = lax.axis_size("seq")
    return lax.ppermute(value, "seq", [(i, (i + 2 * step) % size) for i in range(size)])


def z_groups():
    size = lax.axis_size("seq")
    return [list(range(first, size, 2)) for first in range(2)]


def gather_z(piece):
    nz = lax.axis_size("seq") // 2
    if nz <= 4:
        return jnp.stack([piece] + [shift_z(piece, k) for k in range(1, nz)])
    whole = lax.all_gather(piece, "seq", axis_index_groups=z_groups())
    here = lax.axis_index("seq") // 2
    return jnp.take(whole, (here - jnp.arange(nz)) % nz, axis=0)


def scatter_z(parts, *others):
    nz = lax.axis_size("seq") // 2
    if nz <= 4:
        come = [parts[0]] + [shift_z(parts[k], k) for k in range(1, nz)]
        total = come[0].astype(F32)
        for item in come[1:]:
            total = total + after(item, *others).astype(F32)
        return total.astype(BF)
    here = lax.axis_index("seq") // 2
    ordered = jnp.take(jnp.stack(parts), (jnp.arange(nz) - here) % nz, axis=0)
    return lax.psum_scatter(ordered, "seq", axis_index_groups=z_groups())


def column_part(block, start, width):
    return lax.dynamic_slice_in_dim(block, start, width, 2)


def quarter_mine(block, place):
    part = block.shape[2] // 4
    return column_part(block, (place[CORE] * 2 + place[XPOS]) * part, part)


def gather_weights(block, kind, place, begin=(), beside_after=(), across_after=(), cross=()):
    width = block.shape[2]
    if kind == "zyx":
        part = width // 4
        piece = column_part(block, (place[CORE] * 2 + place[XPOS]) * part, part)
    else:
        part = width // 2
        piece = column_part(block, place[CORE] * part, part)
    piece = after(piece, *begin)
    below = gather_z(piece)
    beside = swap(after(below, *beside_after), "seq", 1)
    stacks = [(below, 0, 0), (beside, 1, 0)]
    if kind == "zyx":
        stacks += [(swap(after(s, *across_after), "grp", 2), y, 1) for s, y, _ in stacks]
    out = [(s, (y, 0, x)) for s, y, x in stacks]
    out += [(swap(after(s, *cross), "grp", 1), (y, 1, x)) for s, y, x in stacks]
    return [s for s, _ in out], [m if kind == "zyx" else (m[0], m[1], None) for _, m in out]


def add_low(a, b):
    return (a.astype(F32) + b.astype(F32)).astype(BF)


def send_core(parts):
    return parts[0], swap(parts[1], "grp", 1)


def step_one(here, there):
    return add_low(here[0], there[0]), add_low(here[1], there[1])


def send_one(kept, sent, kind):
    return kept, swap(sent, "grp", 2) if kind == "xyz" else swap(sent, "seq", 1)


def step_two(kept, come, kind):
    if kind == "xyz":
        return add_low(kept[0], come[0]), add_low(kept[1], come[1])
    sums = [add_low(kept[k], come[k]) for k in range(kept.shape[0])]
    return sums[0], sums[1:]


def send_two(kept, sent, kind, *others):
    if kind == "xyz":
        return kept, swap(sent, "seq", 1)
    ends = scatter_z([kept, *sent], *others)
    return ends[0], ends[1]


def step_three(kept, come, kind):
    if kind == "xyz":
        sums = [add_low(kept[k], come[k]) for k in range(kept.shape[0])]
        return sums[0], sums[1:]
    return kept, come


def send_three(kept, sent, kind, *others):
    if kind == "xyz":
        return scatter_z([kept, *sent], *others)
    return add_low(kept, after(swap(sent, "grp", 2), *others))


def pinned(state, *others):
    return state[0], after(state[1], *others)


def before(value, *states):
    return after(value, *jax.tree.leaves(states))


def share_quarters(quarter):
    beside = swap(quarter, "grp", 2)
    return [quarter, beside, swap(quarter, "grp", 1), swap(beside, "grp", 1)]


def all_sum(value):
    for axis in ("grp", "seq"):
        size = lax.axis_size(axis)
        if size & (size - 1):
            value = lax.psum(value, axis)
            continue
        bit = 1
        while bit < size:
            if 4 * bit <= size:
                a, b, c = (swap(value, axis, bit * k) for k in (1, 2, 3))
                low = (lax.axis_index(axis) // (2 * bit)) % 2 == 0
                near, far = value + a, b + c
                value = jnp.where(low, near, far) + jnp.where(low, far, near)
                bit *= 4
            else:
                value = value + swap(value, axis, bit)
                bit *= 2
    return value


def exchange(pieces):
    return [pieces[0]] + [swap(pieces[j], "seq", j) for j in range(1, len(pieces))]


def start_weights(place, stacks, metas, target, sem):
    for stack, (y_rel, c_rel, x_rel) in zip(stacks, metas):
        nz, _, rows, width = stack.shape
        column = place[CORE] ^ c_rel
        if x_rel is not None:
            column = column * 2 + (place[XPOS] ^ x_rel)
        column = pl.multiple_of(column * width, 128)

        def one(k, carry, stack=stack, y_rel=y_rel, rows=rows, width=width, column=column, nz=nz):
            shard = lax.rem(place[ZPOS] - k + nz, nz) * 2 + (place[YPOS] ^ y_rel)
            row = pl.multiple_of(shard * rows, rows)
            pltpu.make_async_copy(
                stack.at[k], target.at[:, pl.ds(row, rows), pl.ds(column, width)], sem
            ).start()
            return carry

        if nz <= 4:
            for k in range(nz):
                one(k, 0)
        else:
            lax.fori_loop(0, nz, one, 0)


def quarter_column(g, width):
    return (g % 2 * 2 + g // 2) * width


def start_whole(stack, first, target, sem):
    count, _, rows, width = stack.shape
    n = target.shape[0]

    def one(s, carry):
        row = s * rows if isinstance(s, int) else pl.multiple_of(s * rows, rows)
        for g in range(4):
            pltpu.make_async_copy(
                stack.at[s * 4 + g, pl.ds(first, n)],
                target.at[:, pl.ds(row, rows), pl.ds(quarter_column(g, width), width)],
                sem,
            ).start()
        return carry

    if count <= 32:
        for s in range(count // 4):
            one(s, 0)
    else:
        lax.fori_loop(0, count // 4, one, 0)


def wait_all(target, sem):
    pltpu.make_async_copy(target, target, sem).wait()


def start_grads(place, kind, source, index, outs, sem):
    nz = outs[0].shape[2 if kind == "xyz" else 1]
    rows, width = outs[0].shape[-2:]
    for rel in range(4):
        out, x_rel = outs[rel // 2], rel % 2
        column = (place[CORE] ^ (rel // 2)) * 2 + (place[XPOS] ^ x_rel)
        column = pl.multiple_of(column * width, 128)
        for y_rel in range(2):

            def one(k, carry, out=out, x_rel=x_rel, y_rel=y_rel, column=column):
                shard = lax.rem(place[ZPOS] + k, nz) * 2 + (place[YPOS] ^ y_rel)
                row = pl.multiple_of(shard * rows, rows)
                target = out.at[x_rel, y_rel, k, index]
                if kind != "xyz":
                    target = out.at[y_rel, k, x_rel, index]
                pltpu.make_async_copy(
                    source.at[pl.ds(row, rows), pl.ds(column, width)], target, sem
                ).start()
                return carry

            if nz <= 4:
                for k in range(nz):
                    one(k, 0)
            else:
                lax.fori_loop(0, nz, one, 0)


def norm_parts(values):
    centre = values - jnp.mean(values, axis=-1, keepdims=True)
    spread = jnp.mean(centre * centre, axis=-1, keepdims=True)
    scale = lax.rsqrt(spread + eps_norm)
    return centre * scale, scale


def norm_back(values, h_grad, gain):
    xhat, scale = norm_parts(values)
    e = h_grad * gain
    inner = jnp.mean(e * xhat, axis=-1, keepdims=True)
    v_grad = scale * (e - jnp.mean(e, axis=-1, keepdims=True) - xhat * inner)
    return v_grad, jnp.sum(h_grad * xhat, axis=0, keepdims=True)


def two_heads(x):
    lane = lax.broadcasted_iota(jnp.int32, x.shape, 1)
    zero = jnp.zeros_like(x)
    return jnp.where(lane < HD, x, zero), jnp.where(lane < HD, zero, x)


def video_mask(rows, positions):
    key = lax.broadcasted_iota(jnp.int32, (rows, rows), 0)
    query = lax.broadcasted_iota(jnp.int32, (rows, rows), 1)
    return (lax.rem(key, positions) == lax.rem(query, positions)) & (key <= query)


def attend(packed_ref, heads_ref, lse_ref, mask):
    width = heads_ref.shape[-1]
    for pair in range(width // 128):
        lo = pair * 128
        queries = two_heads(packed_ref[0, :, lo : lo + 128] * jnp.asarray(score_scale, BF))
        keys = packed_ref[0, :, width + lo : width + lo + 128]
        values_t = packed_ref[0, :, 2 * width + lo : 2 * width + lo + 128].T
        out = []
        for half in range(2):
            scores = dot_nt(keys, queries[half])
            if mask is not None:
                scores = jnp.where(mask, scores, masked_score)
            top = jnp.max(scores, axis=0, keepdims=True)
            probs = jnp.exp(scores - top)
            total = jnp.sum(probs, axis=0, keepdims=True)
            mixed = dot_nn(values_t[half * HD : half * HD + HD], probs.astype(BF))
            out.append(mixed / total)
            lse_ref[0, 2 * pair + half : 2 * pair + half + 1, :] = top + jnp.log(total)
        heads_ref[0, :, lo : lo + 128] = jnp.concatenate(out, axis=0).astype(BF).T


def attend_back(packed_ref, heads_ref, heads_grad_ref, lse_ref, grad_ref, mask):
    width = heads_ref.shape[-1]
    for pair in range(width // 128):
        lo = pair * 128
        query = packed_ref[0, :, lo : lo + 128] * jnp.asarray(score_scale, BF)
        key = packed_ref[0, :, width + lo : width + lo + 128]
        value = packed_ref[0, :, 2 * width + lo : 2 * width + lo + 128]
        heads_grad = heads_grad_ref[0, :, lo : lo + 128]
        key_t = key.T
        mixed_t = (heads_grad.astype(F32) * heads_ref[0, :, lo : lo + 128].astype(F32)).T
        queries, head_grads = two_heads(query), two_heads(heads_grad)
        probs_two, score_two, query_grad = [], [], []
        for half in range(2):
            scores = dot_nt(key, queries[half])
            if mask is not None:
                scores = jnp.where(mask, scores, masked_score)
            probs = jnp.exp(scores - lse_ref[0, 2 * pair + half : 2 * pair + half + 1, :])
            delta = jnp.sum(mixed_t[half * HD : half * HD + HD], axis=0, keepdims=True)
            probs_grad = dot_nt(value, head_grads[half])
            score_grad = (probs * (probs_grad - delta)).astype(BF)
            probs_two.append(probs.astype(BF))
            score_two.append(score_grad)
            query_grad.append(dot_nn(key_t[half * HD : half * HD + HD], score_grad))
        value_grad = dot_nn(jnp.concatenate(probs_two, 1), jnp.concatenate(head_grads, 0))
        key_grad = dot_nn(jnp.concatenate(score_two, 1), jnp.concatenate(queries, 0))
        grad_ref[0, :, lo : lo + 128] = (
            (jnp.concatenate(query_grad, 0) * score_scale).astype(BF).T
        )
        grad_ref[0, :, width + lo : width + lo + 128] = key_grad.astype(BF)
        grad_ref[0, :, 2 * width + lo : 2 * width + lo + 128] = value_grad.astype(BF)


def gelu_both(pre):
    root = 0.7978845608028654
    square = pre * pre
    bend = jnp.tanh(root * pre * (1.0 + 0.044715 * square))
    half = 0.5 * (1.0 + bend)
    slope = half + 0.5 * pre * (1.0 - bend * bend) * (root * (1.0 + 3 * 0.044715 * square))
    return pre * half, slope


def start_layer(place, lots, refs, weights, sems):
    for i, (first, count, metas) in enumerate(lots):
        stacks, refs = refs[: len(metas)], refs[len(metas) :]
        start_weights(place, stacks, metas, weights.at[pl.ds(first, count)], sems.at[i])


def wait_layer(lots, weights, sems):
    for i, (first, count, _) in enumerate(lots):
        wait_all(weights.at[pl.ds(first, count)], sems.at[i])


def stacks_of(lots):
    return sum(len(metas) for _, _, metas in lots)


def project_in(values, gain, weights, normed_ref, packed_ref):
    xhat, _ = norm_parts(values)
    normed = (xhat * gain).astype(BF)
    normed_ref[0] = normed
    width = normed.shape[1]
    for b in range(3):
        packed_ref[0, :, b * width : (b + 1) * width] = dot_nn(normed, weights[b]).astype(BF)


def load_layer(place, lots, stacks, weights, sems):
    @pl.when(pl.program_id(0) == 0)
    def _():
        start_layer(place, lots, stacks, weights, sems)


def await_layer(lots, weights, sems):
    @pl.when(pl.program_id(0) == 0)
    def _():
        wait_layer(lots, weights, sems)


def spatial_in_body(lots, place, frames_ref, shift_ref, gain_ref, *refs):
    n = stacks_of(lots)
    stacks, (packed_ref, normed_ref, weights, sems) = refs[:n], refs[n:]
    load_layer(place, lots, stacks, weights, sems)
    await_layer(lots, weights, sems)
    values = frames_ref[0].astype(F32) + shift_ref[0]
    project_in(values, gain_ref[0:1, :], weights, normed_ref, packed_ref)


def temporal_fwd_body(place, *refs):
    piece_refs, gain_ref, stack = refs[:4], refs[4], refs[5]
    packed_ref, heads_ref, lse_ref, normed_ref, tokens_ref, resid_ref, third_ref = refs[6:13]
    weights, tokens, sems = refs[13:]
    load_whole(stack, weights, sems)
    frames, positions = piece_refs[0].shape[0], piece_refs[0].shape[1]
    for j, piece in enumerate(piece_refs):
        tokens[pl.ds((place[MEMBER] ^ j) * frames, frames)] = piece[...]
    low = tokens[...].reshape(tokens_ref.shape[1:])
    tokens_ref[0] = low
    values = low.astype(F32)
    await_whole(weights, sems)
    project_in(values, gain_ref[1:2, :], weights, normed_ref, packed_ref)
    attend(packed_ref, heads_ref, lse_ref, video_mask(low.shape[0], positions))
    resid = values + dot_nn(heads_ref[0], weights[3])
    resid_ref[0] = resid
    xhat, _ = norm_parts(resid)
    third_ref[0] = (xhat * gain_ref[2:3, :]).astype(BF)


def load_whole(stack, weights, sems):
    @pl.when(pl.program_id(0) == 0)
    def _():
        start_whole(stack, 0, weights, sems.at[0])


def await_whole(weights, sems):
    @pl.when(pl.program_id(0) == 0)
    def _():
        wait_all(weights, sems.at[0])


def attend_body(positions, place, packed_ref, heads_ref, lse_ref):
    mask = video_mask(packed_ref.shape[1], positions) if positions else None
    attend(packed_ref, heads_ref, lse_ref, mask)


def spatial_out_body(lots, place, heads_ref, frames_ref, shift_ref, *refs):
    n = stacks_of(lots)
    stacks, refs = refs[:n], refs[n:]
    piece_refs, (weights, resid, sems) = refs[:4], refs[4:]
    load_layer(place, lots, stacks, weights, sems)
    values = frames_ref[0].astype(F32) + shift_ref[0]
    await_layer(lots, weights, sems)
    resid[...] = (values + dot_nn(heads_ref[0], weights[lots[0][1] - 1])).astype(BF)
    count = piece_refs[0].shape[1]
    for j, piece in enumerate(piece_refs):
        first = pl.multiple_of((place[MEMBER] ^ j) * count, count)
        piece[0] = resid[pl.ds(first, count), :]


def ffn_body(group, base, last, kind, place, *refs):
    first = group == 0
    third_ref, cot_ref, resid_ref, stack = refs[:4]
    refs = refs[4:]
    if not first:
        dx_in, *refs = refs
    outs, refs = refs[:2], refs[2:]
    if last:
        dx_out, piece_refs, refs = refs[0], refs[1:5], refs[5:]
    else:
        resid_out, dx_out, refs = refs[0], refs[1], refs[2:]
    third, cot, third_t, cot_t, acc, dx, weights, act, pre_grad, staging, sems = refs
    tokens, width = third.shape
    blocks = weights.shape[0] // 2
    chunk = 256
    loads = [(third_ref, third, 0), (cot_ref, cot, 1), (resid_ref, acc, 2)]
    if not first:
        loads.append((dx_in, dx, 3))
    for source, target, s in loads:
        pltpu.make_async_copy(source, target, sems.at[s]).start()
    start_whole(stack, base, weights, sems.at[4])
    for source, target, s in loads[:2]:
        pltpu.make_async_copy(source, target, sems.at[s]).wait()
    for r in range(tokens // chunk):
        rows = slice(r * chunk, (r + 1) * chunk)
        third_t[:, rows] = third[rows, :].T
        cot_t[:, rows] = cot[rows, :].T
    wait_all(weights, sems.at[4])
    for source, target, s in loads[2:]:
        pltpu.make_async_copy(source, target, sems.at[s]).wait()

    def send(source, index):
        start_grads(place, kind, source, index, outs, sems.at[5])

    for b in range(blocks):
        for r in range(tokens // chunk):
            rows = slice(r * chunk, (r + 1) * chunk)
            pre = dot_nn(third[rows, :], weights[b])
            act_grad = dot_nn(cot[rows, :], weights[blocks + b])
            act_now, slope = gelu_both(pre)
            act_now = act_now.astype(BF)
            grad_now = (act_grad * slope).astype(BF)
            act[rows, :] = act_now
            pre_grad[rows, :] = grad_now
            acc[rows, :] += dot_nt(act_now, weights[blocks + b])
            back = dot_nt(grad_now, weights[b])
            if first and b == 0:
                dx[rows, :] = back
            else:
                dx[rows, :] += back
        staging[b] = dot_nn(third_t[...], pre_grad[...]).astype(BF)
        send(staging.at[b], b)
        staging[blocks + b] = dot_nn(cot_t[...], act[...]).astype(BF)
        send(staging.at[blocks + b], blocks + b)
    pltpu.make_async_copy(dx, dx_out, sems.at[6]).start()
    if last:
        low = third
        low[...] = acc[...].astype(BF)
        frames, positions = piece_refs[0].shape[:2]
        tiles = tokens // (FPV * 16)
        per_tile = positions // tiles
        for j, piece in enumerate(piece_refs):
            for tile in range(tiles):
                for f in range(frames):
                    row = pl.multiple_of(
                        tile * (tokens // tiles)
                        + ((place[MEMBER] ^ j) * frames + f) * per_tile,
                        per_tile,
                    )
                    pltpu.make_async_copy(
                        low.at[pl.ds(row, per_tile)],
                        piece.at[f, pl.ds(tile * per_tile, per_tile)],
                        sems.at[7],
                    ).start()
        wait_all(low, sems.at[7])
    else:
        pltpu.make_async_copy(acc, resid_out, sems.at[7]).start()
        pltpu.make_async_copy(acc, resid_out, sems.at[7]).wait()
    pltpu.make_async_copy(dx, dx_out, sems.at[6]).wait()
    wait_all(staging, sems.at[5])


def add_gain(step, ref, row, value):
    @pl.when(step == 0)
    def _():
        ref[row : row + 1, :] = value

    @pl.when(step > 0)
    def _():
        ref[row : row + 1, :] += value


def temporal_bwd_body(
    place, dx_ref, cot_ref, resid_ref, tokens_ref, packed_ref, heads_ref, lse_ref, gain_ref, stack, *refs
):
    branch_ref, grad_ref, gains_out = refs[:3]
    piece_refs = refs[3:7]
    weights, heads_grad, total, sems = refs[7:]
    step = pl.program_id(0)
    load_whole(stack, weights, sems)
    back, gain_three = norm_back(resid_ref[0], dx_ref[0], gain_ref[2:3, :])
    add_gain(step, gains_out, 1, gain_three)
    grad_two = cot_ref[0].astype(F32) + back
    branch = grad_two.astype(BF)
    branch_ref[0] = branch
    await_whole(weights, sems)
    heads_grad[0] = dot_nt(branch, weights[3]).astype(BF)
    frames, positions = piece_refs[0].shape[0], piece_refs[0].shape[1]
    mask = video_mask(branch.shape[0], positions)
    attend_back(packed_ref, heads_ref, heads_grad, lse_ref, grad_ref, mask)
    normed_grad = project_back(grad_ref, weights)
    back, gain_two = norm_back(tokens_ref[0].astype(F32), normed_grad, gain_ref[1:2, :])
    add_gain(step, gains_out, 0, gain_two)
    total[...] = (grad_two + back).astype(BF).reshape(total.shape)
    for j, piece in enumerate(piece_refs):
        piece[...] = total[pl.ds((place[MEMBER] ^ j) * frames, frames)]


def spatial_branch_body(lots, place, *refs):
    n = stacks_of(lots)
    piece_refs, stacks = refs[:4], refs[4 : 4 + n]
    branch_ref, heads_grad_ref, weights, sems = refs[4 + n :]
    load_layer(place, lots, stacks, weights, sems)
    count = piece_refs[0].shape[1]
    for j, piece in enumerate(piece_refs):
        first = pl.multiple_of((place[MEMBER] ^ j) * count, count)
        branch_ref[0, pl.ds(first, count), :] = piece[0]
    await_layer(lots, weights, sems)
    heads_grad_ref[0] = dot_nt(branch_ref[0], weights[lots[0][1] - 1]).astype(BF)


def attend_back_body(positions, place, packed_ref, heads_ref, heads_grad_ref, lse_ref, grad_ref):
    mask = video_mask(packed_ref.shape[1], positions) if positions else None
    attend_back(packed_ref, heads_ref, heads_grad_ref, lse_ref, grad_ref, mask)


def project_back(grad_ref, weights):
    width = weights.shape[1]
    out = dot_nt(grad_ref[0, :, :width], weights[0])
    for b in range(1, 3):
        out = out + dot_nt(grad_ref[0, :, b * width : (b + 1) * width], weights[b])
    return out


def spatial_end_body(lots, place, grad_ref, frames_ref, shift_ref, branch_ref, gain_ref, *refs):
    n = stacks_of(lots)
    stacks, (input_ref, gain_out, column_out, weights, sems) = refs[:n], refs[n:]
    load_layer(place, lots, stacks, weights, sems)
    await_layer(lots, weights, sems)
    normed_grad = project_back(grad_ref, weights)
    values = frames_ref[0].astype(F32) + shift_ref[0]
    back, gain_one = norm_back(values, normed_grad, gain_ref[0:1, :])
    add_gain(pl.program_id(0), gain_out, 0, gain_one)
    grad_zero = branch_ref[0].astype(F32) + back
    input_ref[0] = grad_zero.astype(BF)
    column_out[0] = jnp.sum(grad_zero, axis=0, keepdims=True)


def weight_grad_body(kinds, lots, place, *refs):
    pairs = 1 + max(pair for lot in lots for pair, _ in lot)
    sides, refs = refs[: 2 * pairs], refs[2 * pairs :]
    outs, refs = refs[: 2 * len(lots)], refs[2 * len(lots) :]
    held, refs = refs[: 2 * pairs], refs[2 * pairs :]
    turned, (staging, sems) = refs[:pairs], refs[pairs:]
    for s, (source, target) in enumerate(zip(sides, held)):
        pltpu.make_async_copy(source, target, sems.at[s]).start()
    tokens, width = held[0].shape
    chunk = 256
    done = set()
    at = 0
    for i, lot in enumerate(lots):
        for index, (pair, block) in enumerate(lot):
            if pair not in done:
                done.add(pair)
                wait_all(held[2 * pair], sems.at[2 * pair])
                for r in range(tokens // chunk):
                    rows = slice(r * chunk, (r + 1) * chunk)
                    turned[pair][:, rows] = held[2 * pair][rows, :].T
                wait_all(held[2 * pair + 1], sems.at[2 * pair + 1])
            columns = slice(block * width, (block + 1) * width)
            staging[at] = dot_nn(turned[pair][...], held[2 * pair + 1][:, columns]).astype(BF)
            start_grads(place, kinds[i], staging.at[at], index, outs[2 * i : 2 * i + 2], sems.at[2 * pairs])
            at += 1
    wait_all(staging, sems.at[2 * pairs])


def update(weight, moment_one, moment_two, gradient, step_rate, decay_coef):
    first_new = beta_first * moment_one + (1.0 - beta_first) * gradient
    second_new = beta_second * moment_two + (1.0 - beta_second) * gradient * gradient
    fix_first = 1.0 - beta_first**STEP
    fix_second = 1.0 - beta_second**STEP
    change = first_new * (step_rate / fix_first) / (jnp.sqrt(second_new * (1.0 / fix_second)) + eps_adam)
    return weight - (change + (step_rate * decay_coef) * weight), first_new, second_new


def update_body(lots, place, clip, *refs):
    pieces, refs = refs[: 4 * len(lots)], refs[4 * len(lots) :]
    master, first, second, master_new, first_new, second_new = refs
    matrix, block = pl.program_id(0), pl.program_id(1)
    for i, lot in enumerate(lots):
        mine = functools.reduce(
            jnp.logical_or, [(matrix == m) & (block == b) for m, b in lot]
        )

        @pl.when(mine)
        def _(i=i):
            for rel, piece in enumerate(pieces[4 * i : 4 * i + 4]):
                width = piece.shape[2]
                column = (place[CORE] ^ (rel // 2)) * 2 + (place[XPOS] ^ (rel % 2))
                at = pl.ds(pl.multiple_of(column * width, 128), width)
                new = update(
                    master[0, :, at],
                    first[0, :, at],
                    second[0, :, at],
                    piece[0].astype(F32) * clip[0],
                    rate_matrix,
                    decay_rate,
                )
                master_new[0, :, at], first_new[0, :, at], second_new[0, :, at] = new


def join_body(place, *refs):
    pieces, out_ref = refs[:4], refs[4]
    count = pieces[0].shape[1]
    for j, piece in enumerate(pieces):
        first = pl.multiple_of((place[MEMBER] ^ j) * count, count)
        out_ref[0, pl.ds(first, count), :] = piece[0]


def tile_body(place, *refs):
    pieces, out_ref, tokens = refs[:4], refs[4], refs[5]
    frames = pieces[0].shape[0]
    for j, piece in enumerate(pieces):
        tokens[pl.ds((place[MEMBER] ^ j) * frames, frames)] = piece[...]
    out_ref[0] = tokens[...].reshape(out_ref.shape[1:])


def call(body, place, args, in_specs, out_specs, out_shape, scratch, grid=(1,), limit=60, us=10, scalars=1, aliases={}):
    return pl.pallas_call(
        body,
        out_shape=out_shape,
        grid_spec=pltpu.PrefetchScalarGridSpec(
            num_scalar_prefetch=scalars,
            grid=grid,
            in_specs=in_specs,
            out_specs=out_specs,
            scratch_shapes=scratch,
        ),
        input_output_aliases=aliases,
        compiler_params=pltpu.CompilerParams(vmem_limit_bytes=limit * MIB),
        cost_estimate=pl.CostEstimate(flops=us * 10**9, bytes_accessed=MIB, transcendentals=0),
    )(*place, *args)


def tile(*shape):
    return pl.BlockSpec((1,) + shape, lambda i, *_: (i,) + (0,) * len(shape))


def fixed(*shape):
    return pl.BlockSpec(shape, lambda i, *_: (0,) * len(shape))


def shape_of(*shape, dtype=BF):
    return jax.ShapeDtypeStruct(shape, dtype)


def shards(
    frames_in,
    action_codes,
    cotangent,
    attn_master,
    attn_first,
    attn_second,
    ffn_master,
    ffn_first,
    ffn_second,
    small_master,
    small_first,
    small_second,
):
    frames, positions, width = frames_in.shape
    heads_n = width // HD
    members = FPV // frames
    part = positions // members
    spot = positions // FPV
    tiles = part // spot
    rows_tile = FPV * spot
    tokens = tiles * rows_tile
    seq_size = lax.axis_size("seq")
    nz = seq_size // 2
    seq, grp = lax.axis_index("seq"), lax.axis_index("grp")
    place = jnp.stack([grp % 2, grp // 2, seq % 2, seq // 2, seq % members]).astype(jnp.int32)
    spots = (place,)
    local_rows = attn_master.shape[1]

    def blocks(master, picks):
        return jnp.stack([master[m, :, b * width : (b + 1) * width] for m, b in picks]).astype(BF)

    small_low = small_master.astype(BF)
    if seq_size & (seq_size - 1) == 0:
        small_all = small_low[None]
        bit = 1
        while bit < seq_size:
            small_all = jnp.concatenate([small_all, swap(small_all, "seq", bit)])
            bit *= 2
        small_all = jnp.take(small_all, jnp.arange(seq_size) ^ seq, axis=0)
    else:
        small_all = lax.all_gather(small_low, "seq")
    small_w = small_all.transpose(1, 0, 2).reshape(small_low.shape[0], width)

    qk_s, meta_qk_s = gather_weights(blocks(attn_master, [(0, 0), (0, 1)]), "zyx", place)
    v_s, meta_v_s = gather_weights(
        blocks(attn_master, [(0, 2)]), "zy", place, begin=(qk_s[0],)
    )
    lots_in_s, in_s = ((0, 2, meta_qk_s), (2, 1, meta_v_s)), [*qk_s, *v_s]

    ffn_picks = [(m, 2 * group + b) for group in range(2) for m in range(2) for b in range(2)]
    early = jnp.concatenate(
        [
            quarter_mine(blocks(attn_master, [(1, b) for b in range(4)]), place),
            quarter_mine(blocks(ffn_master, ffn_picks[:4]), place),
        ]
    )
    late = quarter_mine(blocks(ffn_master, ffn_picks[4:]), place)
    early_all = lax.all_gather(early, ("seq", "grp"))
    gains = small_w[:3].astype(F32)
    onehot = (action_codes[:, None] == jnp.arange(CODES)[None, :]).astype(BF)
    code_shift = jnp.dot(onehot, small_w[3:], preferred_element_type=F32)[:, None, :]

    piece_spec = pl.BlockSpec((frames, spot, width), lambda i, *_: (0, i, 0))
    part_spec = pl.BlockSpec((1, part, width), lambda i, *_: (i, 0, 0))
    sems = pltpu.SemaphoreType.DMA

    def held(count):
        return [pltpu.VMEM((count, width, width), BF)]

    def layer(body, lots, stacks, args, in_specs, out_specs, out_shape, scratch, us):
        return call(
            functools.partial(body, lots),
            spots,
            [*args, *stacks],
            in_specs + [ANY] * len(stacks),
            out_specs,
            out_shape,
            held(sum(count for _, count, _ in lots)) + scratch + [sems((len(lots),))],
            grid=(frames,),
            limit=60,
            us=us,
        )

    wide, flat_tile = tile(positions, 3 * width), tile(positions, width)
    wide_shape = shape_of(frames, positions, 3 * width)
    tile_shape = shape_of(frames, positions, width)
    tile32_shape = shape_of(frames, positions, width, dtype=F32)
    lse_spec, lse_shape = tile(heads_n, positions), shape_of(frames, heads_n, positions, dtype=F32)
    piece_shapes = [shape_of(frames, part, width)] * members
    gain_shape = shape_of(1, width, dtype=F32)

    def attention(packed, step):
        return call(
            functools.partial(attend_body, step),
            spots,
            [packed],
            [wide],
            [flat_tile, lse_spec],
            [tile_shape, lse_shape],
            [],
            grid=(frames,),
            limit=60,
            us=22,
        )

    def attention_back(packed, heads, heads_grad, lse, step):
        return call(
            functools.partial(attend_back_body, step),
            spots,
            [packed, heads, heads_grad, lse],
            [wide, flat_tile, flat_tile, lse_spec],
            wide,
            wide_shape,
            [],
            grid=(frames,),
            limit=60,
            us=26,
        )

    packed_s, normed_s = layer(
        spatial_in_body,
        lots_in_s,
        in_s,
        [frames_in, code_shift, gains],
        [flat_tile, tile(1, width), fixed(3, width)],
        [wide, flat_tile],
        [wide_shape, tile_shape],
        [],
        12,
    )
    late_all = lax.all_gather(after(late, packed_s), ("seq", "grp"))
    heads_s, lse_s = attention(packed_s, 0)
    out_s, meta_out_s = gather_weights(
        blocks(attn_master, [(0, 3)]), "zyx", place, begin=(v_s[0],), across_after=(packed_s,), cross=(heads_s,)
    )
    lots_out_s = ((0, 1, meta_out_s),)
    pieces = layer(
        spatial_out_body,
        lots_out_s,
        out_s,
        [heads_s, frames_in, code_shift],
        [flat_tile, flat_tile, tile(1, width)],
        [part_spec] * members,
        piece_shapes,
        [pltpu.VMEM((positions, width), BF)],
        6,
    )
    token_pieces = exchange(pieces)

    packed_t, heads_t, lse_t, normed_t, tokens_t, resid_two, third = call(
        temporal_fwd_body,
        spots,
        [*token_pieces, gains, early_all],
        [piece_spec] * members + [fixed(3, width), ANY],
        [wide, flat_tile, lse_spec] + [flat_tile] * 4,
        [wide_shape, tile_shape, lse_shape, tile_shape, tile_shape, tile32_shape, tile_shape],
        held(4) + [pltpu.VMEM((FPV, spot, width), BF), sems((1,))],
        grid=(tiles,),
        us=37,
    )

    def position_part(array, j):
        return lax.dynamic_slice_in_dim(array, (place[MEMBER] ^ j) * part, part, 1)

    cot_pieces = exchange(
        [after(position_part(cotangent, j), *token_pieces) for j in range(members)]
    )
    cot_tiles = call(
        tile_body,
        spots,
        [before(cot_pieces[0], third), *cot_pieces[1:]],
        [piece_spec] * members,
        tile(rows_tile, width),
        shape_of(tiles, rows_tile, width),
        [pltpu.VMEM((FPV, spot, width), BF)],
        grid=(tiles,),
    )

    def split_shape(kind, n):
        lead = (2, 2, nz) if kind == "xyz" else (2, nz, 2)
        return shape_of(*lead, n, local_rows, width // 4)

    flat = lambda array: array.reshape(tokens, width)
    resid_now = flat(resid_two)
    full32 = shape_of(tokens, width, dtype=F32)
    parts_f = []
    groups = 2
    for group in range(groups):
        last = group == groups - 1
        ends = [full32] + [shape_of(frames, part, width)] * members if last else [full32, full32]
        args = [flat(third), flat(cot_tiles), resid_now, late_all if group else early_all]
        if group:
            args += [dx]
        outs = call(
            functools.partial(ffn_body, group, 0 if group else 4, last, "xyz"),
            spots,
            args,
            [ANY] * len(args),
            [ANY] * (2 + len(ends)),
            [split_shape("xyz", 4)] * 2 + ends,
            [pltpu.VMEM((tokens, width), BF)] * 2
            + [pltpu.VMEM((width, tokens), BF)] * 2
            + [pltpu.VMEM((tokens, width), F32)] * 2
            + [pltpu.VMEM((4, width, width), BF)]
            + [pltpu.VMEM((tokens, width), BF)] * 2
            + [pltpu.VMEM((4, width, width), BF), sems((8,))],
            us=41,
        )
        parts_f.append(outs[:2])
        if last:
            dx, block_pieces = outs[2], outs[3:]
        else:
            resid_now, dx = outs[2:]
            sum_e = send_core(outs[:2])

    quarters = {}
    sum_f = send_core(parts_f[1])
    sum_e = step_one(*pinned(sum_e, dx))
    dx = before(dx, sum_e)
    sum_e = send_one(*sum_e, "xyz")
    outs = call(
        temporal_bwd_body,
        spots,
        [dx.reshape(resid_two.shape), cot_tiles, resid_two, tokens_t, packed_t, heads_t, lse_t, gains, early_all],
        [flat_tile] * 4 + [wide, flat_tile, lse_spec, fixed(3, width), ANY],
        [flat_tile, wide, fixed(2, width)] + [piece_spec] * members,
        [tile_shape, wide_shape, shape_of(2, width, dtype=F32)] + piece_shapes,
        held(4)
        + [
            pltpu.VMEM((1, positions, width), BF),
            pltpu.VMEM((FPV, spot, width), BF),
            sems((1,)),
        ],
        grid=(tiles,),
        us=38,
    )
    branch_t, grad_t, gains_two = outs[:3]
    grad_pieces = exchange(outs[3:])
    block_pieces = exchange(block_pieces)
    join = functools.partial(
        call,
        body=join_body,
        place=spots,
        in_specs=[part_spec] * members,
        out_specs=tile(positions, width),
        out_shape=shape_of(frames, positions, width),
        scratch=[],
        grid=(frames,),
    )
    block_out = join(args=[before(block_pieces[0], grad_t), *block_pieces[1:]])


    def weight_grads(kinds, sides, *lots):
        sides = [side.reshape(tokens, -1) for side in sides]
        outs = call(
            functools.partial(weight_grad_body, kinds, lots),
            spots,
            sides,
            [ANY] * len(sides),
            [ANY] * (2 * len(lots)),
            [split_shape(kind, len(lot)) for kind, lot in zip(kinds, lots) for _ in range(2)],
            [pltpu.VMEM(side.shape, BF) for side in sides]
            + [pltpu.VMEM((width, tokens), BF)] * (len(sides) // 2)
            + [pltpu.VMEM((sum(map(len, lots)), width, width), BF), sems((len(sides) + 1,))],
            us=15,
        )
        return [outs[2 * i : 2 * i + 2] for i in range(len(lots))]

    kinds = ("xyz", "yzx")
    sum_f = step_one(*pinned(sum_f, grad_t))
    (parts_t,) = weight_grads(
        ("xyz",),
        [normed_t, before(grad_t, sum_f, block_out), heads_t, branch_t],
        [(0, 0), (0, 1), (0, 2), (1, 0)],
    )
    sum_f = send_one(*sum_f, "xyz")
    sum_t = send_core(parts_t)

    branch_s, heads_grad_s = layer(
        spatial_branch_body,
        lots_out_s,
        out_s,
        [before(grad_pieces[0], parts_t), *grad_pieces[1:]],
        [part_spec] * members,
        [flat_tile] * 2,
        [tile_shape] * 2,
        [],
        7,
    )
    sum_e = step_two(*pinned(sum_e, branch_s), "xyz")
    sum_t = step_one(*pinned(sum_t, branch_s))
    grad_s = attention_back(packed_s, heads_s, before(heads_grad_s, sum_e, sum_t), lse_s, 0)
    sum_e, sum_t = send_two(*sum_e, "xyz"), send_one(*sum_t, "xyz")
    sum_e = step_three(*pinned(sum_e, grad_s), "xyz")
    sum_f = step_two(*pinned(sum_f, grad_s), "xyz")
    parts_s = weight_grads(
        kinds,
        [normed_s, before(grad_s, sum_e, sum_f), heads_s, branch_s],
        [(0, 0), (0, 1)],
        [(0, 2), (1, 0)],
    )
    quarters["ffn0"] = send_three(*sum_e, "xyz", parts_s[0][0])
    sum_f = send_two(*sum_f, "xyz")
    sums_s = [send_core(parts) for parts in parts_s]
    sum_f = step_three(*pinned(sum_f, parts_s[0][0]), "xyz")
    sum_t = step_two(*pinned(sum_t, parts_s[0][0]), "xyz")
    input_grad, gain_one, columns = layer(
        spatial_end_body,
        lots_in_s,
        in_s,
        [grad_s, frames_in, code_shift, before(branch_s, parts_s, sum_t, sum_f), gains],
        [wide, flat_tile, tile(1, width), flat_tile, fixed(3, width)],
        [flat_tile, fixed(1, width), tile(1, width)],
        [tile_shape, gain_shape, shape_of(frames, 1, width, dtype=F32)],
        [],
        14,
    )
    sum_t = send_two(*sum_t, "xyz")
    quarters["ffn1"] = send_three(*sum_f, "xyz", columns)
    sums_s = [step_one(*pinned(s, columns)) for s in sums_s]
    sums_s = [send_one(*s, kind) for s, kind in zip(sums_s, kinds)]
    sum_t = step_three(*pinned(sum_t, columns), "xyz")
    quarters["t"] = send_three(*sum_t, "xyz")
    sums_s = [send_two(*step_two(*s, kind), kind) for s, kind in zip(sums_s, kinds)]
    sums_s = [send_three(*step_three(*s, kind), kind) for s, kind in zip(sums_s, kinds)]
    quarters["qk"], quarters["vo"] = sums_s

    table_grad = jnp.dot(
        onehot.astype(F32).T, columns[:, 0, :], precision=lax.Precision.HIGHEST
    )
    squares = sum(jnp.sum(jnp.square(q.astype(F32))) for q in quarters.values())
    sums = all_sum(
        jnp.concatenate(
            [gain_one, gains_two, table_grad, jnp.broadcast_to(squares, (1, width))], axis=0
        )
    )
    small_grad = sums[:-1]

    total_squares = sums[-1, 0] + jnp.sum(small_grad * small_grad)
    grad_norm = jnp.sqrt(total_squares)
    clip_factor = 1.0 / jnp.maximum(grad_norm, 1.0)
    shared = {name: share_quarters(q) for name, q in quarters.items()}

    def updated(lots, master, first, second):
        def piece(lot):
            def at(m, b, *_):
                entry = 0
                for k, (matrix, block) in enumerate(lot):
                    entry = jnp.where((m == matrix) & (b == block), k, entry)
                return entry, 0, 0

            return pl.BlockSpec((1, local_rows, width // 4), at)

        block = pl.BlockSpec((1, local_rows, width), lambda m, b, *_: (m, 0, b))
        return call(
            functools.partial(update_body, [lot for _, lot in lots]),
            (place, clip_factor.reshape(1)),
            [p for name, _ in lots for p in shared[name]] + [master, first, second],
            [piece(lot) for _, lot in lots for _ in range(4)] + [block] * 3,
            [block] * 3,
            [shape_of(*master.shape, dtype=F32)] * 3,
            [],
            grid=(2, master.shape[2] // width),
            scalars=2,
        )

    attn_new = updated(
        [("qk", [(0, 0), (0, 1)]), ("vo", [(0, 2), (0, 3)]), ("t", [(1, b) for b in range(4)])],
        attn_master,
        attn_first,
        attn_second,
    )
    ffn_new = updated([("ffn0", ffn_picks[:4]), ("ffn1", ffn_picks[4:])], ffn_master, ffn_first, ffn_second)
    small_decay = jnp.where(jnp.arange(3 + CODES)[:, None] >= 3, decay_rate, 0.0)
    small_cols = small_master.shape[1]
    small_mine = lax.dynamic_slice_in_dim(small_grad, seq * small_cols, small_cols, 1)
    small_new = update(
        small_master, small_first, small_second, small_mine * clip_factor, rate_small, small_decay
    )
    return (block_out, input_grad, grad_norm, *attn_new, *ffn_new, *small_new)


def solution(mesh):
    token = P(("grp", "seq"), None, None)
    matrix = P(None, "seq", None)
    small = P(None, "seq")
    return jax.shard_map(
        shards,
        mesh=mesh,
        in_specs=(token, P(("grp", "seq")), token) + (matrix,) * 6 + (small,) * 3,
        out_specs=(token, token, P()) + (matrix,) * 6 + (small,) * 3,
        check_vma=False,
    )
```

```python
import functools

import jax
import jax.numpy as jnp
from jax import lax
from jax.experimental import pallas as pl
from jax.experimental.pallas import tpu as pltpu
from jax.sharding import PartitionSpec as P

HD = 64
FPV = 16
CODES = 8
STEP = 5
BF = jnp.bfloat16
F32 = jnp.float32

eps_norm = 1e-05
beta_first = 0.5
beta_second = 0.5
rate_matrix = 0.02
rate_small = 0.3
decay_rate = 0.1
eps_adam = 1e-08
masked_score = -1000000000.0
score_scale = HD**-0.5

CORE, XPOS, YPOS, ZPOS, MEMBER = range(5)
ANY = pl.BlockSpec(memory_space=pl.ANY)
MIB = 1 << 20


def dot_nn(a, b):
    return lax.dot_general(a, b, (((1,), (0,)), ((), ())), preferred_element_type=F32)


def dot_nt(a, b):
    return lax.dot_general(a, b, (((1,), (1,)), ((), ())), preferred_element_type=F32)


def after(value, *others):
    return lax.optimization_barrier((value, *others))[0] if others else value


def swap(value, axis, bit):
    size = lax.axis_size(axis)
    return lax.ppermute(value, axis, [(i, i ^ bit) for i in range(size)])


def shift_z(value, step):
    size = lax.axis_size("seq")
    return lax.ppermute(value, "seq", [(i, (i + 2 * step) % size) for i in range(size)])


def z_groups():
    size = lax.axis_size("seq")
    return [list(range(first, size, 2)) for first in range(2)]


def gather_z(piece, *others):
    nz = lax.axis_size("seq") // 2
    if nz <= 4:
        return jnp.stack([piece] + [after(shift_z(piece, k), *others) for k in range(1, nz)])
    whole = lax.all_gather(piece, "seq", axis_index_groups=z_groups())
    here = lax.axis_index("seq") // 2
    return jnp.take(whole, (here - jnp.arange(nz)) % nz, axis=0)


def column_part(block, start, width):
    return lax.dynamic_slice_in_dim(block, start, width, 2)


def quarter_mine(block, place):
    part = block.shape[2] // 4
    return column_part(block, (place[CORE] * 2 + place[XPOS]) * part, part)


def start_gather(block, kind, place, begin=(), then=()):
    width = block.shape[2]
    if kind == "zyx":
        part = width // 4
        piece = column_part(block, (place[CORE] * 2 + place[XPOS]) * part, part)
    else:
        part = width // 2
        piece = column_part(block, place[CORE] * part, part)
    below = gather_z(after(piece, *begin), *then)
    return below, swap(below, "seq", 1)


def finish_gather(below, beside, kind, across_after=(), cross=()):
    stacks = [(below, 0, 0), (beside, 1, 0)]
    if kind == "zyx":
        stacks += [(swap(after(s, *across_after), "grp", 2), y, 1) for s, y, _ in stacks]
    out = [(s, (y, 0, x)) for s, y, x in stacks]
    out += [(swap(after(s, *cross), "grp", 1), (y, 1, x)) for s, y, x in stacks]
    return [s for s, _ in out], [m if kind == "zyx" else (m[0], m[1], None) for _, m in out]


def gather_weights(block, kind, place, begin=()):
    return finish_gather(*start_gather(block, kind, place, begin), kind)


def add_low(*terms):
    return sum(term.astype(F32) for term in terms).astype(BF)


def send_core(parts):
    return [parts[0], swap(parts[1], "grp", 1)]


def step_one(terms, *others):
    terms = [terms[0], before(terms[1], others)]
    return [term[0] for term in terms], add_low(*[term[1] for term in terms])


def send_one(terms, sent, kind):
    return terms + [swap(sent, "grp", 2) if kind == "xyz" else swap(sent, "seq", 1)]


def step_two(terms, kind, *others):
    terms = terms[:-1] + [before(terms[-1], others)]
    if kind == "xyz":
        return [term[0] for term in terms], add_low(*[term[1] for term in terms])
    return step_z(terms)


def step_z(terms):
    nz = terms[0].shape[0]
    return [term[0] for term in terms], [add_low(*[term[k] for term in terms]) for k in range(1, nz)]


def send_z(terms, sent):
    nz = lax.axis_size("seq") // 2
    if nz <= 4:
        return terms + [shift_z(part, k + 1) for k, part in enumerate(sent)]
    here = lax.axis_index("seq") // 2
    parts = jnp.stack([add_low(*terms), *sent])
    ordered = jnp.take(parts, (jnp.arange(nz) - here) % nz, axis=0)
    return [lax.psum_scatter(ordered, "seq", axis_index_groups=z_groups())]


def send_two(terms, sent, kind):
    return terms + [swap(sent, "seq", 1)] if kind == "xyz" else send_z(terms, sent)


def step_three(terms, kind, *others):
    terms = terms[:-1] + [before(terms[-1], others)]
    if kind == "xyz":
        return step_z(terms)
    return [term[0] for term in terms], add_low(*[term[1] for term in terms])


def send_three(terms, sent, kind):
    return send_z(terms, sent) if kind == "xyz" else terms + [swap(sent, "grp", 2)]


def finish(terms, *others):
    return add_low(*terms[:-1], before(terms[-1], others))


def before(value, *states):
    return after(value, *jax.tree.leaves(states))


def share_quarters(quarter):
    beside = swap(quarter, "grp", 2)
    return [quarter, beside, swap(quarter, "grp", 1), swap(beside, "grp", 1)]


def all_sum(value):
    for axis in ("grp", "seq"):
        size = lax.axis_size(axis)
        if size & (size - 1):
            value = lax.psum(value, axis)
            continue
        bit = 1
        while bit < size:
            if 4 * bit <= size:
                a, b, c = (swap(value, axis, bit * k) for k in (1, 2, 3))
                low = (lax.axis_index(axis) // (2 * bit)) % 2 == 0
                near, far = value + a, b + c
                value = jnp.where(low, near, far) + jnp.where(low, far, near)
                bit *= 4
            else:
                value = value + swap(value, axis, bit)
                bit *= 2
    return value


def exchange(pieces):
    return [pieces[0]] + [swap(pieces[j], "seq", j) for j in range(1, len(pieces))]


def start_weights(place, stacks, metas, target, sem):
    for stack, (y_rel, c_rel, x_rel) in zip(stacks, metas):
        nz, _, rows, width = stack.shape
        column = place[CORE] ^ c_rel
        if x_rel is not None:
            column = column * 2 + (place[XPOS] ^ x_rel)
        column = pl.multiple_of(column * width, 128)

        def one(k, carry, stack=stack, y_rel=y_rel, rows=rows, width=width, column=column, nz=nz):
            shard = lax.rem(place[ZPOS] - k + nz, nz) * 2 + (place[YPOS] ^ y_rel)
            row = pl.multiple_of(shard * rows, rows)
            pltpu.make_async_copy(
                stack.at[k], target.at[:, pl.ds(row, rows), pl.ds(column, width)], sem
            ).start()
            return carry

        if nz <= 4:
            for k in range(nz):
                one(k, 0)
        else:
            lax.fori_loop(0, nz, one, 0)


def quarter_column(g, width):
    return (g % 2 * 2 + g // 2) * width


def start_whole(stack, first, target, sem):
    count, _, rows, width = stack.shape
    n = target.shape[0]

    def one(s, carry):
        row = s * rows if isinstance(s, int) else pl.multiple_of(s * rows, rows)
        for g in range(4):
            pltpu.make_async_copy(
                stack.at[s * 4 + g, pl.ds(first, n)],
                target.at[:, pl.ds(row, rows), pl.ds(quarter_column(g, width), width)],
                sem,
            ).start()
        return carry

    if count <= 32:
        for s in range(count // 4):
            one(s, 0)
    else:
        lax.fori_loop(0, count // 4, one, 0)


def wait_all(target, sem):
    pltpu.make_async_copy(target, target, sem).wait()


def start_grads(place, kind, source, index, outs, sem):
    nz = outs[0].shape[2 if kind == "xyz" else 1]
    rows, width = outs[0].shape[-2:]
    for rel in range(4):
        out, x_rel = outs[rel // 2], rel % 2
        column = (place[CORE] ^ (rel // 2)) * 2 + (place[XPOS] ^ x_rel)
        column = pl.multiple_of(column * width, 128)
        for y_rel in range(2):

            def one(k, carry, out=out, x_rel=x_rel, y_rel=y_rel, column=column):
                shard = lax.rem(place[ZPOS] + k, nz) * 2 + (place[YPOS] ^ y_rel)
                row = pl.multiple_of(shard * rows, rows)
                target = out.at[x_rel, y_rel, k, index]
                if kind != "xyz":
                    target = out.at[y_rel, k, x_rel, index]
                pltpu.make_async_copy(
                    source.at[pl.ds(row, rows), pl.ds(column, width)], target, sem
                ).start()
                return carry

            if nz <= 4:
                for k in range(nz):
                    one(k, 0)
            else:
                lax.fori_loop(0, nz, one, 0)


def norm_parts(values):
    centre = values - jnp.mean(values, axis=-1, keepdims=True)
    spread = jnp.mean(centre * centre, axis=-1, keepdims=True)
    scale = lax.rsqrt(spread + eps_norm)
    return centre * scale, scale


def norm_back(values, h_grad, gain):
    xhat, scale = norm_parts(values)
    e = h_grad * gain
    inner = jnp.mean(e * xhat, axis=-1, keepdims=True)
    v_grad = scale * (e - jnp.mean(e, axis=-1, keepdims=True) - xhat * inner)
    return v_grad, jnp.sum(h_grad * xhat, axis=0, keepdims=True)


def two_heads(x):
    lane = lax.broadcasted_iota(jnp.int32, x.shape, 1)
    zero = jnp.zeros_like(x)
    return jnp.where(lane < HD, x, zero), jnp.where(lane < HD, zero, x)


def video_mask(rows, positions):
    key = lax.broadcasted_iota(jnp.int32, (rows, rows), 0)
    query = lax.broadcasted_iota(jnp.int32, (rows, rows), 1)
    return (lax.rem(key, positions) == lax.rem(query, positions)) & (key <= query)


def attend(packed_ref, heads_ref, lse_ref, mask):
    width = heads_ref.shape[-1]
    for pair in range(width // 128):
        lo = pair * 128
        queries = two_heads(packed_ref[0, :, lo : lo + 128] * jnp.asarray(score_scale, BF))
        keys = packed_ref[0, :, width + lo : width + lo + 128]
        values_t = packed_ref[0, :, 2 * width + lo : 2 * width + lo + 128].T
        out = []
        for half in range(2):
            scores = dot_nt(keys, queries[half])
            if mask is not None:
                scores = jnp.where(mask, scores, masked_score)
            top = jnp.max(scores, axis=0, keepdims=True)
            probs = jnp.exp(scores - top)
            total = jnp.sum(probs, axis=0, keepdims=True)
            mixed = dot_nn(values_t[half * HD : half * HD + HD], probs.astype(BF))
            out.append(mixed / total)
            lse_ref[0, 2 * pair + half : 2 * pair + half + 1, :] = top + jnp.log(total)
        heads_ref[0, :, lo : lo + 128] = jnp.concatenate(out, axis=0).astype(BF).T


def attend_back(packed_ref, heads_ref, heads_grad_ref, lse_ref, grad_ref, mask):
    width = heads_ref.shape[-1]
    for pair in range(width // 128):
        lo = pair * 128
        query = packed_ref[0, :, lo : lo + 128] * jnp.asarray(score_scale, BF)
        key = packed_ref[0, :, width + lo : width + lo + 128]
        value = packed_ref[0, :, 2 * width + lo : 2 * width + lo + 128]
        heads_grad = heads_grad_ref[0, :, lo : lo + 128]
        key_t = key.T
        mixed_t = (heads_grad.astype(F32) * heads_ref[0, :, lo : lo + 128].astype(F32)).T
        queries, head_grads = two_heads(query), two_heads(heads_grad)
        probs_two, score_two, query_grad = [], [], []
        for half in range(2):
            scores = dot_nt(key, queries[half])
            if mask is not None:
                scores = jnp.where(mask, scores, masked_score)
            probs = jnp.exp(scores - lse_ref[0, 2 * pair + half : 2 * pair + half + 1, :])
            delta = jnp.sum(mixed_t[half * HD : half * HD + HD], axis=0, keepdims=True)
            probs_grad = dot_nt(value, head_grads[half])
            score_grad = (probs * (probs_grad - delta)).astype(BF)
            probs_two.append(probs.astype(BF))
            score_two.append(score_grad)
            query_grad.append(dot_nn(key_t[half * HD : half * HD + HD], score_grad))
        value_grad = dot_nn(jnp.concatenate(probs_two, 1), jnp.concatenate(head_grads, 0))
        key_grad = dot_nn(jnp.concatenate(score_two, 1), jnp.concatenate(queries, 0))
        grad_ref[0, :, lo : lo + 128] = (
            (jnp.concatenate(query_grad, 0) * score_scale).astype(BF).T
        )
        grad_ref[0, :, width + lo : width + lo + 128] = key_grad.astype(BF)
        grad_ref[0, :, 2 * width + lo : 2 * width + lo + 128] = value_grad.astype(BF)


def gelu_both(pre):
    root = 0.7978845608028654
    square = pre * pre
    bend = jnp.tanh(root * pre * (1.0 + 0.044715 * square))
    half = 0.5 * (1.0 + bend)
    slope = half + 0.5 * pre * (1.0 - bend * bend) * (root * (1.0 + 3 * 0.044715 * square))
    return pre * half, slope


def start_layer(place, lots, refs, weights, sems):
    for i, (first, count, metas) in enumerate(lots):
        stacks, refs = refs[: len(metas)], refs[len(metas) :]
        start_weights(place, stacks, metas, weights.at[pl.ds(first, count)], sems.at[i])


def wait_layer(lots, weights, sems):
    for i, (first, count, _) in enumerate(lots):
        wait_all(weights.at[pl.ds(first, count)], sems.at[i])


def stacks_of(lots):
    return sum(len(metas) for _, _, metas in lots)


def project_in(values, gain, weights, normed_ref, packed_ref):
    xhat, _ = norm_parts(values)
    normed = (xhat * gain).astype(BF)
    normed_ref[0] = normed
    width = normed.shape[1]
    for b in range(3):
        packed_ref[0, :, b * width : (b + 1) * width] = dot_nn(normed, weights[b]).astype(BF)


def load_layer(place, lots, stacks, weights, sems):
    @pl.when(pl.program_id(0) == 0)
    def _():
        start_layer(place, lots, stacks, weights, sems)


def await_layer(lots, weights, sems):
    @pl.when(pl.program_id(0) == 0)
    def _():
        wait_layer(lots, weights, sems)


def spatial_in_body(lots, place, frames_ref, shift_ref, gain_ref, *refs):
    n = stacks_of(lots)
    stacks, (packed_ref, normed_ref, weights, sems) = refs[:n], refs[n:]
    load_layer(place, lots, stacks, weights, sems)
    await_layer(lots, weights, sems)
    values = frames_ref[0].astype(F32) + shift_ref[0]
    project_in(values, gain_ref[0:1, :], weights, normed_ref, packed_ref)


def temporal_fwd_body(place, *refs):
    piece_refs, gain_ref, stack = refs[:4], refs[4], refs[5]
    packed_ref, heads_ref, lse_ref, normed_ref, tokens_ref, resid_ref, third_ref = refs[6:13]
    weights, tokens, sems = refs[13:]
    load_whole(stack, weights, sems)
    frames, positions = piece_refs[0].shape[0], piece_refs[0].shape[1]
    for j, piece in enumerate(piece_refs):
        tokens[pl.ds((place[MEMBER] ^ j) * frames, frames)] = piece[...]
    low = tokens[...].reshape(tokens_ref.shape[1:])
    tokens_ref[0] = low
    values = low.astype(F32)
    await_whole(weights, sems)
    project_in(values, gain_ref[1:2, :], weights, normed_ref, packed_ref)
    attend(packed_ref, heads_ref, lse_ref, video_mask(low.shape[0], positions))
    resid = values + dot_nn(heads_ref[0], weights[3])
    resid_ref[0] = resid
    xhat, _ = norm_parts(resid)
    third_ref[0] = (xhat * gain_ref[2:3, :]).astype(BF)


def load_whole(stack, weights, sems):
    @pl.when(pl.program_id(0) == 0)
    def _():
        start_whole(stack, 0, weights, sems.at[0])


def await_whole(weights, sems):
    @pl.when(pl.program_id(0) == 0)
    def _():
        wait_all(weights, sems.at[0])


def attend_body(positions, place, packed_ref, heads_ref, lse_ref):
    mask = video_mask(packed_ref.shape[1], positions) if positions else None
    attend(packed_ref, heads_ref, lse_ref, mask)


def spatial_out_body(lots, place, heads_ref, frames_ref, shift_ref, *refs):
    n = stacks_of(lots)
    stacks, refs = refs[:n], refs[n:]
    piece_refs, (weights, resid, sems) = refs[:4], refs[4:]
    load_layer(place, lots, stacks, weights, sems)
    values = frames_ref[0].astype(F32) + shift_ref[0]
    await_layer(lots, weights, sems)
    resid[...] = (values + dot_nn(heads_ref[0], weights[lots[0][1] - 1])).astype(BF)
    count = piece_refs[0].shape[1]
    for j, piece in enumerate(piece_refs):
        first = pl.multiple_of((place[MEMBER] ^ j) * count, count)
        piece[0] = resid[pl.ds(first, count), :]


def ffn_body(group, base, last, kind, place, *refs):
    first = group == 0
    third_ref, cot_ref, resid_ref, stack = refs[:4]
    refs = refs[4:]
    if not first:
        dx_in, *refs = refs
    outs, refs = refs[:2], refs[2:]
    if last:
        dx_out, piece_refs, refs = refs[0], refs[1:5], refs[5:]
    else:
        resid_out, dx_out, refs = refs[0], refs[1], refs[2:]
    third, cot, third_t, cot_t, acc, dx, weights, act, pre_grad, staging, sems = refs
    tokens, width = third.shape
    blocks = weights.shape[0] // 2
    chunk = 256
    loads = [(third_ref, third, 0), (cot_ref, cot, 1), (resid_ref, acc, 2)]
    if not first:
        loads.append((dx_in, dx, 3))
    for source, target, s in loads[:2]:
        pltpu.make_async_copy(source, target, sems.at[s]).start()
    for b in range(blocks):
        start_whole(stack, base + 2 * b, weights.at[pl.ds(2 * b, 2)], sems.at[8 + b])
        if b == 0:
            for source, target, s in loads[2:]:
                pltpu.make_async_copy(source, target, sems.at[s]).start()
    for source, target, s in loads[:2]:
        pltpu.make_async_copy(source, target, sems.at[s]).wait()
    for source, target, s in loads[2:]:
        pltpu.make_async_copy(source, target, sems.at[s]).wait()

    def finish_sums():
        pltpu.make_async_copy(dx, dx_out, sems.at[6]).start()
        if not last:
            pltpu.make_async_copy(acc, resid_out, sems.at[7]).start()
            return
        low = third
        low[...] = acc[...].astype(BF)
        frames, positions = piece_refs[0].shape[:2]
        tiles = tokens // (FPV * 16)
        per_tile = positions // tiles
        for j, piece in enumerate(piece_refs):
            for tile in range(tiles):
                for f in range(frames):
                    row = pl.multiple_of(
                        tile * (tokens // tiles)
                        + ((place[MEMBER] ^ j) * frames + f) * per_tile,
                        per_tile,
                    )
                    pltpu.make_async_copy(
                        low.at[pl.ds(row, per_tile)],
                        piece.at[f, pl.ds(tile * per_tile, per_tile)],
                        sems.at[7],
                    ).start()

    def send(source, index):
        start_grads(place, kind, source, index, outs, sems.at[5])

    for b in range(blocks):
        w_up, w_down = weights.at[2 * b], weights.at[2 * b + 1]
        wait_all(weights.at[pl.ds(2 * b, 2)], sems.at[8 + b])
        for r in range(tokens // chunk):
            rows = slice(r * chunk, (r + 1) * chunk)
            pre = dot_nn(third[rows, :], w_up[...])
            act_grad = dot_nn(cot[rows, :], w_down[...])
            act_now, slope = gelu_both(pre)
            act_now = act_now.astype(BF)
            grad_now = (act_grad * slope).astype(BF)
            act[rows, :] = act_now
            pre_grad[rows, :] = grad_now
            if b == 0:
                third_t[:, rows] = third[rows, :].T
                cot_t[:, rows] = cot[rows, :].T
            acc[rows, :] += dot_nt(act_now, w_down[...])
            back = dot_nt(grad_now, w_up[...])
            if first and b == 0:
                dx[rows, :] = back
            else:
                dx[rows, :] += back
        if b == blocks - 1:
            finish_sums()
        staging[2 * b] = dot_nn(third_t[...], pre_grad[...]).astype(BF)
        send(staging.at[2 * b], 2 * b)
        staging[2 * b + 1] = dot_nn(cot_t[...], act[...]).astype(BF)
        send(staging.at[2 * b + 1], 2 * b + 1)
    if last:
        wait_all(third, sems.at[7])
    else:
        wait_all(acc, sems.at[7])
    wait_all(dx, sems.at[6])
    wait_all(staging, sems.at[5])


def add_gain(step, ref, row, value):
    @pl.when(step == 0)
    def _():
        ref[row : row + 1, :] = value

    @pl.when(step > 0)
    def _():
        ref[row : row + 1, :] += value


def temporal_bwd_body(
    place, dx_ref, cot_ref, resid_ref, tokens_ref, packed_ref, heads_ref, lse_ref, gain_ref, stack, *refs
):
    branch_ref, grad_ref, gains_out = refs[:3]
    piece_refs = refs[3:7]
    weights, heads_grad, total, sems = refs[7:]
    step = pl.program_id(0)
    load_whole(stack, weights, sems)
    back, gain_three = norm_back(resid_ref[0], dx_ref[0], gain_ref[2:3, :])
    add_gain(step, gains_out, 1, gain_three)
    grad_two = cot_ref[0].astype(F32) + back
    branch = grad_two.astype(BF)
    branch_ref[0] = branch
    await_whole(weights, sems)
    heads_grad[0] = dot_nt(branch, weights[3]).astype(BF)
    frames, positions = piece_refs[0].shape[0], piece_refs[0].shape[1]
    mask = video_mask(branch.shape[0], positions)
    attend_back(packed_ref, heads_ref, heads_grad, lse_ref, grad_ref, mask)
    normed_grad = project_back(grad_ref, weights)
    back, gain_two = norm_back(tokens_ref[0].astype(F32), normed_grad, gain_ref[1:2, :])
    add_gain(step, gains_out, 0, gain_two)
    total[...] = (grad_two + back).astype(BF).reshape(total.shape)
    for j, piece in enumerate(piece_refs):
        piece[...] = total[pl.ds((place[MEMBER] ^ j) * frames, frames)]


def spatial_branch_body(lots, place, *refs):
    n = stacks_of(lots)
    piece_refs, stacks = refs[:4], refs[4 : 4 + n]
    branch_ref, heads_grad_ref, weights, sems = refs[4 + n :]
    load_layer(place, lots, stacks, weights, sems)
    count = piece_refs[0].shape[1]
    for j, piece in enumerate(piece_refs):
        first = pl.multiple_of((place[MEMBER] ^ j) * count, count)
        branch_ref[0, pl.ds(first, count), :] = piece[0]
    await_layer(lots, weights, sems)
    heads_grad_ref[0] = dot_nt(branch_ref[0], weights[lots[0][1] - 1]).astype(BF)


def attend_back_body(positions, place, packed_ref, heads_ref, heads_grad_ref, lse_ref, grad_ref):
    mask = video_mask(packed_ref.shape[1], positions) if positions else None
    attend_back(packed_ref, heads_ref, heads_grad_ref, lse_ref, grad_ref, mask)


def project_back(grad_ref, weights):
    width = weights.shape[1]
    out = dot_nt(grad_ref[0, :, :width], weights[0])
    for b in range(1, 3):
        out = out + dot_nt(grad_ref[0, :, b * width : (b + 1) * width], weights[b])
    return out


def spatial_end_body(lots, place, grad_ref, frames_ref, shift_ref, branch_ref, gain_ref, *refs):
    n = stacks_of(lots)
    stacks, (input_ref, gain_out, column_out, weights, sems) = refs[:n], refs[n:]
    load_layer(place, lots, stacks, weights, sems)
    await_layer(lots, weights, sems)
    normed_grad = project_back(grad_ref, weights)
    values = frames_ref[0].astype(F32) + shift_ref[0]
    back, gain_one = norm_back(values, normed_grad, gain_ref[0:1, :])
    add_gain(pl.program_id(0), gain_out, 0, gain_one)
    grad_zero = branch_ref[0].astype(F32) + back
    input_ref[0] = grad_zero.astype(BF)
    column_out[0] = jnp.sum(grad_zero, axis=0, keepdims=True)


def weight_grad_body(kinds, lots, place, *refs):
    pairs = 1 + max(pair for lot in lots for pair, _ in lot)
    sides, refs = refs[: 2 * pairs], refs[2 * pairs :]
    outs, refs = refs[: 2 * len(lots)], refs[2 * len(lots) :]
    held, refs = refs[: 2 * pairs], refs[2 * pairs :]
    turned, (staging, sems) = refs[:pairs], refs[pairs:]
    for s, (source, target) in enumerate(zip(sides, held)):
        pltpu.make_async_copy(source, target, sems.at[s]).start()
    tokens, width = held[0].shape
    chunk = 256
    done = set()
    at = 0
    for i, lot in enumerate(lots):
        for index, (pair, block) in enumerate(lot):
            if pair not in done:
                done.add(pair)
                wait_all(held[2 * pair], sems.at[2 * pair])
                for r in range(tokens // chunk):
                    rows = slice(r * chunk, (r + 1) * chunk)
                    turned[pair][:, rows] = held[2 * pair][rows, :].T
                wait_all(held[2 * pair + 1], sems.at[2 * pair + 1])
            columns = slice(block * width, (block + 1) * width)
            staging[at] = dot_nn(turned[pair][...], held[2 * pair + 1][:, columns]).astype(BF)
            start_grads(place, kinds[i], staging.at[at], index, outs[2 * i : 2 * i + 2], sems.at[2 * pairs])
            at += 1
    wait_all(staging, sems.at[2 * pairs])


def update(weight, moment_one, moment_two, gradient, step_rate, decay_coef):
    first_new = beta_first * moment_one + (1.0 - beta_first) * gradient
    second_new = beta_second * moment_two + (1.0 - beta_second) * gradient * gradient
    fix_first = 1.0 - beta_first**STEP
    fix_second = 1.0 - beta_second**STEP
    change = first_new * (step_rate / fix_first) / (jnp.sqrt(second_new * (1.0 / fix_second)) + eps_adam)
    return weight - (change + (step_rate * decay_coef) * weight), first_new, second_new


def update_body(lots, place, clip, *refs):
    pieces, refs = refs[: 4 * len(lots)], refs[4 * len(lots) :]
    olds, news = refs[:6], refs[6:]
    array, matrix, block = pl.program_id(0), pl.program_id(1), pl.program_id(2)
    for i, lot in enumerate(lots):
        mine = functools.reduce(
            jnp.logical_or,
            [(array == a) & (matrix == m) & (block == b) for a, m, b in lot],
        )
        which = lot[0][0]

        @pl.when(mine)
        def _(i=i, which=which):
            master, first, second = olds[3 * which : 3 * which + 3]
            master_new, first_new, second_new = news[3 * which : 3 * which + 3]
            for rel, piece in enumerate(pieces[4 * i : 4 * i + 4]):
                width = piece.shape[2]
                column = (place[CORE] ^ (rel // 2)) * 2 + (place[XPOS] ^ (rel % 2))
                at = pl.ds(pl.multiple_of(column * width, 128), width)
                new = update(
                    master[0, :, at],
                    first[0, :, at],
                    second[0, :, at],
                    piece[0].astype(F32) * clip[0],
                    rate_matrix,
                    decay_rate,
                )
                master_new[0, :, at], first_new[0, :, at], second_new[0, :, at] = new


def join_body(place, *refs):
    pieces, out_ref = refs[:4], refs[4]
    count = pieces[0].shape[1]
    for j, piece in enumerate(pieces):
        first = pl.multiple_of((place[MEMBER] ^ j) * count, count)
        out_ref[0, pl.ds(first, count), :] = piece[0]


def tile_body(place, *refs):
    pieces, out_ref, tokens = refs[:4], refs[4], refs[5]
    frames = pieces[0].shape[0]
    for j, piece in enumerate(pieces):
        tokens[pl.ds((place[MEMBER] ^ j) * frames, frames)] = piece[...]
    out_ref[0] = tokens[...].reshape(out_ref.shape[1:])


def call(body, place, args, in_specs, out_specs, out_shape, scratch, grid=(1,), limit=60, us=10, scalars=1, aliases={}):
    return pl.pallas_call(
        body,
        out_shape=out_shape,
        grid_spec=pltpu.PrefetchScalarGridSpec(
            num_scalar_prefetch=scalars,
            grid=grid,
            in_specs=in_specs,
            out_specs=out_specs,
            scratch_shapes=scratch,
        ),
        input_output_aliases=aliases,
        compiler_params=pltpu.CompilerParams(vmem_limit_bytes=limit * MIB),
        cost_estimate=pl.CostEstimate(flops=us * 10**9, bytes_accessed=MIB, transcendentals=0),
    )(*place, *args)


def tile(*shape):
    return pl.BlockSpec((1,) + shape, lambda i, *_: (i,) + (0,) * len(shape))


def fixed(*shape):
    return pl.BlockSpec(shape, lambda i, *_: (0,) * len(shape))


def shape_of(*shape, dtype=BF):
    return jax.ShapeDtypeStruct(shape, dtype)


def shards(
    frames_in,
    action_codes,
    cotangent,
    attn_master,
    attn_first,
    attn_second,
    ffn_master,
    ffn_first,
    ffn_second,
    small_master,
    small_first,
    small_second,
):
    frames, positions, width = frames_in.shape
    heads_n = width // HD
    members = FPV // frames
    part = positions // members
    spot = positions // FPV
    tiles = part // spot
    rows_tile = FPV * spot
    tokens = tiles * rows_tile
    seq_size = lax.axis_size("seq")
    nz = seq_size // 2
    seq, grp = lax.axis_index("seq"), lax.axis_index("grp")
    place = jnp.stack([grp % 2, grp // 2, seq % 2, seq // 2, seq % members]).astype(jnp.int32)
    spots = (place,)
    local_rows = attn_master.shape[1]

    def blocks(master, picks):
        return jnp.stack([master[m, :, b * width : (b + 1) * width] for m, b in picks]).astype(BF)

    small_low = small_master.astype(BF)
    if seq_size & (seq_size - 1) == 0:
        small_all = small_low[None]
        bit = 1
        while bit < seq_size:
            small_all = jnp.concatenate([small_all, swap(small_all, "seq", bit)])
            bit *= 2
        small_all = jnp.take(small_all, jnp.arange(seq_size) ^ seq, axis=0)
    else:
        small_all = lax.all_gather(small_low, "seq")
    small_w = small_all.transpose(1, 0, 2).reshape(small_low.shape[0], width)

    qk_s, meta_qk_s = gather_weights(blocks(attn_master, [(0, 0), (0, 1)]), "zyx", place)
    v_s, meta_v_s = gather_weights(
        blocks(attn_master, [(0, 2)]), "zy", place, begin=(qk_s[0],)
    )
    below_o, beside_o = start_gather(
        blocks(attn_master, [(0, 3)]), "zy", place, begin=(v_s[0],)
    )
    lots_in_s, in_s = ((0, 2, meta_qk_s), (2, 1, meta_v_s)), [*qk_s, *v_s]

    ffn_picks = [(m, 2 * group + b) for group in range(2) for b in range(2) for m in range(2)]
    early = jnp.concatenate(
        [
            quarter_mine(blocks(attn_master, [(1, b) for b in range(4)]), place),
            quarter_mine(blocks(ffn_master, ffn_picks[:4]), place),
        ]
    )
    late = quarter_mine(blocks(ffn_master, ffn_picks[4:]), place)
    early_all = lax.all_gather(early, ("seq", "grp"))
    gains = small_w[:3].astype(F32)
    onehot = (action_codes[:, None] == jnp.arange(CODES)[None, :]).astype(BF)
    code_shift = jnp.dot(onehot, small_w[3:], preferred_element_type=F32)[:, None, :]

    piece_spec = pl.BlockSpec((frames, spot, width), lambda i, *_: (0, i, 0))
    part_spec = pl.BlockSpec((1, part, width), lambda i, *_: (i, 0, 0))
    sems = pltpu.SemaphoreType.DMA

    def held(count):
        return [pltpu.VMEM((count, width, width), BF)]

    def layer(body, lots, stacks, args, in_specs, out_specs, out_shape, scratch, us):
        return call(
            functools.partial(body, lots),
            spots,
            [*args, *stacks],
            in_specs + [ANY] * len(stacks),
            out_specs,
            out_shape,
            held(sum(count for _, count, _ in lots)) + scratch + [sems((len(lots),))],
            grid=(frames,),
            limit=60,
            us=us,
        )

    wide, flat_tile = tile(positions, 3 * width), tile(positions, width)
    wide_shape = shape_of(frames, positions, 3 * width)
    tile_shape = shape_of(frames, positions, width)
    tile32_shape = shape_of(frames, positions, width, dtype=F32)
    lse_spec, lse_shape = tile(heads_n, positions), shape_of(frames, heads_n, positions, dtype=F32)
    piece_shapes = [shape_of(frames, part, width)] * members
    gain_shape = shape_of(1, width, dtype=F32)

    def attention(packed, step):
        return call(
            functools.partial(attend_body, step),
            spots,
            [packed],
            [wide],
            [flat_tile, lse_spec],
            [tile_shape, lse_shape],
            [],
            grid=(frames,),
            limit=60,
            us=22,
        )

    def attention_back(packed, heads, heads_grad, lse, step):
        return call(
            functools.partial(attend_back_body, step),
            spots,
            [packed, heads, heads_grad, lse],
            [wide, flat_tile, flat_tile, lse_spec],
            wide,
            wide_shape,
            [],
            grid=(frames,),
            limit=60,
            us=26,
        )

    packed_s, normed_s = layer(
        spatial_in_body,
        lots_in_s,
        in_s,
        [before(frames_in, below_o), code_shift, gains],
        [flat_tile, tile(1, width), fixed(3, width)],
        [wide, flat_tile],
        [wide_shape, tile_shape],
        [],
        12,
    )
    heads_s, lse_s = attention(packed_s, 0)
    out_s, meta_out_s = finish_gather(
        below_o, beside_o, "zy", cross=(heads_s,)
    )
    lots_out_s = ((0, 1, meta_out_s),)
    pieces = layer(
        spatial_out_body,
        lots_out_s,
        out_s,
        [heads_s, frames_in, code_shift],
        [flat_tile, flat_tile, tile(1, width)],
        [part_spec] * members,
        piece_shapes,
        [pltpu.VMEM((positions, width), BF)],
        6,
    )
    token_pieces = exchange(pieces)
    late_all = lax.all_gather(before(late, token_pieces), ("seq", "grp"))

    packed_t, heads_t, lse_t, normed_t, tokens_t, resid_two, third = call(
        temporal_fwd_body,
        spots,
        [*token_pieces, gains, early_all],
        [piece_spec] * members + [fixed(3, width), ANY],
        [wide, flat_tile, lse_spec] + [flat_tile] * 4,
        [wide_shape, tile_shape, lse_shape, tile_shape, tile_shape, tile32_shape, tile_shape],
        held(4) + [pltpu.VMEM((FPV, spot, width), BF), sems((1,))],
        grid=(tiles,),
        us=37,
    )

    def position_part(array, j):
        return lax.dynamic_slice_in_dim(array, (place[MEMBER] ^ j) * part, part, 1)

    cot_pieces = exchange(
        [after(position_part(cotangent, j), *token_pieces) for j in range(members)]
    )
    cot_tiles = call(
        tile_body,
        spots,
        [before(cot_pieces[0], third), *cot_pieces[1:]],
        [piece_spec] * members,
        tile(rows_tile, width),
        shape_of(tiles, rows_tile, width),
        [pltpu.VMEM((FPV, spot, width), BF)],
        grid=(tiles,),
    )

    def split_shape(kind, n):
        lead = (2, 2, nz) if kind == "xyz" else (2, nz, 2)
        return shape_of(*lead, n, local_rows, width // 4)

    flat = lambda array: array.reshape(tokens, width)
    resid_now = flat(resid_two)
    full32 = shape_of(tokens, width, dtype=F32)
    parts_f = []
    groups = 2
    for group in range(groups):
        last = group == groups - 1
        ends = [full32] + [shape_of(frames, part, width)] * members if last else [full32, full32]
        args = [flat(third), flat(cot_tiles), resid_now, late_all if group else early_all]
        if group:
            args += [dx]
        outs = call(
            functools.partial(ffn_body, group, 0 if group else 4, last, "xyz"),
            spots,
            args,
            [ANY] * len(args),
            [ANY] * (2 + len(ends)),
            [split_shape("xyz", 4)] * 2 + ends,
            [pltpu.VMEM((tokens, width), BF)] * 2
            + [pltpu.VMEM((width, tokens), BF)] * 2
            + [pltpu.VMEM((tokens, width), F32)] * 2
            + [pltpu.VMEM((4, width, width), BF)]
            + [pltpu.VMEM((tokens, width), BF)] * 2
            + [pltpu.VMEM((4, width, width), BF), sems((10,))],
            us=41,
        )
        parts_f.append(outs[:2])
        if last:
            dx, block_pieces = outs[2], outs[3:]
        else:
            resid_now, dx = outs[2:]
            sum_e = send_core(outs[:2])

    quarters = {}
    sum_f = send_core(parts_f[1])
    sum_e, sent_e = step_one(sum_e, dx)
    dx = before(dx, sent_e)
    sum_e = send_one(sum_e, sent_e, "xyz")
    outs = call(
        temporal_bwd_body,
        spots,
        [dx.reshape(resid_two.shape), cot_tiles, resid_two, tokens_t, packed_t, heads_t, lse_t, gains, early_all],
        [flat_tile] * 4 + [wide, flat_tile, lse_spec, fixed(3, width), ANY],
        [flat_tile, wide, fixed(2, width)] + [piece_spec] * members,
        [tile_shape, wide_shape, shape_of(2, width, dtype=F32)] + piece_shapes,
        held(4)
        + [
            pltpu.VMEM((1, positions, width), BF),
            pltpu.VMEM((FPV, spot, width), BF),
            sems((1,)),
        ],
        grid=(tiles,),
        us=38,
    )
    branch_t, grad_t, gains_two = outs[:3]
    grad_pieces = exchange(outs[3:])
    block_pieces = exchange(block_pieces)
    join = functools.partial(
        call,
        body=join_body,
        place=spots,
        in_specs=[part_spec] * members,
        out_specs=tile(positions, width),
        out_shape=shape_of(frames, positions, width),
        scratch=[],
        grid=(frames,),
    )
    block_out = join(args=[before(block_pieces[0], grad_t), *block_pieces[1:]])


    def weight_grads(kinds, sides, *lots):
        sides = [side.reshape(tokens, -1) for side in sides]
        outs = call(
            functools.partial(weight_grad_body, kinds, lots),
            spots,
            sides,
            [ANY] * len(sides),
            [ANY] * (2 * len(lots)),
            [split_shape(kind, len(lot)) for kind, lot in zip(kinds, lots) for _ in range(2)],
            [pltpu.VMEM(side.shape, BF) for side in sides]
            + [pltpu.VMEM((width, tokens), BF)] * (len(sides) // 2)
            + [pltpu.VMEM((sum(map(len, lots)), width, width), BF), sems((len(sides) + 1,))],
            us=15,
        )
        return [outs[2 * i : 2 * i + 2] for i in range(len(lots))]

    sum_e, sent_e = step_two(sum_e, "xyz", grad_t)
    sum_f, sent_f = step_one(sum_f, grad_t)
    (parts_t,) = weight_grads(
        ("xyz",),
        [normed_t, before(grad_t, sent_e, sent_f, block_out), heads_t, branch_t],
        [(0, 0), (0, 1), (0, 2), (1, 0)],
    )
    sum_f = send_one(sum_f, sent_f, "xyz")
    sum_t, sent_t = step_one(send_core(parts_t))

    branch_s, heads_grad_s = layer(
        spatial_branch_body,
        lots_out_s,
        out_s,
        [before(grad_pieces[0], sent_t), *grad_pieces[1:]],
        [part_spec] * members,
        [flat_tile] * 2,
        [tile_shape] * 2,
        [],
        7,
    )
    sum_t = send_one(sum_t, sent_t, "xyz")
    sum_f, sent_f = step_two(sum_f, "xyz", branch_s)
    grad_s = attention_back(packed_s, heads_s, before(heads_grad_s, sent_f), lse_s, 0)
    sum_e = send_two(sum_e, after(sent_e, branch_s), "xyz")
    sum_f = send_two(sum_f, sent_f, "xyz")
    sum_e, sent_e = step_three(sum_e, "xyz", grad_s)
    (parts_qk,) = weight_grads(
        ("xyz",), [normed_s, before(grad_s, sent_e)], [(0, 0), (0, 1)]
    )
    sum_e = send_three(sum_e, sent_e, "xyz")
    sum_qk = send_core(parts_qk)
    sum_f, sent_f = step_three(sum_f, "xyz", parts_qk[0])
    sum_t, sent_t = step_two(sum_t, "xyz", parts_qk[0])
    (parts_vo,) = weight_grads(
        ("xyz",), [normed_s, before(grad_s, sent_f, sent_t), heads_s, branch_s], [(0, 2), (1, 0)]
    )
    sum_f, sum_t = send_three(sum_f, sent_f, "xyz"), send_two(sum_t, sent_t, "xyz")
    quarters["ffn0"] = finish(sum_e, parts_vo[0])
    sum_vo = send_core(parts_vo)
    sum_qk, sent_qk = step_one(sum_qk, parts_vo[0])
    sum_vo, sent_vo = step_one(sum_vo, sent_qk)
    input_grad, gain_one, columns = layer(
        spatial_end_body,
        lots_in_s,
        in_s,
        [grad_s, frames_in, code_shift, before(branch_s, sent_qk, sent_vo, quarters["ffn0"]), gains],
        [wide, flat_tile, tile(1, width), flat_tile, fixed(3, width)],
        [flat_tile, fixed(1, width), tile(1, width)],
        [tile_shape, gain_shape, shape_of(frames, 1, width, dtype=F32)],
        [],
        14,
    )
    sum_qk = send_one(sum_qk, sent_qk, "xyz")
    sum_qk, sent_qk = step_two(sum_qk, "xyz", columns)
    sum_qk = send_two(sum_qk, sent_qk, "xyz")
    quarters["ffn1"] = finish(sum_f, columns)
    sum_t, sent_t = step_three(sum_t, "xyz", columns)
    sum_t = send_three(sum_t, sent_t, "xyz")
    sum_vo = send_one(sum_vo, sent_vo, "xyz")
    sum_vo, sent_vo = step_two(sum_vo, "xyz", sent_qk, sent_t)
    sum_vo = send_two(sum_vo, sent_vo, "xyz")
    sum_qk, sent_qk = step_three(sum_qk, "xyz", sent_vo)
    sum_qk = send_three(sum_qk, sent_qk, "xyz")
    shared = {
        name: share_quarters(before(quarters[name], sent_qk)) for name in ("ffn0", "ffn1")
    }
    quarters["t"] = finish(sum_t, sent_qk)
    sum_vo, sent_vo = step_three(sum_vo, "xyz", quarters["t"])
    sum_vo = send_three(sum_vo, sent_vo, "xyz")
    quarters["qk"] = finish(sum_qk, sent_vo)
    shared["t"] = share_quarters(before(quarters["t"], sent_vo))
    quarters["vo"] = finish(sum_vo, shared["ffn0"], shared["ffn1"])

    table_grad = jnp.dot(
        onehot.astype(F32).T, columns[:, 0, :], precision=lax.Precision.HIGHEST
    )
    squares = sum(jnp.sum(jnp.square(q.astype(F32))) for q in quarters.values())
    sums = all_sum(
        jnp.concatenate(
            [gain_one, gains_two, table_grad, jnp.broadcast_to(squares, (1, width))], axis=0
        )
    )
    small_grad = sums[:-1]

    total_squares = sums[-1, 0] + jnp.sum(small_grad * small_grad)
    grad_norm = jnp.sqrt(total_squares)
    clip_factor = 1.0 / jnp.maximum(grad_norm, 1.0)
    for name in ("qk", "vo"):
        shared[name] = share_quarters(quarters[name])

    lots = [
        ("qk", [(0, 0, 0), (0, 0, 1)]),
        ("vo", [(0, 0, 2), (0, 0, 3)]),
        ("t", [(0, 1, b) for b in range(4)]),
        ("ffn0", [(1, *pick) for pick in ffn_picks[:4]]),
        ("ffn1", [(1, *pick) for pick in ffn_picks[4:]]),
    ]

    def piece_spec_of(lot):
        def at(a, m, b, *_):
            entry = 0
            for k, (array, matrix, block) in enumerate(lot):
                entry = jnp.where((a == array) & (m == matrix) & (b == block), k, entry)
            return entry, 0, 0

        return pl.BlockSpec((1, local_rows, width // 4), at)

    columns_n = attn_master.shape[2] // width
    attn_block = pl.BlockSpec(
        (1, local_rows, width),
        lambda a, m, b, *_: (jnp.where(a == 0, m, 1), 0, jnp.where(a == 0, b, columns_n - 1)),
    )
    ffn_block = pl.BlockSpec(
        (1, local_rows, width), lambda a, m, b, *_: (jnp.where(a == 1, m, 0), 0, jnp.where(a == 1, b, 0))
    )
    blocks_six = [attn_block] * 3 + [ffn_block] * 3
    updated = call(
        functools.partial(update_body, [lot for _, lot in lots]),
        (place, clip_factor.reshape(1)),
        [p for name, _ in lots for p in shared[name]]
        + [attn_master, attn_first, attn_second, ffn_master, ffn_first, ffn_second],
        [piece_spec_of(lot) for _, lot in lots for _ in range(4)] + blocks_six,
        blocks_six,
        [shape_of(*attn_master.shape, dtype=F32)] * 3 + [shape_of(*ffn_master.shape, dtype=F32)] * 3,
        [],
        grid=(2, 2, columns_n),
        scalars=2,
    )
    small_decay = jnp.where(jnp.arange(3 + CODES)[:, None] >= 3, decay_rate, 0.0)
    small_cols = small_master.shape[1]
    small_mine = lax.dynamic_slice_in_dim(small_grad, seq * small_cols, small_cols, 1)
    small_new = update(
        small_master, small_first, small_second, small_mine * clip_factor, rate_small, small_decay
    )
    return (block_out, input_grad, grad_norm, *updated, *small_new)


def solution(mesh):
    token = P(("grp", "seq"), None, None)
    matrix = P(None, "seq", None)
    small = P(None, "seq")
    return jax.shard_map(
        shards,
        mesh=mesh,
        in_specs=(token, P(("grp", "seq")), token) + (matrix,) * 6 + (small,) * 3,
        out_specs=(token, token, P()) + (matrix,) * 6 + (small,) * 3,
        check_vma=False,
    )
```

```python
import functools

import jax
import jax.numpy as jnp
from jax import lax
from jax.experimental import pallas as pl
from jax.experimental.pallas import tpu as pltpu
from jax.sharding import PartitionSpec as P

HD = 64
FPV = 16
CODES = 8
STEP = 5
BF = jnp.bfloat16
F32 = jnp.float32

eps_norm = 1e-05
beta_first = 0.5
beta_second = 0.5
rate_matrix = 0.02
rate_small = 0.3
decay_rate = 0.1
eps_adam = 1e-08
masked_score = -1000000000.0
score_scale = HD**-0.5

CORE, XPOS, YPOS, ZPOS, MEMBER = range(5)
ANY = pl.BlockSpec(memory_space=pl.ANY)
MIB = 1 << 20


def dot_nn(a, b):
    return lax.dot_general(a, b, (((1,), (0,)), ((), ())), preferred_element_type=F32)


def dot_nt(a, b):
    return lax.dot_general(a, b, (((1,), (1,)), ((), ())), preferred_element_type=F32)


def after(value, *others):
    return lax.optimization_barrier((value, *others))[0] if others else value


def swap(value, axis, bit):
    size = lax.axis_size(axis)
    return lax.ppermute(value, axis, [(i, i ^ bit) for i in range(size)])


def shift_z(value, step):
    size = lax.axis_size("seq")
    return lax.ppermute(value, "seq", [(i, (i + 2 * step) % size) for i in range(size)])


def z_groups():
    size = lax.axis_size("seq")
    return [list(range(first, size, 2)) for first in range(2)]


def gather_z(piece, *others):
    nz = lax.axis_size("seq") // 2
    if nz <= 4:
        return jnp.stack([piece] + [after(shift_z(piece, k), *others) for k in range(1, nz)])
    whole = lax.all_gather(piece, "seq", axis_index_groups=z_groups())
    here = lax.axis_index("seq") // 2
    return jnp.take(whole, (here - jnp.arange(nz)) % nz, axis=0)


def column_part(block, start, width):
    return lax.dynamic_slice_in_dim(block, start, width, 2)


def quarter_mine(block, place):
    part = block.shape[2] // 4
    return column_part(block, (place[CORE] * 2 + place[XPOS]) * part, part)


def start_gather(block, kind, place, begin=(), then=()):
    width = block.shape[2]
    if kind == "zyx":
        part = width // 4
        piece = column_part(block, (place[CORE] * 2 + place[XPOS]) * part, part)
    else:
        part = width // 2
        piece = column_part(block, place[CORE] * part, part)
    below = gather_z(after(piece, *begin), *then)
    return below, swap(below, "seq", 1)


def finish_gather(below, beside, kind, across_after=(), cross=()):
    stacks = [(below, 0, 0), (beside, 1, 0)]
    if kind == "zyx":
        stacks += [(swap(after(s, *across_after), "grp", 2), y, 1) for s, y, _ in stacks]
    out = [(s, (y, 0, x)) for s, y, x in stacks]
    out += [(swap(after(s, *cross), "grp", 1), (y, 1, x)) for s, y, x in stacks]
    return [s for s, _ in out], [m if kind == "zyx" else (m[0], m[1], None) for _, m in out]


def gather_weights(block, kind, place, begin=()):
    return finish_gather(*start_gather(block, kind, place, begin), kind)


def add_low(*terms):
    return sum(term.astype(F32) for term in terms).astype(BF)


def send_core(parts):
    return [parts[0], swap(parts[1], "grp", 1)]


def step_one(terms, *others):
    terms = [terms[0], before(terms[1], others)]
    return [term[0] for term in terms], add_low(*[term[1] for term in terms])


def send_one(terms, sent, kind):
    return terms + [swap(sent, "grp", 2) if kind == "xyz" else swap(sent, "seq", 1)]


def step_two(terms, kind, *others):
    terms = terms[:-1] + [before(terms[-1], others)]
    if kind == "xyz":
        return [term[0] for term in terms], add_low(*[term[1] for term in terms])
    return step_z(terms)


def step_z(terms):
    nz = terms[0].shape[0]
    return [term[0] for term in terms], [add_low(*[term[k] for term in terms]) for k in range(1, nz)]


def send_z(terms, sent):
    nz = lax.axis_size("seq") // 2
    if nz <= 4:
        return terms + [shift_z(part, k + 1) for k, part in enumerate(sent)]
    here = lax.axis_index("seq") // 2
    parts = jnp.stack([add_low(*terms), *sent])
    ordered = jnp.take(parts, (jnp.arange(nz) - here) % nz, axis=0)
    return [lax.psum_scatter(ordered, "seq", axis_index_groups=z_groups())]


def send_two(terms, sent, kind):
    return terms + [swap(sent, "seq", 1)] if kind == "xyz" else send_z(terms, sent)


def step_three(terms, kind, *others):
    terms = terms[:-1] + [before(terms[-1], others)]
    if kind == "xyz":
        return step_z(terms)
    return [term[0] for term in terms], add_low(*[term[1] for term in terms])


def send_three(terms, sent, kind):
    return send_z(terms, sent) if kind == "xyz" else terms + [swap(sent, "grp", 2)]


def finish(terms, *others):
    return add_low(*terms[:-1], before(terms[-1], others))


def before(value, *states):
    return after(value, *jax.tree.leaves(states))


def share_quarters(quarter):
    beside = swap(quarter, "grp", 2)
    return [quarter, beside, swap(quarter, "grp", 1), swap(beside, "grp", 1)]


def all_sum(value):
    for axis in ("grp", "seq"):
        size = lax.axis_size(axis)
        if size & (size - 1):
            value = lax.psum(value, axis)
            continue
        bit = 1
        while bit < size:
            if 4 * bit <= size:
                a, b, c = (swap(value, axis, bit * k) for k in (1, 2, 3))
                low = (lax.axis_index(axis) // (2 * bit)) % 2 == 0
                near, far = value + a, b + c
                value = jnp.where(low, near, far) + jnp.where(low, far, near)
                bit *= 4
            else:
                value = value + swap(value, axis, bit)
                bit *= 2
    return value


def exchange(pieces):
    return [pieces[0]] + [swap(pieces[j], "seq", j) for j in range(1, len(pieces))]


def start_weights(place, stacks, metas, target, sem):
    for stack, (y_rel, c_rel, x_rel) in zip(stacks, metas):
        nz, _, rows, width = stack.shape
        column = place[CORE] ^ c_rel
        if x_rel is not None:
            column = column * 2 + (place[XPOS] ^ x_rel)
        column = pl.multiple_of(column * width, 128)

        def one(k, carry, stack=stack, y_rel=y_rel, rows=rows, width=width, column=column, nz=nz):
            shard = lax.rem(place[ZPOS] - k + nz, nz) * 2 + (place[YPOS] ^ y_rel)
            row = pl.multiple_of(shard * rows, rows)
            pltpu.make_async_copy(
                stack.at[k], target.at[:, pl.ds(row, rows), pl.ds(column, width)], sem
            ).start()
            return carry

        if nz <= 4:
            for k in range(nz):
                one(k, 0)
        else:
            lax.fori_loop(0, nz, one, 0)


def quarter_column(g, width):
    return (g % 2 * 2 + g // 2) * width


def start_whole(stack, first, target, sem):
    count, _, rows, width = stack.shape
    n = target.shape[0]

    def one(s, carry):
        row = s * rows if isinstance(s, int) else pl.multiple_of(s * rows, rows)
        for g in range(4):
            pltpu.make_async_copy(
                stack.at[s * 4 + g, pl.ds(first, n)],
                target.at[:, pl.ds(row, rows), pl.ds(quarter_column(g, width), width)],
                sem,
            ).start()
        return carry

    if count <= 32:
        for s in range(count // 4):
            one(s, 0)
    else:
        lax.fori_loop(0, count // 4, one, 0)


def wait_all(target, sem):
    pltpu.make_async_copy(target, target, sem).wait()


def start_grads(place, kind, source, index, outs, sem):
    nz = outs[0].shape[2 if kind == "xyz" else 1]
    rows, width = outs[0].shape[-2:]
    for rel in range(4):
        out, x_rel = outs[rel // 2], rel % 2
        column = (place[CORE] ^ (rel // 2)) * 2 + (place[XPOS] ^ x_rel)
        column = pl.multiple_of(column * width, 128)
        for y_rel in range(2):

            def one(k, carry, out=out, x_rel=x_rel, y_rel=y_rel, column=column):
                shard = lax.rem(place[ZPOS] + k, nz) * 2 + (place[YPOS] ^ y_rel)
                row = pl.multiple_of(shard * rows, rows)
                target = out.at[x_rel, y_rel, k, index]
                if kind != "xyz":
                    target = out.at[y_rel, k, x_rel, index]
                pltpu.make_async_copy(
                    source.at[pl.ds(row, rows), pl.ds(column, width)], target, sem
                ).start()
                return carry

            if nz <= 4:
                for k in range(nz):
                    one(k, 0)
            else:
                lax.fori_loop(0, nz, one, 0)


def norm_parts(values):
    centre = values - jnp.mean(values, axis=-1, keepdims=True)
    spread = jnp.mean(centre * centre, axis=-1, keepdims=True)
    scale = lax.rsqrt(spread + eps_norm)
    return centre * scale, scale


def norm_back(values, h_grad, gain):
    xhat, scale = norm_parts(values)
    e = h_grad * gain
    inner = jnp.mean(e * xhat, axis=-1, keepdims=True)
    v_grad = scale * (e - jnp.mean(e, axis=-1, keepdims=True) - xhat * inner)
    return v_grad, jnp.sum(h_grad * xhat, axis=0, keepdims=True)


def two_heads(x):
    lane = lax.broadcasted_iota(jnp.int32, x.shape, 1)
    zero = jnp.zeros_like(x)
    return jnp.where(lane < HD, x, zero), jnp.where(lane < HD, zero, x)


def video_mask(rows, positions):
    key = lax.broadcasted_iota(jnp.int32, (rows, rows), 0)
    query = lax.broadcasted_iota(jnp.int32, (rows, rows), 1)
    return (lax.rem(key, positions) == lax.rem(query, positions)) & (key <= query)


def attend(packed_ref, heads_ref, lse_ref, mask):
    width = heads_ref.shape[-1]
    for pair in range(width // 128):
        lo = pair * 128
        queries = two_heads(packed_ref[0, :, lo : lo + 128] * jnp.asarray(score_scale, BF))
        keys = packed_ref[0, :, width + lo : width + lo + 128]
        values_t = packed_ref[0, :, 2 * width + lo : 2 * width + lo + 128].T
        out = []
        for half in range(2):
            scores = dot_nt(keys, queries[half])
            if mask is not None:
                scores = jnp.where(mask, scores, masked_score)
            top = jnp.max(scores, axis=0, keepdims=True)
            probs = jnp.exp(scores - top)
            total = jnp.sum(probs, axis=0, keepdims=True)
            mixed = dot_nn(values_t[half * HD : half * HD + HD], probs.astype(BF))
            out.append(mixed / total)
            lse_ref[0, 2 * pair + half : 2 * pair + half + 1, :] = top + jnp.log(total)
        heads_ref[0, :, lo : lo + 128] = jnp.concatenate(out, axis=0).astype(BF).T


def attend_back(packed_ref, heads_ref, heads_grad_ref, lse_ref, grad_ref, mask):
    width = heads_ref.shape[-1]
    for pair in range(width // 128):
        lo = pair * 128
        query = packed_ref[0, :, lo : lo + 128] * jnp.asarray(score_scale, BF)
        key = packed_ref[0, :, width + lo : width + lo + 128]
        value = packed_ref[0, :, 2 * width + lo : 2 * width + lo + 128]
        heads_grad = heads_grad_ref[0, :, lo : lo + 128]
        key_t = key.T
        mixed_t = (heads_grad.astype(F32) * heads_ref[0, :, lo : lo + 128].astype(F32)).T
        queries, head_grads = two_heads(query), two_heads(heads_grad)
        probs_two, score_two, query_grad = [], [], []
        for half in range(2):
            scores = dot_nt(key, queries[half])
            if mask is not None:
                scores = jnp.where(mask, scores, masked_score)
            probs = jnp.exp(scores - lse_ref[0, 2 * pair + half : 2 * pair + half + 1, :])
            delta = jnp.sum(mixed_t[half * HD : half * HD + HD], axis=0, keepdims=True)
            probs_grad = dot_nt(value, head_grads[half])
            score_grad = (probs * (probs_grad - delta)).astype(BF)
            probs_two.append(probs.astype(BF))
            score_two.append(score_grad)
            query_grad.append(dot_nn(key_t[half * HD : half * HD + HD], score_grad))
        value_grad = dot_nn(jnp.concatenate(probs_two, 1), jnp.concatenate(head_grads, 0))
        key_grad = dot_nn(jnp.concatenate(score_two, 1), jnp.concatenate(queries, 0))
        grad_ref[0, :, lo : lo + 128] = (
            (jnp.concatenate(query_grad, 0) * score_scale).astype(BF).T
        )
        grad_ref[0, :, width + lo : width + lo + 128] = key_grad.astype(BF)
        grad_ref[0, :, 2 * width + lo : 2 * width + lo + 128] = value_grad.astype(BF)


def gelu_both(pre):
    root = 0.7978845608028654
    square = pre * pre
    bend = jnp.tanh(root * pre * (1.0 + 0.044715 * square))
    half = 0.5 * (1.0 + bend)
    slope = half + 0.5 * pre * (1.0 - bend * bend) * (root * (1.0 + 3 * 0.044715 * square))
    return pre * half, slope


def start_layer(place, lots, refs, weights, sems):
    for i, (first, count, metas) in enumerate(lots):
        stacks, refs = refs[: len(metas)], refs[len(metas) :]
        start_weights(place, stacks, metas, weights.at[pl.ds(first, count)], sems.at[i])


def wait_layer(lots, weights, sems):
    for i, (first, count, _) in enumerate(lots):
        wait_all(weights.at[pl.ds(first, count)], sems.at[i])


def stacks_of(lots):
    return sum(len(metas) for _, _, metas in lots)


def project_in(values, gain, weights, normed_ref, packed_ref):
    xhat, _ = norm_parts(values)
    normed = (xhat * gain).astype(BF)
    normed_ref[0] = normed
    width = normed.shape[1]
    for b in range(3):
        packed_ref[0, :, b * width : (b + 1) * width] = dot_nn(normed, weights[b]).astype(BF)


def load_layer(place, lots, stacks, weights, sems):
    @pl.when(pl.program_id(0) == 0)
    def _():
        start_layer(place, lots, stacks, weights, sems)


def await_layer(lots, weights, sems):
    @pl.when(pl.program_id(0) == 0)
    def _():
        wait_layer(lots, weights, sems)


def spatial_in_body(lots, place, frames_ref, shift_ref, gain_ref, *refs):
    n = stacks_of(lots)
    stacks, (packed_ref, normed_ref, weights, sems) = refs[:n], refs[n:]
    load_layer(place, lots, stacks, weights, sems)
    await_layer(lots, weights, sems)
    values = frames_ref[0].astype(F32) + shift_ref[0]
    project_in(values, gain_ref[0:1, :], weights, normed_ref, packed_ref)


def temporal_fwd_body(place, *refs):
    piece_refs, gain_ref, stack = refs[:4], refs[4], refs[5]
    packed_ref, heads_ref, lse_ref, normed_ref, tokens_ref, resid_ref, third_ref = refs[6:13]
    weights, tokens, sems = refs[13:]
    load_whole(stack, weights, sems, (QKV, OUT))
    frames, positions = piece_refs[0].shape[0], piece_refs[0].shape[1]
    for j, piece in enumerate(piece_refs):
        tokens[pl.ds((place[MEMBER] ^ j) * frames, frames)] = piece[...]
    low = tokens[...].reshape(tokens_ref.shape[1:])
    tokens_ref[0] = low
    values = low.astype(F32)
    await_whole(weights, sems, *QKV)
    project_in(values, gain_ref[1:2, :], weights, normed_ref, packed_ref)
    attend(packed_ref, heads_ref, lse_ref, video_mask(low.shape[0], positions))
    await_whole(weights, sems, *OUT)
    resid = values + dot_nn(heads_ref[0], weights[3])
    resid_ref[0] = resid
    xhat, _ = norm_parts(resid)
    third_ref[0] = (xhat * gain_ref[2:3, :]).astype(BF)


QKV, OUT = (0, 3), (3, 1)


def load_whole(stack, weights, sems, order):
    @pl.when(pl.program_id(0) == 0)
    def _():
        for first, count in order:
            start_whole(stack, first, weights.at[pl.ds(first, count)], sems.at[first // 3])


def await_whole(weights, sems, first, count):
    @pl.when(pl.program_id(0) == 0)
    def _():
        wait_all(weights.at[pl.ds(first, count)], sems.at[first // 3])


def attend_body(positions, place, packed_ref, heads_ref, lse_ref):
    mask = video_mask(packed_ref.shape[1], positions) if positions else None
    attend(packed_ref, heads_ref, lse_ref, mask)


def spatial_out_body(lots, place, heads_ref, frames_ref, shift_ref, *refs):
    n = stacks_of(lots)
    stacks, refs = refs[:n], refs[n:]
    piece_refs, (weights, resid, sems) = refs[:4], refs[4:]
    load_layer(place, lots, stacks, weights, sems)
    values = frames_ref[0].astype(F32) + shift_ref[0]
    await_layer(lots, weights, sems)
    resid[...] = (values + dot_nn(heads_ref[0], weights[lots[0][1] - 1])).astype(BF)
    count = piece_refs[0].shape[1]
    for j, piece in enumerate(piece_refs):
        first = pl.multiple_of((place[MEMBER] ^ j) * count, count)
        piece[0] = resid[pl.ds(first, count), :]


def ffn_body(group, base, last, kind, place, *refs):
    first = group == 0
    third_ref, cot_ref, resid_ref, stack = refs[:4]
    refs = refs[4:]
    if not first:
        dx_in, *refs = refs
    outs, refs = refs[:2], refs[2:]
    if last:
        dx_out, piece_refs, refs = refs[0], refs[1:5], refs[5:]
    else:
        resid_out, dx_out, refs = refs[0], refs[1], refs[2:]
    third, cot, third_t, cot_t, acc, dx, weights, act, pre_grad, staging, sems = refs
    tokens, width = third.shape
    blocks = weights.shape[0] // 2
    chunk = 256
    loads = [(third_ref, third, 0), (cot_ref, cot, 1), (resid_ref, acc, 2)]
    if not first:
        loads.append((dx_in, dx, 3))
    for source, target, s in loads[:2]:
        pltpu.make_async_copy(source, target, sems.at[s]).start()
    for b in range(blocks):
        start_whole(stack, base + 2 * b, weights.at[pl.ds(2 * b, 2)], sems.at[8 + b])
        if b == 0:
            for source, target, s in loads[2:]:
                pltpu.make_async_copy(source, target, sems.at[s]).start()
    for source, target, s in loads[:2]:
        pltpu.make_async_copy(source, target, sems.at[s]).wait()
    for source, target, s in loads[2:]:
        pltpu.make_async_copy(source, target, sems.at[s]).wait()

    def finish_sums():
        pltpu.make_async_copy(dx, dx_out, sems.at[6]).start()
        if not last:
            pltpu.make_async_copy(acc, resid_out, sems.at[7]).start()
            return
        low = third
        low[...] = acc[...].astype(BF)
        frames, positions = piece_refs[0].shape[:2]
        tiles = tokens // (FPV * 16)
        per_tile = positions // tiles
        for j, piece in enumerate(piece_refs):
            for tile in range(tiles):
                for f in range(frames):
                    row = pl.multiple_of(
                        tile * (tokens // tiles)
                        + ((place[MEMBER] ^ j) * frames + f) * per_tile,
                        per_tile,
                    )
                    pltpu.make_async_copy(
                        low.at[pl.ds(row, per_tile)],
                        piece.at[f, pl.ds(tile * per_tile, per_tile)],
                        sems.at[7],
                    ).start()

    def send(source, index):
        start_grads(place, kind, source, index, outs, sems.at[5])

    for b in range(blocks):
        w_up, w_down = weights.at[2 * b], weights.at[2 * b + 1]
        wait_all(weights.at[pl.ds(2 * b, 2)], sems.at[8 + b])
        for r in range(tokens // chunk):
            rows = slice(r * chunk, (r + 1) * chunk)
            pre = dot_nn(third[rows, :], w_up[...])
            act_grad = dot_nn(cot[rows, :], w_down[...])
            act_now, slope = gelu_both(pre)
            act_now = act_now.astype(BF)
            grad_now = (act_grad * slope).astype(BF)
            act[rows, :] = act_now
            pre_grad[rows, :] = grad_now
            if b == 0:
                third_t[:, rows] = third[rows, :].T
                cot_t[:, rows] = cot[rows, :].T
            acc[rows, :] += dot_nt(act_now, w_down[...])
            back = dot_nt(grad_now, w_up[...])
            if first and b == 0:
                dx[rows, :] = back
            else:
                dx[rows, :] += back
        if b == blocks - 1:
            finish_sums()
        staging[2 * b] = dot_nn(third_t[...], pre_grad[...]).astype(BF)
        send(staging.at[2 * b], 2 * b)
        staging[2 * b + 1] = dot_nn(cot_t[...], act[...]).astype(BF)
        send(staging.at[2 * b + 1], 2 * b + 1)
    if last:
        wait_all(third, sems.at[7])
    else:
        wait_all(acc, sems.at[7])
    wait_all(dx, sems.at[6])
    wait_all(staging, sems.at[5])


def add_gain(step, ref, row, value):
    @pl.when(step == 0)
    def _():
        ref[row : row + 1, :] = value

    @pl.when(step > 0)
    def _():
        ref[row : row + 1, :] += value


def temporal_bwd_body(
    place, dx_ref, cot_ref, resid_ref, tokens_ref, packed_ref, heads_ref, lse_ref, gain_ref, stack, *refs
):
    branch_ref, grad_ref, gains_out = refs[:3]
    piece_refs = refs[3:7]
    weights, heads_grad, total, sems = refs[7:]
    step = pl.program_id(0)
    load_whole(stack, weights, sems, (OUT, QKV))
    back, gain_three = norm_back(resid_ref[0], dx_ref[0], gain_ref[2:3, :])
    add_gain(step, gains_out, 1, gain_three)
    grad_two = cot_ref[0].astype(F32) + back
    branch = grad_two.astype(BF)
    branch_ref[0] = branch
    await_whole(weights, sems, *OUT)
    heads_grad[0] = dot_nt(branch, weights[3]).astype(BF)
    frames, positions = piece_refs[0].shape[0], piece_refs[0].shape[1]
    mask = video_mask(branch.shape[0], positions)
    attend_back(packed_ref, heads_ref, heads_grad, lse_ref, grad_ref, mask)
    await_whole(weights, sems, *QKV)
    normed_grad = project_back(grad_ref, weights)
    back, gain_two = norm_back(tokens_ref[0].astype(F32), normed_grad, gain_ref[1:2, :])
    add_gain(step, gains_out, 0, gain_two)
    total[...] = (grad_two + back).astype(BF).reshape(total.shape)
    for j, piece in enumerate(piece_refs):
        piece[...] = total[pl.ds((place[MEMBER] ^ j) * frames, frames)]


def spatial_branch_body(lots, place, *refs):
    n = stacks_of(lots)
    piece_refs, stacks = refs[:4], refs[4 : 4 + n]
    branch_ref, heads_grad_ref, weights, sems = refs[4 + n :]
    load_layer(place, lots, stacks, weights, sems)
    count = piece_refs[0].shape[1]
    for j, piece in enumerate(piece_refs):
        first = pl.multiple_of((place[MEMBER] ^ j) * count, count)
        branch_ref[0, pl.ds(first, count), :] = piece[0]
    await_layer(lots, weights, sems)
    heads_grad_ref[0] = dot_nt(branch_ref[0], weights[lots[0][1] - 1]).astype(BF)


def attend_back_body(positions, place, packed_ref, heads_ref, heads_grad_ref, lse_ref, grad_ref):
    mask = video_mask(packed_ref.shape[1], positions) if positions else None
    attend_back(packed_ref, heads_ref, heads_grad_ref, lse_ref, grad_ref, mask)


def project_back(grad_ref, weights):
    width = weights.shape[1]
    out = dot_nt(grad_ref[0, :, :width], weights[0])
    for b in range(1, 3):
        out = out + dot_nt(grad_ref[0, :, b * width : (b + 1) * width], weights[b])
    return out


def spatial_end_body(lots, place, grad_ref, frames_ref, shift_ref, branch_ref, gain_ref, *refs):
    n = stacks_of(lots)
    stacks, (input_ref, gain_out, column_out, weights, sems) = refs[:n], refs[n:]
    load_layer(place, lots, stacks, weights, sems)
    await_layer(lots, weights, sems)
    normed_grad = project_back(grad_ref, weights)
    values = frames_ref[0].astype(F32) + shift_ref[0]
    back, gain_one = norm_back(values, normed_grad, gain_ref[0:1, :])
    add_gain(pl.program_id(0), gain_out, 0, gain_one)
    grad_zero = branch_ref[0].astype(F32) + back
    input_ref[0] = grad_zero.astype(BF)
    column_out[0] = jnp.sum(grad_zero, axis=0, keepdims=True)


def weight_grad_body(kinds, lots, place, *refs):
    pairs = 1 + max(pair for lot in lots for pair, _ in lot)
    sides, refs = refs[: 2 * pairs], refs[2 * pairs :]
    outs, refs = refs[: 2 * len(lots)], refs[2 * len(lots) :]
    held, refs = refs[: 2 * pairs], refs[2 * pairs :]
    turned, (staging, sems) = refs[:pairs], refs[pairs:]
    for s, (source, target) in enumerate(zip(sides, held)):
        pltpu.make_async_copy(source, target, sems.at[s]).start()
    tokens, width = held[0].shape
    chunk = 256
    done = set()
    at = 0
    for i, lot in enumerate(lots):
        for index, (pair, block) in enumerate(lot):
            if pair not in done:
                done.add(pair)
                wait_all(held[2 * pair], sems.at[2 * pair])
                for r in range(tokens // chunk):
                    rows = slice(r * chunk, (r + 1) * chunk)
                    turned[pair][:, rows] = held[2 * pair][rows, :].T
                wait_all(held[2 * pair + 1], sems.at[2 * pair + 1])
            columns = slice(block * width, (block + 1) * width)
            staging[at] = dot_nn(turned[pair][...], held[2 * pair + 1][:, columns]).astype(BF)
            start_grads(place, kinds[i], staging.at[at], index, outs[2 * i : 2 * i + 2], sems.at[2 * pairs])
            at += 1
    wait_all(staging, sems.at[2 * pairs])


def update(weight, moment_one, moment_two, gradient, step_rate, decay_coef):
    first_new = beta_first * moment_one + (1.0 - beta_first) * gradient
    second_new = beta_second * moment_two + (1.0 - beta_second) * gradient * gradient
    fix_first = 1.0 - beta_first**STEP
    fix_second = 1.0 - beta_second**STEP
    change = first_new * (step_rate / fix_first) / (jnp.sqrt(second_new * (1.0 / fix_second)) + eps_adam)
    return weight - (change + (step_rate * decay_coef) * weight), first_new, second_new


def update_body(lots, place, clip, *refs):
    pieces, refs = refs[: 4 * len(lots)], refs[4 * len(lots) :]
    olds, news = refs[:6], refs[6:]
    array, matrix, block = pl.program_id(0), pl.program_id(1), pl.program_id(2)
    for i, lot in enumerate(lots):
        mine = functools.reduce(
            jnp.logical_or,
            [(array == a) & (matrix == m) & (block == b) for a, m, b in lot],
        )
        which = lot[0][0]

        @pl.when(mine)
        def _(i=i, which=which):
            master, first, second = olds[3 * which : 3 * which + 3]
            master_new, first_new, second_new = news[3 * which : 3 * which + 3]
            for rel, piece in enumerate(pieces[4 * i : 4 * i + 4]):
                width = piece.shape[2]
                column = (place[CORE] ^ (rel // 2)) * 2 + (place[XPOS] ^ (rel % 2))
                at = pl.ds(pl.multiple_of(column * width, 128), width)
                new = update(
                    master[0, :, at],
                    first[0, :, at],
                    second[0, :, at],
                    piece[0].astype(F32) * clip[0],
                    rate_matrix,
                    decay_rate,
                )
                master_new[0, :, at], first_new[0, :, at], second_new[0, :, at] = new


def join_body(place, *refs):
    pieces, out_ref = refs[:4], refs[4]
    count = pieces[0].shape[1]
    for j, piece in enumerate(pieces):
        first = pl.multiple_of((place[MEMBER] ^ j) * count, count)
        out_ref[0, pl.ds(first, count), :] = piece[0]


def tile_body(place, *refs):
    pieces, out_ref, tokens = refs[:4], refs[4], refs[5]
    frames = pieces[0].shape[0]
    for j, piece in enumerate(pieces):
        tokens[pl.ds((place[MEMBER] ^ j) * frames, frames)] = piece[...]
    out_ref[0] = tokens[...].reshape(out_ref.shape[1:])


def call(body, place, args, in_specs, out_specs, out_shape, scratch, grid=(1,), limit=60, us=10, scalars=1, aliases={}):
    return pl.pallas_call(
        body,
        out_shape=out_shape,
        grid_spec=pltpu.PrefetchScalarGridSpec(
            num_scalar_prefetch=scalars,
            grid=grid,
            in_specs=in_specs,
            out_specs=out_specs,
            scratch_shapes=scratch,
        ),
        input_output_aliases=aliases,
        compiler_params=pltpu.CompilerParams(vmem_limit_bytes=limit * MIB),
        cost_estimate=pl.CostEstimate(flops=us * 10**9, bytes_accessed=MIB, transcendentals=0),
    )(*place, *args)


def tile(*shape):
    return pl.BlockSpec((1,) + shape, lambda i, *_: (i,) + (0,) * len(shape))


def fixed(*shape):
    return pl.BlockSpec(shape, lambda i, *_: (0,) * len(shape))


def shape_of(*shape, dtype=BF):
    return jax.ShapeDtypeStruct(shape, dtype)


def shards(
    frames_in,
    action_codes,
    cotangent,
    attn_master,
    attn_first,
    attn_second,
    ffn_master,
    ffn_first,
    ffn_second,
    small_master,
    small_first,
    small_second,
):
    frames, positions, width = frames_in.shape
    heads_n = width // HD
    members = FPV // frames
    part = positions // members
    spot = positions // FPV
    tiles = part // spot
    rows_tile = FPV * spot
    tokens = tiles * rows_tile
    seq_size = lax.axis_size("seq")
    nz = seq_size // 2
    seq, grp = lax.axis_index("seq"), lax.axis_index("grp")
    place = jnp.stack([grp % 2, grp // 2, seq % 2, seq // 2, seq % members]).astype(jnp.int32)
    spots = (place,)
    local_rows = attn_master.shape[1]

    def blocks(master, picks):
        return jnp.stack([master[m, :, b * width : (b + 1) * width] for m, b in picks]).astype(BF)

    small_low = small_master.astype(BF)
    if seq_size & (seq_size - 1) == 0:
        small_all = small_low[None]
        bit = 1
        while bit < seq_size:
            small_all = jnp.concatenate([small_all, swap(small_all, "seq", bit)])
            bit *= 2
        small_all = jnp.take(small_all, jnp.arange(seq_size) ^ seq, axis=0)
    else:
        small_all = lax.all_gather(small_low, "seq")
    small_w = small_all.transpose(1, 0, 2).reshape(small_low.shape[0], width)

    qk_s, meta_qk_s = gather_weights(blocks(attn_master, [(0, 0), (0, 1)]), "zyx", place)
    v_s, meta_v_s = gather_weights(
        blocks(attn_master, [(0, 2)]), "zy", place, begin=(qk_s[0],)
    )
    below_o, beside_o = start_gather(
        blocks(attn_master, [(0, 3)]), "zy", place, begin=(v_s[0],)
    )
    lots_in_s, in_s = ((0, 2, meta_qk_s), (2, 1, meta_v_s)), [*qk_s, *v_s]

    ffn_picks = [(m, 2 * group + b) for group in range(2) for b in range(2) for m in range(2)]
    early = jnp.concatenate(
        [
            quarter_mine(blocks(attn_master, [(1, b) for b in range(4)]), place),
            quarter_mine(blocks(ffn_master, ffn_picks[:4]), place),
        ]
    )
    late = quarter_mine(blocks(ffn_master, ffn_picks[4:]), place)
    early_all = lax.all_gather(early, ("seq", "grp"))
    gains = small_w[:3].astype(F32)
    onehot = (action_codes[:, None] == jnp.arange(CODES)[None, :]).astype(BF)
    code_shift = jnp.dot(onehot, small_w[3:], preferred_element_type=F32)[:, None, :]

    piece_spec = pl.BlockSpec((frames, spot, width), lambda i, *_: (0, i, 0))
    part_spec = pl.BlockSpec((1, part, width), lambda i, *_: (i, 0, 0))
    sems = pltpu.SemaphoreType.DMA

    def held(count):
        return [pltpu.VMEM((count, width, width), BF)]

    def layer(body, lots, stacks, args, in_specs, out_specs, out_shape, scratch, us):
        return call(
            functools.partial(body, lots),
            spots,
            [*args, *stacks],
            in_specs + [ANY] * len(stacks),
            out_specs,
            out_shape,
            held(sum(count for _, count, _ in lots)) + scratch + [sems((len(lots),))],
            grid=(frames,),
            limit=60,
            us=us,
        )

    wide, flat_tile = tile(positions, 3 * width), tile(positions, width)
    wide_shape = shape_of(frames, positions, 3 * width)
    tile_shape = shape_of(frames, positions, width)
    tile32_shape = shape_of(frames, positions, width, dtype=F32)
    lse_spec, lse_shape = tile(heads_n, positions), shape_of(frames, heads_n, positions, dtype=F32)
    piece_shapes = [shape_of(frames, part, width)] * members
    gain_shape = shape_of(1, width, dtype=F32)

    def attention(packed, step):
        return call(
            functools.partial(attend_body, step),
            spots,
            [packed],
            [wide],
            [flat_tile, lse_spec],
            [tile_shape, lse_shape],
            [],
            grid=(frames,),
            limit=60,
            us=22,
        )

    def attention_back(packed, heads, heads_grad, lse, step):
        return call(
            functools.partial(attend_back_body, step),
            spots,
            [packed, heads, heads_grad, lse],
            [wide, flat_tile, flat_tile, lse_spec],
            wide,
            wide_shape,
            [],
            grid=(frames,),
            limit=60,
            us=26,
        )

    packed_s, normed_s = layer(
        spatial_in_body,
        lots_in_s,
        in_s,
        [before(frames_in, below_o), code_shift, gains],
        [flat_tile, tile(1, width), fixed(3, width)],
        [wide, flat_tile],
        [wide_shape, tile_shape],
        [],
        12,
    )
    heads_s, lse_s = attention(packed_s, 0)
    out_s, meta_out_s = finish_gather(
        below_o, beside_o, "zy", cross=(heads_s,)
    )
    lots_out_s = ((0, 1, meta_out_s),)
    pieces = layer(
        spatial_out_body,
        lots_out_s,
        out_s,
        [heads_s, frames_in, code_shift],
        [flat_tile, flat_tile, tile(1, width)],
        [part_spec] * members,
        piece_shapes,
        [pltpu.VMEM((positions, width), BF)],
        6,
    )
    token_pieces = exchange(pieces)
    late_all = lax.all_gather(before(late, token_pieces), ("seq", "grp"))

    packed_t, heads_t, lse_t, normed_t, tokens_t, resid_two, third = call(
        temporal_fwd_body,
        spots,
        [*token_pieces, gains, early_all],
        [piece_spec] * members + [fixed(3, width), ANY],
        [wide, flat_tile, lse_spec] + [flat_tile] * 4,
        [wide_shape, tile_shape, lse_shape, tile_shape, tile_shape, tile32_shape, tile_shape],
        held(4) + [pltpu.VMEM((FPV, spot, width), BF), sems((2,))],
        grid=(tiles,),
        us=37,
    )

    def position_part(array, j):
        return lax.dynamic_slice_in_dim(array, (place[MEMBER] ^ j) * part, part, 1)

    cot_pieces = exchange(
        [after(position_part(cotangent, j), *token_pieces) for j in range(members)]
    )
    cot_tiles = call(
        tile_body,
        spots,
        [before(cot_pieces[0], third), *cot_pieces[1:]],
        [piece_spec] * members,
        tile(rows_tile, width),
        shape_of(tiles, rows_tile, width),
        [pltpu.VMEM((FPV, spot, width), BF)],
        grid=(tiles,),
    )

    def split_shape(kind, n):
        lead = (2, 2, nz) if kind == "xyz" else (2, nz, 2)
        return shape_of(*lead, n, local_rows, width // 4)

    flat = lambda array: array.reshape(tokens, width)
    resid_now = flat(resid_two)
    full32 = shape_of(tokens, width, dtype=F32)
    parts_f = []
    groups = 2
    for group in range(groups):
        last = group == groups - 1
        ends = [full32] + [shape_of(frames, part, width)] * members if last else [full32, full32]
        args = [flat(third), flat(cot_tiles), resid_now, late_all if group else early_all]
        if group:
            args += [dx]
        outs = call(
            functools.partial(ffn_body, group, 0 if group else 4, last, "xyz"),
            spots,
            args,
            [ANY] * len(args),
            [ANY] * (2 + len(ends)),
            [split_shape("xyz", 4)] * 2 + ends,
            [pltpu.VMEM((tokens, width), BF)] * 2
            + [pltpu.VMEM((width, tokens), BF)] * 2
            + [pltpu.VMEM((tokens, width), F32)] * 2
            + [pltpu.VMEM((4, width, width), BF)]
            + [pltpu.VMEM((tokens, width), BF)] * 2
            + [pltpu.VMEM((4, width, width), BF), sems((10,))],
            us=41,
        )
        parts_f.append(outs[:2])
        if last:
            dx, block_pieces = outs[2], outs[3:]
        else:
            resid_now, dx = outs[2:]
            sum_e = send_core(outs[:2])

    quarters = {}
    sum_f = send_core(parts_f[1])
    sum_e, sent_e = step_one(sum_e, dx)
    dx = before(dx, sent_e)
    sum_e = send_one(sum_e, sent_e, "xyz")
    outs = call(
        temporal_bwd_body,
        spots,
        [dx.reshape(resid_two.shape), cot_tiles, resid_two, tokens_t, packed_t, heads_t, lse_t, gains, early_all],
        [flat_tile] * 4 + [wide, flat_tile, lse_spec, fixed(3, width), ANY],
        [flat_tile, wide, fixed(2, width)] + [piece_spec] * members,
        [tile_shape, wide_shape, shape_of(2, width, dtype=F32)] + piece_shapes,
        held(4)
        + [
            pltpu.VMEM((1, positions, width), BF),
            pltpu.VMEM((FPV, spot, width), BF),
            sems((2,)),
        ],
        grid=(tiles,),
        us=38,
    )
    branch_t, grad_t, gains_two = outs[:3]
    grad_pieces = exchange(outs[3:])
    block_pieces = exchange(block_pieces)
    join = functools.partial(
        call,
        body=join_body,
        place=spots,
        in_specs=[part_spec] * members,
        out_specs=tile(positions, width),
        out_shape=shape_of(frames, positions, width),
        scratch=[],
        grid=(frames,),
    )
    block_out = join(args=[before(block_pieces[0], grad_t), *block_pieces[1:]])


    def weight_grads(kinds, sides, *lots):
        sides = [side.reshape(tokens, -1) for side in sides]
        outs = call(
            functools.partial(weight_grad_body, kinds, lots),
            spots,
            sides,
            [ANY] * len(sides),
            [ANY] * (2 * len(lots)),
            [split_shape(kind, len(lot)) for kind, lot in zip(kinds, lots) for _ in range(2)],
            [pltpu.VMEM(side.shape, BF) for side in sides]
            + [pltpu.VMEM((width, tokens), BF)] * (len(sides) // 2)
            + [pltpu.VMEM((sum(map(len, lots)), width, width), BF), sems((len(sides) + 1,))],
            us=15,
        )
        return [outs[2 * i : 2 * i + 2] for i in range(len(lots))]

    sum_f, sent_f = step_one(sum_f, grad_t)
    sum_e, sent_e = step_two(sum_e, "xyz", grad_t, sent_f)
    sum_f = send_one(sum_f, sent_f, "xyz")

    branch_s, heads_grad_s = layer(
        spatial_branch_body,
        lots_out_s,
        out_s,
        [before(grad_pieces[0], sent_e, sent_f, block_out), *grad_pieces[1:]],
        [part_spec] * members,
        [flat_tile] * 2,
        [tile_shape] * 2,
        [],
        7,
    )
    sum_e = send_two(sum_e, before(sent_e, grad_pieces), "xyz")
    parts_tq, parts_tv = weight_grads(
        ("xyz", "yzx"),
        [normed_t, before(grad_t, branch_s), heads_t, branch_t],
        [(0, 0), (0, 1)],
        [(0, 2), (1, 0)],
    )
    sum_tq, sum_tv = send_core(parts_tq), send_core(parts_tv)
    sum_e, sent_e = step_three(sum_e, "xyz", parts_tq[0])
    sum_f, sent_f = step_two(sum_f, "xyz", parts_tq[0])
    grad_s = attention_back(packed_s, heads_s, before(heads_grad_s, sent_e, sent_f), lse_s, 0)
    sum_e, sum_f = send_three(sum_e, sent_e, "xyz"), send_two(sum_f, sent_f, "xyz")
    sum_tq, sent_tq = step_one(sum_tq, grad_s)
    sum_tv, sent_tv = step_one(sum_tv, grad_s)
    sum_f, sent_f = step_three(sum_f, "xyz", grad_s)
    (parts_qk,) = weight_grads(
        ("xyz",), [normed_s, before(grad_s, sent_tq, sent_tv, sent_f)], [(0, 0), (0, 1)]
    )
    sum_tq, sum_tv = send_one(sum_tq, sent_tq, "xyz"), send_one(sum_tv, sent_tv, "yzx")
    sum_f = send_three(sum_f, sent_f, "xyz")
    quarters["ffn0"] = finish(sum_e, parts_qk[0])
    sum_qk = send_core(parts_qk)
    (parts_vo,) = weight_grads(
        ("xyz",),
        [normed_s, before(grad_s, parts_qk, quarters["ffn0"]), heads_s, branch_s],
        [(0, 2), (1, 0)],
    )
    sum_vo = send_core(parts_vo)
    sum_qk, sent_qk = step_one(sum_qk, parts_vo[0])
    sum_tq, sent_tq = step_two(sum_tq, "xyz", parts_vo[0])
    sum_tv, sent_tv = step_two(sum_tv, "yzx", parts_vo[0])
    input_grad, gain_one, columns = layer(
        spatial_end_body,
        lots_in_s,
        in_s,
        [grad_s, frames_in, code_shift, before(branch_s, sent_qk, sent_tq, sent_tv), gains],
        [wide, flat_tile, tile(1, width), flat_tile, fixed(3, width)],
        [flat_tile, fixed(1, width), tile(1, width)],
        [tile_shape, gain_shape, shape_of(frames, 1, width, dtype=F32)],
        [],
        14,
    )
    sum_qk = send_one(sum_qk, sent_qk, "xyz")
    sum_tq, sum_tv = send_two(sum_tq, sent_tq, "xyz"), send_two(sum_tv, sent_tv, "yzx")
    sum_vo, sent_vo = step_one(sum_vo, columns)
    sum_vo = send_one(sum_vo, sent_vo, "xyz")
    sum_qk, sent_qk = step_two(sum_qk, "xyz", columns, sent_vo)
    sum_qk = send_two(sum_qk, sent_qk, "xyz")
    sum_tq, sent_tq = step_three(sum_tq, "xyz", columns, sent_qk)
    sum_tv, sent_tv = step_three(sum_tv, "yzx", columns, sent_qk)
    sum_tq, sum_tv = send_three(sum_tq, sent_tq, "xyz"), send_three(sum_tv, sent_tv, "yzx")
    quarters["ffn1"] = finish(sum_f, columns, sent_tq)
    sum_qk, sent_qk = step_three(sum_qk, "xyz", sent_tq, sent_tv)
    sum_qk = send_three(sum_qk, sent_qk, "xyz")
    ffn_quarter = before(jnp.concatenate([quarters["ffn0"], quarters["ffn1"]]), sent_qk)
    ffn_shared = share_quarters(ffn_quarter)
    sum_vo, sent_vo = step_two(sum_vo, "xyz", sent_qk)
    sum_vo = send_two(sum_vo, sent_vo, "xyz")
    quarters["tq"], quarters["tv"] = finish(sum_tq, sent_vo), finish(sum_tv, sent_vo)
    sum_vo, sent_vo = step_three(sum_vo, "xyz", quarters["tq"], quarters["tv"])
    sum_vo = send_three(sum_vo, sent_vo, "xyz")
    quarters["qk"] = finish(sum_qk, sent_vo)
    quarters["vo"] = finish(sum_vo, ffn_shared)
    attn_quarter = jnp.concatenate([quarters[name] for name in ("qk", "vo", "tq", "tv")])
    attn_shared = share_quarters(attn_quarter)

    table_grad = jnp.dot(
        onehot.astype(F32).T, columns[:, 0, :], precision=lax.Precision.HIGHEST
    )
    squares = sum(jnp.sum(jnp.square(q.astype(F32))) for q in (attn_quarter, ffn_quarter))
    sums = all_sum(
        jnp.concatenate(
            [gain_one, gains_two, table_grad, jnp.broadcast_to(squares, (1, width))], axis=0
        )
    )
    small_grad = sums[:-1]

    total_squares = sums[-1, 0] + jnp.sum(small_grad * small_grad)
    grad_norm = jnp.sqrt(total_squares)
    clip_factor = 1.0 / jnp.maximum(grad_norm, 1.0)
    lots = [
        (attn_shared, [(0, m, b) for m in range(2) for b in range(4)]),
        (ffn_shared, [(1, *pick) for pick in ffn_picks]),
    ]

    def piece_spec_of(lot):
        def at(a, m, b, *_):
            entry = 0
            for k, (array, matrix, block) in enumerate(lot):
                entry = jnp.where((a == array) & (m == matrix) & (b == block), k, entry)
            return entry, 0, 0

        return pl.BlockSpec((1, local_rows, width // 4), at)

    columns_n = attn_master.shape[2] // width
    attn_block = pl.BlockSpec(
        (1, local_rows, width),
        lambda a, m, b, *_: (jnp.where(a == 0, m, 1), 0, jnp.where(a == 0, b, columns_n - 1)),
    )
    ffn_block = pl.BlockSpec(
        (1, local_rows, width), lambda a, m, b, *_: (jnp.where(a == 1, m, 0), 0, jnp.where(a == 1, b, 0))
    )
    blocks_six = [attn_block] * 3 + [ffn_block] * 3
    updated = call(
        functools.partial(update_body, [lot for _, lot in lots]),
        (place, clip_factor.reshape(1)),
        [piece for pieces, _ in lots for piece in pieces]
        + [attn_master, attn_first, attn_second, ffn_master, ffn_first, ffn_second],
        [piece_spec_of(lot) for _, lot in lots for _ in range(4)] + blocks_six,
        blocks_six,
        [shape_of(*attn_master.shape, dtype=F32)] * 3 + [shape_of(*ffn_master.shape, dtype=F32)] * 3,
        [],
        grid=(2, 2, columns_n),
        scalars=2,
    )
    small_decay = jnp.where(jnp.arange(3 + CODES)[:, None] >= 3, decay_rate, 0.0)
    small_cols = small_master.shape[1]
    small_mine = lax.dynamic_slice_in_dim(small_grad, seq * small_cols, small_cols, 1)
    small_new = update(
        small_master, small_first, small_second, small_mine * clip_factor, rate_small, small_decay
    )
    return (block_out, input_grad, grad_norm, *updated, *small_new)


def solution(mesh):
    token = P(("grp", "seq"), None, None)
    matrix = P(None, "seq", None)
    small = P(None, "seq")
    return jax.shard_map(
        shards,
        mesh=mesh,
        in_specs=(token, P(("grp", "seq")), token) + (matrix,) * 6 + (small,) * 3,
        out_specs=(token, token, P()) + (matrix,) * 6 + (small,) * 3,
        check_vma=False,
    )
```

```python
import functools

import jax
import jax.numpy as jnp
from jax import lax
from jax.experimental import pallas as pl
from jax.experimental.pallas import tpu as pltpu
from jax.sharding import PartitionSpec as P

HD = 64
FPV = 16
CODES = 8
STEP = 5
BF = jnp.bfloat16
F32 = jnp.float32

eps_norm = 1e-05
beta_first = 0.5
beta_second = 0.5
rate_matrix = 0.02
rate_small = 0.3
decay_rate = 0.1
eps_adam = 1e-08
masked_score = -1000000000.0
score_scale = HD**-0.5

CORE, XPOS, YPOS, ZPOS, MEMBER = range(5)
ANY = pl.BlockSpec(memory_space=pl.ANY)
MIB = 1 << 20


def dot_nn(a, b):
    return lax.dot_general(a, b, (((1,), (0,)), ((), ())), preferred_element_type=F32)


def dot_nt(a, b):
    return lax.dot_general(a, b, (((1,), (1,)), ((), ())), preferred_element_type=F32)


def after(value, *others):
    return lax.optimization_barrier((value, *others))[0] if others else value


def swap(value, axis, bit):
    size = lax.axis_size(axis)
    return lax.ppermute(value, axis, [(i, i ^ bit) for i in range(size)])


def shift_z(value, step):
    size = lax.axis_size("seq")
    return lax.ppermute(value, "seq", [(i, (i + 2 * step) % size) for i in range(size)])


def z_groups():
    size = lax.axis_size("seq")
    return [list(range(first, size, 2)) for first in range(2)]


def gather_z(piece, *others):
    nz = lax.axis_size("seq") // 2
    if nz <= 4:
        return jnp.stack([piece] + [after(shift_z(piece, k), *others) for k in range(1, nz)])
    whole = lax.all_gather(piece, "seq", axis_index_groups=z_groups())
    here = lax.axis_index("seq") // 2
    return jnp.take(whole, (here - jnp.arange(nz)) % nz, axis=0)


def column_part(block, start, width):
    return lax.dynamic_slice_in_dim(block, start, width, 2)


def quarter_mine(block, place):
    part = block.shape[2] // 4
    return column_part(block, (place[CORE] * 2 + place[XPOS]) * part, part)


def start_gather(block, kind, place, begin=(), then=()):
    width = block.shape[2]
    if kind == "zyx":
        part = width // 4
        piece = column_part(block, (place[CORE] * 2 + place[XPOS]) * part, part)
    else:
        part = width // 2
        piece = column_part(block, place[CORE] * part, part)
    below = gather_z(after(piece, *begin), *then)
    return below, swap(below, "seq", 1)


def finish_gather(below, beside, kind, across_after=(), cross=()):
    stacks = [(below, 0, 0), (beside, 1, 0)]
    if kind == "zyx":
        stacks += [(swap(after(s, *across_after), "grp", 2), y, 1) for s, y, _ in stacks]
    out = [(s, (y, 0, x)) for s, y, x in stacks]
    out += [(swap(after(s, *cross), "grp", 1), (y, 1, x)) for s, y, x in stacks]
    return [s for s, _ in out], [m if kind == "zyx" else (m[0], m[1], None) for _, m in out]


def gather_weights(block, kind, place, begin=()):
    return finish_gather(*start_gather(block, kind, place, begin), kind)


def add_low(*terms):
    return sum(term.astype(F32) for term in terms).astype(BF)


def send_core(parts):
    return [parts[0], swap(parts[1], "grp", 1)]


def step_one(terms, *others):
    terms = [terms[0], before(terms[1], others)]
    return [term[0] for term in terms], add_low(*[term[1] for term in terms])


def send_one(terms, sent, kind):
    return terms + [swap(sent, "grp", 2) if kind == "xyz" else swap(sent, "seq", 1)]


def step_two(terms, kind, *others):
    terms = terms[:-1] + [before(terms[-1], others)]
    if kind == "xyz":
        return [term[0] for term in terms], add_low(*[term[1] for term in terms])
    return step_z(terms)


def step_z(terms):
    nz = terms[0].shape[0]
    return [term[0] for term in terms], [add_low(*[term[k] for term in terms]) for k in range(1, nz)]


def send_z(terms, sent):
    nz = lax.axis_size("seq") // 2
    if nz <= 4:
        return terms + [shift_z(part, k + 1) for k, part in enumerate(sent)]
    here = lax.axis_index("seq") // 2
    parts = jnp.stack([add_low(*terms), *sent])
    ordered = jnp.take(parts, (jnp.arange(nz) - here) % nz, axis=0)
    return [lax.psum_scatter(ordered, "seq", axis_index_groups=z_groups())]


def send_two(terms, sent, kind):
    return terms + [swap(sent, "seq", 1)] if kind == "xyz" else send_z(terms, sent)


def step_three(terms, kind, *others):
    terms = terms[:-1] + [before(terms[-1], others)]
    if kind == "xyz":
        return step_z(terms)
    return [term[0] for term in terms], add_low(*[term[1] for term in terms])


def send_three(terms, sent, kind):
    return send_z(terms, sent) if kind == "xyz" else terms + [swap(sent, "grp", 2)]


def finish(terms, *others):
    return add_low(*terms[:-1], before(terms[-1], others))


def before(value, *states):
    return after(value, *jax.tree.leaves(states))


def share_quarters(quarter):
    beside = swap(quarter, "grp", 2)
    return [quarter, beside, swap(quarter, "grp", 1), swap(beside, "grp", 1)]


def all_sum(value):
    for axis in ("grp", "seq"):
        size = lax.axis_size(axis)
        if size & (size - 1):
            value = lax.psum(value, axis)
            continue
        bit = 1
        while bit < size:
            if 4 * bit <= size:
                a, b, c = (swap(value, axis, bit * k) for k in (1, 2, 3))
                low = (lax.axis_index(axis) // (2 * bit)) % 2 == 0
                near, far = value + a, b + c
                value = jnp.where(low, near, far) + jnp.where(low, far, near)
                bit *= 4
            else:
                value = value + swap(value, axis, bit)
                bit *= 2
    return value


def exchange(pieces):
    return [pieces[0]] + [swap(pieces[j], "seq", j) for j in range(1, len(pieces))]


def start_weights(place, stacks, metas, target, sem):
    for stack, (y_rel, c_rel, x_rel) in zip(stacks, metas):
        nz, _, rows, width = stack.shape
        column = place[CORE] ^ c_rel
        if x_rel is not None:
            column = column * 2 + (place[XPOS] ^ x_rel)
        column = pl.multiple_of(column * width, 128)

        def one(k, carry, stack=stack, y_rel=y_rel, rows=rows, width=width, column=column, nz=nz):
            shard = lax.rem(place[ZPOS] - k + nz, nz) * 2 + (place[YPOS] ^ y_rel)
            row = pl.multiple_of(shard * rows, rows)
            pltpu.make_async_copy(
                stack.at[k], target.at[:, pl.ds(row, rows), pl.ds(column, width)], sem
            ).start()
            return carry

        if nz <= 4:
            for k in range(nz):
                one(k, 0)
        else:
            lax.fori_loop(0, nz, one, 0)


def quarter_column(g, width):
    return (g % 2 * 2 + g // 2) * width


def start_whole(stack, first, target, sem):
    count, _, rows, width = stack.shape
    n = target.shape[0]

    def one(s, carry):
        row = s * rows if isinstance(s, int) else pl.multiple_of(s * rows, rows)
        for g in range(4):
            pltpu.make_async_copy(
                stack.at[s * 4 + g, pl.ds(first, n)],
                target.at[:, pl.ds(row, rows), pl.ds(quarter_column(g, width), width)],
                sem,
            ).start()
        return carry

    if count <= 32:
        for s in range(count // 4):
            one(s, 0)
    else:
        lax.fori_loop(0, count // 4, one, 0)


def wait_all(target, sem):
    pltpu.make_async_copy(target, target, sem).wait()


def start_grads(place, kind, source, index, outs, sem):
    nz = outs[0].shape[2 if kind == "xyz" else 1]
    rows, width = outs[0].shape[-2:]
    for rel in range(4):
        out, x_rel = outs[rel // 2], rel % 2
        column = (place[CORE] ^ (rel // 2)) * 2 + (place[XPOS] ^ x_rel)
        column = pl.multiple_of(column * width, 128)
        for y_rel in range(2):

            def one(k, carry, out=out, x_rel=x_rel, y_rel=y_rel, column=column):
                shard = lax.rem(place[ZPOS] + k, nz) * 2 + (place[YPOS] ^ y_rel)
                row = pl.multiple_of(shard * rows, rows)
                target = out.at[x_rel, y_rel, k, index]
                if kind != "xyz":
                    target = out.at[y_rel, k, x_rel, index]
                pltpu.make_async_copy(
                    source.at[pl.ds(row, rows), pl.ds(column, width)], target, sem
                ).start()
                return carry

            if nz <= 4:
                for k in range(nz):
                    one(k, 0)
            else:
                lax.fori_loop(0, nz, one, 0)


def norm_parts(values):
    centre = values - jnp.mean(values, axis=-1, keepdims=True)
    spread = jnp.mean(centre * centre, axis=-1, keepdims=True)
    scale = lax.rsqrt(spread + eps_norm)
    return centre * scale, scale


def norm_back(values, h_grad, gain):
    xhat, scale = norm_parts(values)
    e = h_grad * gain
    inner = jnp.mean(e * xhat, axis=-1, keepdims=True)
    v_grad = scale * (e - jnp.mean(e, axis=-1, keepdims=True) - xhat * inner)
    return v_grad, jnp.sum(h_grad * xhat, axis=0, keepdims=True)


def two_heads(x):
    lane = lax.broadcasted_iota(jnp.int32, x.shape, 1)
    zero = jnp.zeros_like(x)
    return jnp.where(lane < HD, x, zero), jnp.where(lane < HD, zero, x)


def video_mask(rows, positions):
    key = lax.broadcasted_iota(jnp.int32, (rows, rows), 0)
    query = lax.broadcasted_iota(jnp.int32, (rows, rows), 1)
    return (lax.rem(key, positions) == lax.rem(query, positions)) & (key <= query)


def attend(packed_ref, heads_ref, lse_ref, mask):
    width = heads_ref.shape[-1]
    for pair in range(width // 128):
        lo = pair * 128
        queries = two_heads(packed_ref[0, :, lo : lo + 128] * jnp.asarray(score_scale, BF))
        keys = packed_ref[0, :, width + lo : width + lo + 128]
        values_t = packed_ref[0, :, 2 * width + lo : 2 * width + lo + 128].T
        out = []
        for half in range(2):
            scores = dot_nt(keys, queries[half])
            if mask is not None:
                scores = jnp.where(mask, scores, masked_score)
            top = jnp.max(scores, axis=0, keepdims=True)
            probs = jnp.exp(scores - top)
            total = jnp.sum(probs, axis=0, keepdims=True)
            mixed = dot_nn(values_t[half * HD : half * HD + HD], probs.astype(BF))
            out.append(mixed / total)
            lse_ref[0, 2 * pair + half : 2 * pair + half + 1, :] = top + jnp.log(total)
        heads_ref[0, :, lo : lo + 128] = jnp.concatenate(out, axis=0).astype(BF).T


def attend_back(packed_ref, heads_ref, heads_grad_ref, lse_ref, grad_ref, mask):
    width = heads_ref.shape[-1]
    for pair in range(width // 128):
        lo = pair * 128
        query = packed_ref[0, :, lo : lo + 128] * jnp.asarray(score_scale, BF)
        key = packed_ref[0, :, width + lo : width + lo + 128]
        value = packed_ref[0, :, 2 * width + lo : 2 * width + lo + 128]
        heads_grad = heads_grad_ref[0, :, lo : lo + 128]
        key_t = key.T
        mixed_t = (heads_grad.astype(F32) * heads_ref[0, :, lo : lo + 128].astype(F32)).T
        queries, head_grads = two_heads(query), two_heads(heads_grad)
        probs_two, score_two, query_grad = [], [], []
        for half in range(2):
            scores = dot_nt(key, queries[half])
            if mask is not None:
                scores = jnp.where(mask, scores, masked_score)
            probs = jnp.exp(scores - lse_ref[0, 2 * pair + half : 2 * pair + half + 1, :])
            delta = jnp.sum(mixed_t[half * HD : half * HD + HD], axis=0, keepdims=True)
            probs_grad = dot_nt(value, head_grads[half])
            score_grad = (probs * (probs_grad - delta)).astype(BF)
            probs_two.append(probs.astype(BF))
            score_two.append(score_grad)
            query_grad.append(dot_nn(key_t[half * HD : half * HD + HD], score_grad))
        value_grad = dot_nn(jnp.concatenate(probs_two, 1), jnp.concatenate(head_grads, 0))
        key_grad = dot_nn(jnp.concatenate(score_two, 1), jnp.concatenate(queries, 0))
        grad_ref[0, :, lo : lo + 128] = (
            (jnp.concatenate(query_grad, 0) * score_scale).astype(BF).T
        )
        grad_ref[0, :, width + lo : width + lo + 128] = key_grad.astype(BF)
        grad_ref[0, :, 2 * width + lo : 2 * width + lo + 128] = value_grad.astype(BF)


def gelu_both(pre):
    root = 0.7978845608028654
    square = pre * pre
    bend = jnp.tanh(root * pre * (1.0 + 0.044715 * square))
    half = 0.5 * (1.0 + bend)
    slope = half + 0.5 * pre * (1.0 - bend * bend) * (root * (1.0 + 3 * 0.044715 * square))
    return pre * half, slope


def start_layer(place, lots, refs, weights, sems):
    for i, (first, count, metas) in enumerate(lots):
        stacks, refs = refs[: len(metas)], refs[len(metas) :]
        start_weights(place, stacks, metas, weights.at[pl.ds(first, count)], sems.at[i])


def wait_layer(lots, weights, sems, block=None):
    for i, (first, count, _) in enumerate(lots):
        if block is None or block == first:
            wait_all(weights.at[pl.ds(first, count)], sems.at[i])


def stacks_of(lots):
    return sum(len(metas) for _, _, metas in lots)


def project_in(values, gain, weights, normed_ref, packed_ref, ready=lambda b: None):
    xhat, _ = norm_parts(values)
    normed = (xhat * gain).astype(BF)
    normed_ref[0] = normed
    width = normed.shape[1]
    for b in range(3):
        ready(b)
        packed_ref[0, :, b * width : (b + 1) * width] = dot_nn(normed, weights[b]).astype(BF)


def load_layer(place, lots, stacks, weights, sems):
    @pl.when(pl.program_id(0) == 0)
    def _():
        start_layer(place, lots, stacks, weights, sems)


def await_layer(lots, weights, sems, block=None):
    @pl.when(pl.program_id(0) == 0)
    def _():
        wait_layer(lots, weights, sems, block)


def spatial_in_body(lots, place, frames_ref, shift_ref, gain_ref, *refs):
    n = stacks_of(lots)
    stacks, (packed_ref, normed_ref, weights, sems) = refs[:n], refs[n:]
    load_layer(place, lots, stacks, weights, sems)
    values = frames_ref[0].astype(F32) + shift_ref[0]
    ready = functools.partial(await_layer, lots, weights, sems)
    project_in(values, gain_ref[0:1, :], weights, normed_ref, packed_ref, ready)


def temporal_fwd_body(place, *refs):
    piece_refs, gain_ref, stack = refs[:4], refs[4], refs[5]
    packed_ref, heads_ref, lse_ref, normed_ref, tokens_ref, resid_ref, third_ref = refs[6:13]
    weights, tokens, sems = refs[13:]
    load_whole(stack, weights, sems, (QKV, OUT))
    frames, positions = piece_refs[0].shape[0], piece_refs[0].shape[1]
    for j, piece in enumerate(piece_refs):
        tokens[pl.ds((place[MEMBER] ^ j) * frames, frames)] = piece[...]
    low = tokens[...].reshape(tokens_ref.shape[1:])
    tokens_ref[0] = low
    values = low.astype(F32)
    await_whole(weights, sems, *QKV)
    project_in(values, gain_ref[1:2, :], weights, normed_ref, packed_ref)
    attend(packed_ref, heads_ref, lse_ref, video_mask(low.shape[0], positions))
    await_whole(weights, sems, *OUT)
    resid = values + dot_nn(heads_ref[0], weights[3])
    resid_ref[0] = resid
    xhat, _ = norm_parts(resid)
    third_ref[0] = (xhat * gain_ref[2:3, :]).astype(BF)


QKV, OUT = (0, 3), (3, 1)


def load_whole(stack, weights, sems, order):
    @pl.when(pl.program_id(0) == 0)
    def _():
        for first, count in order:
            start_whole(stack, first, weights.at[pl.ds(first, count)], sems.at[first // 3])


def await_whole(weights, sems, first, count):
    @pl.when(pl.program_id(0) == 0)
    def _():
        wait_all(weights.at[pl.ds(first, count)], sems.at[first // 3])


def attend_body(positions, place, packed_ref, heads_ref, lse_ref):
    mask = video_mask(packed_ref.shape[1], positions) if positions else None
    attend(packed_ref, heads_ref, lse_ref, mask)


def spatial_out_body(lots, place, heads_ref, frames_ref, shift_ref, *refs):
    n = stacks_of(lots)
    stacks, refs = refs[:n], refs[n:]
    piece_refs, (weights, resid, sems) = refs[:4], refs[4:]
    load_layer(place, lots, stacks, weights, sems)
    values = frames_ref[0].astype(F32) + shift_ref[0]
    await_layer(lots, weights, sems)
    resid[...] = (values + dot_nn(heads_ref[0], weights[lots[0][1] - 1])).astype(BF)
    count = piece_refs[0].shape[1]
    for j, piece in enumerate(piece_refs):
        first = pl.multiple_of((place[MEMBER] ^ j) * count, count)
        piece[0] = resid[pl.ds(first, count), :]


def ffn_body(group, base, last, kind, place, *refs):
    first = group == 0
    third_ref, cot_ref, resid_ref, stack = refs[:4]
    refs = refs[4:]
    if not first:
        dx_in, *refs = refs
    outs, refs = refs[:2], refs[2:]
    if last:
        dx_out, piece_refs, refs = refs[0], refs[1:5], refs[5:]
    else:
        resid_out, dx_out, refs = refs[0], refs[1], refs[2:]
    third, cot, third_t, cot_t, acc, dx, weights, act, pre_grad, staging, sems = refs
    tokens, width = third.shape
    blocks = weights.shape[0] // 2
    chunk = 256
    loads = [(third_ref, third, 0), (cot_ref, cot, 1), (resid_ref, acc, 2)]
    if not first:
        loads.append((dx_in, dx, 3))
    for source, target, s in loads[:2]:
        pltpu.make_async_copy(source, target, sems.at[s]).start()
    for b in range(blocks):
        start_whole(stack, base + 2 * b, weights.at[pl.ds(2 * b, 2)], sems.at[8 + b])
        if b == 0:
            for source, target, s in loads[2:]:
                pltpu.make_async_copy(source, target, sems.at[s]).start()
    for source, target, s in loads[:2]:
        pltpu.make_async_copy(source, target, sems.at[s]).wait()
    for source, target, s in loads[2:]:
        pltpu.make_async_copy(source, target, sems.at[s]).wait()

    def finish_sums():
        pltpu.make_async_copy(dx, dx_out, sems.at[6]).start()
        if not last:
            pltpu.make_async_copy(acc, resid_out, sems.at[7]).start()
            return
        low = third
        low[...] = acc[...].astype(BF)
        frames, positions = piece_refs[0].shape[:2]
        tiles = tokens // (FPV * 16)
        per_tile = positions // tiles
        for j, piece in enumerate(piece_refs):
            for tile in range(tiles):
                for f in range(frames):
                    row = pl.multiple_of(
                        tile * (tokens // tiles)
                        + ((place[MEMBER] ^ j) * frames + f) * per_tile,
                        per_tile,
                    )
                    pltpu.make_async_copy(
                        low.at[pl.ds(row, per_tile)],
                        piece.at[f, pl.ds(tile * per_tile, per_tile)],
                        sems.at[7],
                    ).start()

    def send(source, index):
        start_grads(place, kind, source, index, outs, sems.at[5])

    for b in range(blocks):
        w_up, w_down = weights.at[2 * b], weights.at[2 * b + 1]
        wait_all(weights.at[pl.ds(2 * b, 2)], sems.at[8 + b])
        for r in range(tokens // chunk):
            rows = slice(r * chunk, (r + 1) * chunk)
            pre = dot_nn(third[rows, :], w_up[...])
            act_grad = dot_nn(cot[rows, :], w_down[...])
            act_now, slope = gelu_both(pre)
            act_now = act_now.astype(BF)
            grad_now = (act_grad * slope).astype(BF)
            act[rows, :] = act_now
            pre_grad[rows, :] = grad_now
            if b == 0:
                third_t[:, rows] = third[rows, :].T
                cot_t[:, rows] = cot[rows, :].T
            acc[rows, :] += dot_nt(act_now, w_down[...])
            back = dot_nt(grad_now, w_up[...])
            if first and b == 0:
                dx[rows, :] = back
            else:
                dx[rows, :] += back
        if b == blocks - 1:
            finish_sums()
        staging[2 * b] = dot_nn(third_t[...], pre_grad[...]).astype(BF)
        send(staging.at[2 * b], 2 * b)
        staging[2 * b + 1] = dot_nn(cot_t[...], act[...]).astype(BF)
        send(staging.at[2 * b + 1], 2 * b + 1)
    if last:
        wait_all(third, sems.at[7])
    else:
        wait_all(acc, sems.at[7])
    wait_all(dx, sems.at[6])
    wait_all(staging, sems.at[5])


def add_gain(step, ref, row, value):
    @pl.when(step == 0)
    def _():
        ref[row : row + 1, :] = value

    @pl.when(step > 0)
    def _():
        ref[row : row + 1, :] += value


def temporal_bwd_body(
    place, dx_ref, cot_ref, resid_ref, tokens_ref, packed_ref, heads_ref, lse_ref, gain_ref, stack, *refs
):
    branch_ref, grad_ref, gains_out = refs[:3]
    piece_refs = refs[3:7]
    weights, heads_grad, total, sems = refs[7:]
    step = pl.program_id(0)
    load_whole(stack, weights, sems, (OUT, QKV))
    back, gain_three = norm_back(resid_ref[0], dx_ref[0], gain_ref[2:3, :])
    add_gain(step, gains_out, 1, gain_three)
    grad_two = cot_ref[0].astype(F32) + back
    branch = grad_two.astype(BF)
    branch_ref[0] = branch
    await_whole(weights, sems, *OUT)
    heads_grad[0] = dot_nt(branch, weights[3]).astype(BF)
    frames, positions = piece_refs[0].shape[0], piece_refs[0].shape[1]
    mask = video_mask(branch.shape[0], positions)
    attend_back(packed_ref, heads_ref, heads_grad, lse_ref, grad_ref, mask)
    await_whole(weights, sems, *QKV)
    normed_grad = project_back(grad_ref, weights)
    back, gain_two = norm_back(tokens_ref[0].astype(F32), normed_grad, gain_ref[1:2, :])
    add_gain(step, gains_out, 0, gain_two)
    total[...] = (grad_two + back).astype(BF).reshape(total.shape)
    for j, piece in enumerate(piece_refs):
        piece[...] = total[pl.ds((place[MEMBER] ^ j) * frames, frames)]


def spatial_branch_body(lots, place, *refs):
    n = stacks_of(lots)
    piece_refs, stacks = refs[:4], refs[4 : 4 + n]
    branch_ref, heads_grad_ref, weights, sems = refs[4 + n :]
    load_layer(place, lots, stacks, weights, sems)
    count = piece_refs[0].shape[1]
    for j, piece in enumerate(piece_refs):
        first = pl.multiple_of((place[MEMBER] ^ j) * count, count)
        branch_ref[0, pl.ds(first, count), :] = piece[0]
    await_layer(lots, weights, sems)
    heads_grad_ref[0] = dot_nt(branch_ref[0], weights[lots[0][1] - 1]).astype(BF)


def attend_back_body(positions, place, packed_ref, heads_ref, heads_grad_ref, lse_ref, grad_ref):
    mask = video_mask(packed_ref.shape[1], positions) if positions else None
    attend_back(packed_ref, heads_ref, heads_grad_ref, lse_ref, grad_ref, mask)


def project_back(grad_ref, weights, ready=lambda b: None):
    width = weights.shape[1]
    ready(0)
    out = dot_nt(grad_ref[0, :, :width], weights[0])
    for b in range(1, 3):
        ready(b)
        out = out + dot_nt(grad_ref[0, :, b * width : (b + 1) * width], weights[b])
    return out


def spatial_end_body(lots, place, grad_ref, frames_ref, shift_ref, branch_ref, gain_ref, *refs):
    n = stacks_of(lots)
    stacks, (input_ref, gain_out, column_out, weights, sems) = refs[:n], refs[n:]
    load_layer(place, lots, stacks, weights, sems)
    normed_grad = project_back(
        grad_ref, weights, functools.partial(await_layer, lots, weights, sems)
    )
    values = frames_ref[0].astype(F32) + shift_ref[0]
    back, gain_one = norm_back(values, normed_grad, gain_ref[0:1, :])
    add_gain(pl.program_id(0), gain_out, 0, gain_one)
    grad_zero = branch_ref[0].astype(F32) + back
    input_ref[0] = grad_zero.astype(BF)
    column_out[0] = jnp.sum(grad_zero, axis=0, keepdims=True)


def weight_grad_body(kinds, lots, place, *refs):
    uses = [use for lot in lots for use in lot]
    pairs = 1 + max(pair for pair, _ in uses)
    sides, refs = refs[: 2 * pairs], refs[2 * pairs :]
    outs, refs = refs[: 2 * len(lots)], refs[2 * len(lots) :]
    lefts, turned, refs = refs[:pairs], refs[pairs : 2 * pairs], refs[2 * pairs :]
    rights, staging, sems = refs
    tokens, width = lefts[0].shape
    chunk = 256
    seen = []
    for at, (pair, block) in enumerate(uses):
        if pair not in seen:
            seen.append(pair)
            pltpu.make_async_copy(sides[2 * pair], lefts[pair], sems.at[pair]).start()
        pltpu.make_async_copy(
            sides[2 * pair + 1].at[:, pl.ds(block * width, width)], rights.at[at], sems.at[pairs + at]
        ).start()
    seen = []
    at = 0
    for i, lot in enumerate(lots):
        for index, (pair, _) in enumerate(lot):
            if pair not in seen:
                seen.append(pair)
                wait_all(lefts[pair], sems.at[pair])
                for r in range(tokens // chunk):
                    rows = slice(r * chunk, (r + 1) * chunk)
                    turned[pair][:, rows] = lefts[pair][rows, :].T
            wait_all(rights.at[at], sems.at[pairs + at])
            staging[at] = dot_nn(turned[pair][...], rights[at]).astype(BF)
            start_grads(
                place, kinds[i], staging.at[at], index, outs[2 * i : 2 * i + 2], sems.at[pairs + len(uses)]
            )
            at += 1
    wait_all(staging, sems.at[pairs + len(uses)])


def update(weight, moment_one, moment_two, gradient, step_rate, decay_coef):
    first_new = beta_first * moment_one + (1.0 - beta_first) * gradient
    second_new = beta_second * moment_two + (1.0 - beta_second) * gradient * gradient
    fix_first = 1.0 - beta_first**STEP
    fix_second = 1.0 - beta_second**STEP
    change = first_new * (step_rate / fix_first) / (jnp.sqrt(second_new * (1.0 / fix_second)) + eps_adam)
    return weight - (change + (step_rate * decay_coef) * weight), first_new, second_new


def update_body(lots, place, clip, *refs):
    pieces, refs = refs[: 4 * len(lots)], refs[4 * len(lots) :]
    olds, news = refs[:6], refs[6:]
    array, matrix, block = pl.program_id(0), pl.program_id(1), pl.program_id(2)
    for i, lot in enumerate(lots):
        mine = functools.reduce(
            jnp.logical_or,
            [(array == a) & (matrix == m) & (block == b) for a, m, b in lot],
        )
        which = lot[0][0]

        @pl.when(mine)
        def _(i=i, which=which):
            master, first, second = olds[3 * which : 3 * which + 3]
            master_new, first_new, second_new = news[3 * which : 3 * which + 3]
            for rel, piece in enumerate(pieces[4 * i : 4 * i + 4]):
                width = piece.shape[2]
                column = (place[CORE] ^ (rel // 2)) * 2 + (place[XPOS] ^ (rel % 2))
                at = pl.ds(pl.multiple_of(column * width, 128), width)
                new = update(
                    master[0, :, at],
                    first[0, :, at],
                    second[0, :, at],
                    piece[0].astype(F32) * clip[0],
                    rate_matrix,
                    decay_rate,
                )
                master_new[0, :, at], first_new[0, :, at], second_new[0, :, at] = new


def join_body(place, *refs):
    pieces, out_ref = refs[:4], refs[4]
    count = pieces[0].shape[1]
    for j, piece in enumerate(pieces):
        first = pl.multiple_of((place[MEMBER] ^ j) * count, count)
        out_ref[0, pl.ds(first, count), :] = piece[0]


def tile_body(place, *refs):
    pieces, out_ref, tokens = refs[:4], refs[4], refs[5]
    frames = pieces[0].shape[0]
    for j, piece in enumerate(pieces):
        tokens[pl.ds((place[MEMBER] ^ j) * frames, frames)] = piece[...]
    out_ref[0] = tokens[...].reshape(out_ref.shape[1:])


def call(body, place, args, in_specs, out_specs, out_shape, scratch, grid=(1,), limit=60, us=10, scalars=1, aliases={}):
    return pl.pallas_call(
        body,
        out_shape=out_shape,
        grid_spec=pltpu.PrefetchScalarGridSpec(
            num_scalar_prefetch=scalars,
            grid=grid,
            in_specs=in_specs,
            out_specs=out_specs,
            scratch_shapes=scratch,
        ),
        input_output_aliases=aliases,
        compiler_params=pltpu.CompilerParams(vmem_limit_bytes=limit * MIB),
        cost_estimate=pl.CostEstimate(flops=us * 10**9, bytes_accessed=MIB, transcendentals=0),
    )(*place, *args)


def tile(*shape):
    return pl.BlockSpec((1,) + shape, lambda i, *_: (i,) + (0,) * len(shape))


def fixed(*shape):
    return pl.BlockSpec(shape, lambda i, *_: (0,) * len(shape))


def shape_of(*shape, dtype=BF):
    return jax.ShapeDtypeStruct(shape, dtype)


def shards(
    frames_in,
    action_codes,
    cotangent,
    attn_master,
    attn_first,
    attn_second,
    ffn_master,
    ffn_first,
    ffn_second,
    small_master,
    small_first,
    small_second,
):
    frames, positions, width = frames_in.shape
    heads_n = width // HD
    members = FPV // frames
    part = positions // members
    spot = positions // FPV
    tiles = part // spot
    rows_tile = FPV * spot
    tokens = tiles * rows_tile
    seq_size = lax.axis_size("seq")
    nz = seq_size // 2
    seq, grp = lax.axis_index("seq"), lax.axis_index("grp")
    place = jnp.stack([grp % 2, grp // 2, seq % 2, seq // 2, seq % members]).astype(jnp.int32)
    spots = (place,)
    local_rows = attn_master.shape[1]

    def blocks(master, picks):
        return jnp.stack([master[m, :, b * width : (b + 1) * width] for m, b in picks]).astype(BF)

    small_low = small_master.astype(BF)
    if seq_size & (seq_size - 1) == 0:
        small_all = small_low[None]
        bit = 1
        while bit < seq_size:
            small_all = jnp.concatenate([small_all, swap(small_all, "seq", bit)])
            bit *= 2
        small_all = jnp.take(small_all, jnp.arange(seq_size) ^ seq, axis=0)
    else:
        small_all = lax.all_gather(small_low, "seq")
    small_w = small_all.transpose(1, 0, 2).reshape(small_low.shape[0], width)

    qk_s, meta_qk_s = gather_weights(blocks(attn_master, [(0, 0), (0, 1)]), "zyx", place)
    v_s, meta_v_s = gather_weights(
        blocks(attn_master, [(0, 2)]), "zy", place, begin=(qk_s[0],)
    )
    below_o, beside_o = start_gather(
        blocks(attn_master, [(0, 3)]), "zy", place, begin=(v_s[0],)
    )
    lots_in_s, in_s = ((0, 2, meta_qk_s), (2, 1, meta_v_s)), [*qk_s, *v_s]

    ffn_picks = [(m, 2 * group + b) for group in range(2) for b in range(2) for m in range(2)]
    early = jnp.concatenate(
        [
            quarter_mine(blocks(attn_master, [(1, b) for b in range(4)]), place),
            quarter_mine(blocks(ffn_master, ffn_picks[:4]), place),
        ]
    )
    late = quarter_mine(blocks(ffn_master, ffn_picks[4:]), place)
    early_all = lax.all_gather(early, ("seq", "grp"))
    gains = small_w[:3].astype(F32)
    onehot = (action_codes[:, None] == jnp.arange(CODES)[None, :]).astype(BF)
    code_shift = jnp.dot(onehot, small_w[3:], preferred_element_type=F32)[:, None, :]

    piece_spec = pl.BlockSpec((frames, spot, width), lambda i, *_: (0, i, 0))
    part_spec = pl.BlockSpec((1, part, width), lambda i, *_: (i, 0, 0))
    sems = pltpu.SemaphoreType.DMA

    def held(count):
        return [pltpu.VMEM((count, width, width), BF)]

    def layer(body, lots, stacks, args, in_specs, out_specs, out_shape, scratch, us):
        return call(
            functools.partial(body, lots),
            spots,
            [*args, *stacks],
            in_specs + [ANY] * len(stacks),
            out_specs,
            out_shape,
            held(sum(count for _, count, _ in lots)) + scratch + [sems((len(lots),))],
            grid=(frames,),
            limit=60,
            us=us,
        )

    wide, flat_tile = tile(positions, 3 * width), tile(positions, width)
    wide_shape = shape_of(frames, positions, 3 * width)
    tile_shape = shape_of(frames, positions, width)
    tile32_shape = shape_of(frames, positions, width, dtype=F32)
    lse_spec, lse_shape = tile(heads_n, positions), shape_of(frames, heads_n, positions, dtype=F32)
    piece_shapes = [shape_of(frames, part, width)] * members
    gain_shape = shape_of(1, width, dtype=F32)

    def attention(packed, step):
        return call(
            functools.partial(attend_body, step),
            spots,
            [packed],
            [wide],
            [flat_tile, lse_spec],
            [tile_shape, lse_shape],
            [],
            grid=(frames,),
            limit=60,
            us=22,
        )

    def attention_back(packed, heads, heads_grad, lse, step):
        return call(
            functools.partial(attend_back_body, step),
            spots,
            [packed, heads, heads_grad, lse],
            [wide, flat_tile, flat_tile, lse_spec],
            wide,
            wide_shape,
            [],
            grid=(frames,),
            limit=60,
            us=26,
        )

    packed_s, normed_s = layer(
        spatial_in_body,
        lots_in_s,
        in_s,
        [before(frames_in, below_o), code_shift, gains],
        [flat_tile, tile(1, width), fixed(3, width)],
        [wide, flat_tile],
        [wide_shape, tile_shape],
        [],
        12,
    )
    heads_s, lse_s = attention(packed_s, 0)
    out_s, meta_out_s = finish_gather(
        below_o, beside_o, "zy", cross=(heads_s,)
    )
    lots_out_s = ((0, 1, meta_out_s),)
    pieces = layer(
        spatial_out_body,
        lots_out_s,
        out_s,
        [heads_s, frames_in, code_shift],
        [flat_tile, flat_tile, tile(1, width)],
        [part_spec] * members,
        piece_shapes,
        [pltpu.VMEM((positions, width), BF)],
        6,
    )
    token_pieces = exchange(pieces)
    late_all = lax.all_gather(before(late, token_pieces), ("seq", "grp"))

    packed_t, heads_t, lse_t, normed_t, tokens_t, resid_two, third = call(
        temporal_fwd_body,
        spots,
        [*token_pieces, gains, early_all],
        [piece_spec] * members + [fixed(3, width), ANY],
        [wide, flat_tile, lse_spec] + [flat_tile] * 4,
        [wide_shape, tile_shape, lse_shape, tile_shape, tile_shape, tile32_shape, tile_shape],
        held(4) + [pltpu.VMEM((FPV, spot, width), BF), sems((2,))],
        grid=(tiles,),
        us=37,
    )

    def position_part(array, j):
        return lax.dynamic_slice_in_dim(array, (place[MEMBER] ^ j) * part, part, 1)

    cot_pieces = exchange(
        [after(position_part(cotangent, j), *token_pieces) for j in range(members)]
    )
    cot_tiles = call(
        tile_body,
        spots,
        [before(cot_pieces[0], third), *cot_pieces[1:]],
        [piece_spec] * members,
        tile(rows_tile, width),
        shape_of(tiles, rows_tile, width),
        [pltpu.VMEM((FPV, spot, width), BF)],
        grid=(tiles,),
    )

    def split_shape(kind, n):
        lead = (2, 2, nz) if kind == "xyz" else (2, nz, 2)
        return shape_of(*lead, n, local_rows, width // 4)

    flat = lambda array: array.reshape(tokens, width)
    resid_now = flat(resid_two)
    full32 = shape_of(tokens, width, dtype=F32)
    parts_f = []
    groups = 2
    for group in range(groups):
        last = group == groups - 1
        ends = [full32] + [shape_of(frames, part, width)] * members if last else [full32, full32]
        args = [flat(third), flat(cot_tiles), resid_now, late_all if group else early_all]
        if group:
            args += [dx]
        outs = call(
            functools.partial(ffn_body, group, 0 if group else 4, last, "xyz"),
            spots,
            args,
            [ANY] * len(args),
            [ANY] * (2 + len(ends)),
            [split_shape("xyz", 4)] * 2 + ends,
            [pltpu.VMEM((tokens, width), BF)] * 2
            + [pltpu.VMEM((width, tokens), BF)] * 2
            + [pltpu.VMEM((tokens, width), F32)] * 2
            + [pltpu.VMEM((4, width, width), BF)]
            + [pltpu.VMEM((tokens, width), BF)] * 2
            + [pltpu.VMEM((4, width, width), BF), sems((10,))],
            us=41,
        )
        parts_f.append(outs[:2])
        if last:
            dx, block_pieces = outs[2], outs[3:]
        else:
            resid_now, dx = outs[2:]
            sum_e = send_core(outs[:2])

    quarters = {}
    sum_f = send_core(parts_f[1])
    sum_e, sent_e = step_one(sum_e, dx)
    dx = before(dx, sent_e)
    sum_e = send_one(sum_e, sent_e, "xyz")
    outs = call(
        temporal_bwd_body,
        spots,
        [dx.reshape(resid_two.shape), cot_tiles, resid_two, tokens_t, packed_t, heads_t, lse_t, gains, early_all],
        [flat_tile] * 4 + [wide, flat_tile, lse_spec, fixed(3, width), ANY],
        [flat_tile, wide, fixed(2, width)] + [piece_spec] * members,
        [tile_shape, wide_shape, shape_of(2, width, dtype=F32)] + piece_shapes,
        held(4)
        + [
            pltpu.VMEM((1, positions, width), BF),
            pltpu.VMEM((FPV, spot, width), BF),
            sems((2,)),
        ],
        grid=(tiles,),
        us=38,
    )
    branch_t, grad_t, gains_two = outs[:3]
    grad_pieces = exchange(outs[3:])
    block_pieces = exchange(block_pieces)
    join = functools.partial(
        call,
        body=join_body,
        place=spots,
        in_specs=[part_spec] * members,
        out_specs=tile(positions, width),
        out_shape=shape_of(frames, positions, width),
        scratch=[],
        grid=(frames,),
    )
    block_out = join(args=[before(block_pieces[0], grad_t), *block_pieces[1:]])


    def weight_grads(kinds, sides, *lots):
        sides = [side.reshape(tokens, -1) for side in sides]
        outs = call(
            functools.partial(weight_grad_body, kinds, lots),
            spots,
            sides,
            [ANY] * len(sides),
            [ANY] * (2 * len(lots)),
            [split_shape(kind, len(lot)) for kind, lot in zip(kinds, lots) for _ in range(2)],
            [pltpu.VMEM((tokens, width), BF)] * (len(sides) // 2)
            + [pltpu.VMEM((width, tokens), BF)] * (len(sides) // 2)
            + [pltpu.VMEM((sum(map(len, lots)), tokens, width), BF)]
            + [pltpu.VMEM((sum(map(len, lots)), width, width), BF)]
            + [sems((len(sides) // 2 + sum(map(len, lots)) + 1,))],
            us=15,
        )
        return [outs[2 * i : 2 * i + 2] for i in range(len(lots))]

    sum_f, sent_f = step_one(sum_f, grad_t)
    sum_e, sent_e = step_two(sum_e, "xyz", grad_t, sent_f)
    sum_f = send_one(sum_f, sent_f, "xyz")

    branch_s, heads_grad_s = layer(
        spatial_branch_body,
        lots_out_s,
        out_s,
        [before(grad_pieces[0], sent_e, sent_f, block_out), *grad_pieces[1:]],
        [part_spec] * members,
        [flat_tile] * 2,
        [tile_shape] * 2,
        [],
        7,
    )
    sum_e = send_two(sum_e, before(sent_e, grad_pieces), "xyz")
    parts_tq, parts_tv = weight_grads(
        ("xyz", "yzx"),
        [normed_t, before(grad_t, branch_s), heads_t, branch_t],
        [(0, 0), (0, 1)],
        [(0, 2), (1, 0)],
    )
    sum_tq, sum_tv = send_core(parts_tq), send_core(parts_tv)
    sum_e, sent_e = step_three(sum_e, "xyz", parts_tq[0])
    sum_f, sent_f = step_two(sum_f, "xyz", parts_tq[0])
    grad_s = attention_back(packed_s, heads_s, before(heads_grad_s, sent_e, sent_f), lse_s, 0)
    sum_e, sum_f = send_three(sum_e, sent_e, "xyz"), send_two(sum_f, sent_f, "xyz")
    sum_tq, sent_tq = step_one(sum_tq, grad_s)
    sum_tv, sent_tv = step_one(sum_tv, grad_s)
    sum_f, sent_f = step_three(sum_f, "xyz", grad_s)
    (parts_qk,) = weight_grads(
        ("xyz",), [normed_s, before(grad_s, sent_tq, sent_tv, sent_f)], [(0, 0), (0, 1)]
    )
    sum_tq, sum_tv = send_one(sum_tq, sent_tq, "xyz"), send_one(sum_tv, sent_tv, "yzx")
    sum_f = send_three(sum_f, sent_f, "xyz")
    quarters["ffn0"] = finish(sum_e, parts_qk[0])
    sum_qk = send_core(parts_qk)
    (parts_vo,) = weight_grads(
        ("xyz",),
        [normed_s, before(grad_s, parts_qk, quarters["ffn0"]), heads_s, branch_s],
        [(0, 2), (1, 0)],
    )
    sum_vo = send_core(parts_vo)
    sum_qk, sent_qk = step_one(sum_qk, parts_vo[0])
    sum_tq, sent_tq = step_two(sum_tq, "xyz", parts_vo[0])
    sum_tv, sent_tv = step_two(sum_tv, "yzx", parts_vo[0])
    input_grad, gain_one, columns = layer(
        spatial_end_body,
        lots_in_s,
        in_s,
        [grad_s, frames_in, code_shift, before(branch_s, sent_qk, sent_tq, sent_tv), gains],
        [wide, flat_tile, tile(1, width), flat_tile, fixed(3, width)],
        [flat_tile, fixed(1, width), tile(1, width)],
        [tile_shape, gain_shape, shape_of(frames, 1, width, dtype=F32)],
        [],
        14,
    )
    sum_qk = send_one(sum_qk, sent_qk, "xyz")
    sum_tq, sum_tv = send_two(sum_tq, sent_tq, "xyz"), send_two(sum_tv, sent_tv, "yzx")
    sum_vo, sent_vo = step_one(sum_vo, columns)
    sum_vo = send_one(sum_vo, sent_vo, "xyz")
    sum_qk, sent_qk = step_two(sum_qk, "xyz", columns, sent_vo)
    sum_qk = send_two(sum_qk, sent_qk, "xyz")
    sum_tq, sent_tq = step_three(sum_tq, "xyz", columns, sent_qk)
    sum_tq = send_three(sum_tq, sent_tq, "xyz")
    quarters["ffn1"] = finish(sum_f, columns, sent_tq)
    sum_qk, sent_qk = step_three(sum_qk, "xyz", sent_tq)
    sum_qk = send_three(sum_qk, sent_qk, "xyz")
    ffn_quarter = before(jnp.concatenate([quarters["ffn0"], quarters["ffn1"]]), sent_qk)
    ffn_shared = share_quarters(ffn_quarter)
    sum_vo, sent_vo = step_two(sum_vo, "xyz", sent_qk)
    sum_vo = send_two(sum_vo, sent_vo, "xyz")
    sum_tv, sent_tv = step_three(sum_tv, "yzx", sent_vo)
    sum_tv = send_three(sum_tv, sent_tv, "yzx")
    quarters["tq"] = finish(sum_tq, sent_tv)
    sum_vo, sent_vo = step_three(sum_vo, "xyz", quarters["tq"])
    sum_vo = send_three(sum_vo, sent_vo, "xyz")
    quarters["qk"] = finish(sum_qk, sent_vo)
    quarters["tv"] = finish(sum_tv, sent_vo)
    quarters["vo"] = finish(sum_vo, ffn_shared)
    attn_quarter = jnp.concatenate([quarters[name] for name in ("qk", "vo", "tq", "tv")])
    attn_shared = share_quarters(attn_quarter)

    table_grad = jnp.dot(
        onehot.astype(F32).T, columns[:, 0, :], precision=lax.Precision.HIGHEST
    )
    squares = sum(jnp.sum(jnp.square(q.astype(F32))) for q in (attn_quarter, ffn_quarter))
    sums = all_sum(
        jnp.concatenate(
            [gain_one, gains_two, table_grad, jnp.broadcast_to(squares, (1, width))], axis=0
        )
    )
    small_grad = sums[:-1]

    total_squares = sums[-1, 0] + jnp.sum(small_grad * small_grad)
    grad_norm = jnp.sqrt(total_squares)
    clip_factor = 1.0 / jnp.maximum(grad_norm, 1.0)
    lots = [
        (attn_shared, [(0, m, b) for m in range(2) for b in range(4)]),
        (ffn_shared, [(1, *pick) for pick in ffn_picks]),
    ]

    def piece_spec_of(lot):
        def at(a, m, b, *_):
            entry = 0
            for k, (array, matrix, block) in enumerate(lot):
                entry = jnp.where((a == array) & (m == matrix) & (b == block), k, entry)
            return entry, 0, 0

        return pl.BlockSpec((1, local_rows, width // 4), at)

    columns_n = attn_master.shape[2] // width
    attn_block = pl.BlockSpec(
        (1, local_rows, width),
        lambda a, m, b, *_: (jnp.where(a == 0, m, 1), 0, jnp.where(a == 0, b, columns_n - 1)),
    )
    ffn_block = pl.BlockSpec(
        (1, local_rows, width), lambda a, m, b, *_: (jnp.where(a == 1, m, 0), 0, jnp.where(a == 1, b, 0))
    )
    blocks_six = [attn_block] * 3 + [ffn_block] * 3
    updated = call(
        functools.partial(update_body, [lot for _, lot in lots]),
        (place, clip_factor.reshape(1)),
        [piece for pieces, _ in lots for piece in pieces]
        + [attn_master, attn_first, attn_second, ffn_master, ffn_first, ffn_second],
        [piece_spec_of(lot) for _, lot in lots for _ in range(4)] + blocks_six,
        blocks_six,
        [shape_of(*attn_master.shape, dtype=F32)] * 3 + [shape_of(*ffn_master.shape, dtype=F32)] * 3,
        [],
        grid=(2, 2, columns_n),
        scalars=2,
    )
    small_decay = jnp.where(jnp.arange(3 + CODES)[:, None] >= 3, decay_rate, 0.0)
    small_cols = small_master.shape[1]
    small_mine = lax.dynamic_slice_in_dim(small_grad, seq * small_cols, small_cols, 1)
    small_new = update(
        small_master, small_first, small_second, small_mine * clip_factor, rate_small, small_decay
    )
    return (block_out, input_grad, grad_norm, *updated, *small_new)


def solution(mesh):
    token = P(("grp", "seq"), None, None)
    matrix = P(None, "seq", None)
    small = P(None, "seq")
    return jax.shard_map(
        shards,
        mesh=mesh,
        in_specs=(token, P(("grp", "seq")), token) + (matrix,) * 6 + (small,) * 3,
        out_specs=(token, token, P()) + (matrix,) * 6 + (small,) * 3,
        check_vma=False,
    )
```
